32 devices in a mesh: dp: 2 (over x), row: 8 (over z, y), col: 2 (over core).
Axes of the slice: x: 2, y: 2, z: 4, core: 2. Of those that a mesh axis runs over, the one named last changes fastest.
Arguments:
- tokens_in: bfloat16 [32768, 1024], P(('dp', 'row', 'col'))
- grad_out: bfloat16 [32768, 1024], P(('dp', 'row', 'col')), may hold values from -6 to 6
- gain_attn: bfloat16 [1024], P(('row', 'col')), may hold values from 0.099609375 to 1.8984375
- gain_ffn: bfloat16 [1024], P(('row', 'col')), may hold values from 0.099609375 to 1.8984375
- w_query: bfloat16 [1024, 1024], P('row', 'col'), may hold values from -0.1875 to 0.1875
- w_key: bfloat16 [1024, 1024], P('row', 'col'), may hold values from -0.1875 to 0.1875
- w_value: bfloat16 [1024, 1024], P('row', 'col'), may hold values from -0.1875 to 0.1875
- w_gate: bfloat16 [1024, 1024], P('row', 'col'), may hold values from -0.1875 to 0.1875
- w_out: bfloat16 [1024, 1024], P('row', 'col'), may hold values from -0.375 to 0.375
- w_ffn_gate: bfloat16 [1024, 2816], P('row', 'col'), may hold values from -0.1875 to 0.1875
- w_ffn_up: bfloat16 [1024, 2816], P('row', 'col'), may hold values from -0.1875 to 0.1875
- w_ffn_down: bfloat16 [2816, 1024], P('row', 'col'), may hold values from -0.109375 to 0.109375
- persist_key: bfloat16 [16, 1024], P(None, ('row', 'col')), may hold values from -6 to 6
- persist_value: bfloat16 [16, 1024], P(None, ('row', 'col')), may hold values from -6 to 6
- mem_rate: float32 [16, 8], P(None, 'col'), may hold values from 0.05 to 0.5
- mem_momentum: float32 [16, 8], P(None, 'col'), may hold values from 0.2 to 0.9
- mem_forget: float32 [16, 8], P(None, 'col'), may hold values from 0.002 to 0.5
- segment_ids: int32 [32768], P(('dp', 'row')), may hold values from 0 to 31, as said below
- decay_index: int32 [512], P(('dp', 'row')), may hold values from 0 to 15
Outputs:
- out: bfloat16 [32768, 1024], P(('dp', 'row', 'col'))
- grad_in: bfloat16 [32768, 1024], P(('dp', 'row', 'col'))
- g_query: float32 [1024, 1024], P('row', 'col')
- g_key: float32 [1024, 1024], P('row', 'col')
- g_value: float32 [1024, 1024], P('row', 'col')
- g_gate: float32 [1024, 1024], P('row', 'col')
- g_out: float32 [1024, 1024], P('row', 'col')
- g_ffn_gate: float32 [1024, 2816], P('row', 'col')
- g_ffn_up: float32 [1024, 2816], P('row', 'col')
- g_ffn_down: float32 [2816, 1024], P('row', 'col')
- g_gain_attn: float32 [1024], P(('row', 'col'))
- g_gain_ffn: float32 [1024], P(('row', 'col'))
- g_persist_key: float32 [16, 1024], P(None, ('row', 'col'))
- g_persist_value: float32 [16, 1024], P(None, ('row', 'col'))
- rms_stats: float32 [3], replicated
The draws below stay inside these ranges and needn't reach their ends.
Inputs may be any that keep to these rules, and one draw needn't show every extreme that they name: `segment_ids`: within each aligned sequence of 2048 tokens the ids start at 0, never fall, and change exactly at document starts; the last document of every sequence has id 2048 // 64 - 1. Documents cover whole aligned blocks of 64 tokens, and every sequence holds two documents or more.
All inputs are finite; a program needn't handle non-finite values.
Results may differ from the reference program's by a relative error of at most 0.015.
Values may be sent and summed in bfloat16 or wider, within the bound.
A program may use at most 256 MiB of HBM per device.

```python
import math
import jax
import jax.numpy as jnp
from jax import lax

D = 1024
H = 8
HD = 128
FF = 2816
P_SIZE = 16
SEG = 1024
CH = 64
NTAB = 16
SEQ = 2048
TOKENS = 32768
GROUP_TOK = 16384
NCHUNK = 512


def draw_tokens_in(key, part):
    index = jnp.arange(TOKENS)
    place = jnp.mod(index, GROUP_TOK).astype(jnp.float32)
    ramp = index.astype(jnp.float32) / TOKENS + place / GROUP_TOK - 1.0
    row_scale = jnp.exp(jnp.log(3.0) * ramp)[:, None]
    base = jax.random.normal(key, (TOKENS, D), jnp.float32)
    return (base * row_scale).astype(jnp.bfloat16)


def draw_segment_ids(key, part):
    sequences = TOKENS // SEQ
    per_seq = SEQ // CH
    coins = jax.random.randint(jax.random.fold_in(key, 1), (sequences, per_seq), 0, 12)
    forced = jax.random.randint(jax.random.fold_in(key, 2), (sequences, 1), 1, per_seq)
    column = jnp.arange(per_seq)[None, :]
    starts = ((coins == 0) | (column == 0) | (column == forced)).astype(jnp.int32)
    span_ids = jnp.cumsum(starts, axis=1) - 1
    last_id = jnp.max(span_ids, axis=1, keepdims=True)
    span_ids = jnp.where(span_ids == last_id, per_seq - 1, span_ids)
    return jnp.repeat(span_ids, CH, axis=1).reshape(TOKENS).astype(jnp.int32)


def with_ends(array, key, low, largest):
    dims = array.shape
    spot = [jax.random.randint(jax.random.fold_in(key, axis), (), 0, dims[axis]) for axis in range(len(dims))]
    array = array.at[tuple(spot)].set(low)
    longest = dims.index(max(dims))
    spot[longest] = (spot[longest] + 1) % dims[longest]
    return array.at[tuple(spot)].set(largest)


def block_scale(key, shape, shards, low, top_value):
    def one(axis_at, blocks):
        draws = jax.random.uniform(jax.random.fold_in(jax.random.fold_in(key, 6), axis_at), (blocks,), jnp.float32, low / len(shards), top_value / len(shards))
        return jnp.repeat(jnp.exp(draws), shape[axis_at] // blocks).reshape((-1,) + (1,) * (len(shape) - axis_at - 1))

    level = one(*shards[0])
    for cut in shards[1:]:
        level = level * one(*cut)
    return level


def bell_draw(own_key, dims, spread, bound, pieces=(), kind=jnp.bfloat16):
    loudness = block_scale(own_key, dims, pieces, -0.22, 0.18) if pieces else 1.0
    array = jax.random.normal(own_key, dims, jnp.float32) * spread * loudness
    return jnp.minimum(jnp.maximum(array, -bound), bound).astype(kind)


def setup_inputs(seed: int = 0) -> dict:
    seeds = jax.random.split(jax.random.key(seed), 20)
    tokens_in = draw_tokens_in(jax.random.fold_in(seeds[19], 71), 0)
    grad_out = bell_draw(seeds[1], (TOKENS, D), 1.0, 6.0, ((0, 32),))
    gain_attn = jnp.clip(1.0 + 0.18 * jax.random.normal(seeds[2], (D,), jnp.float32), 0.099609375, 1.8984375).astype(jnp.bfloat16)
    gain_ffn = jnp.clip(1.0 + 0.18 * jax.random.normal(seeds[3], (D,), jnp.float32), 0.099609375, 1.8984375).astype(jnp.bfloat16)
    w_query = bell_draw(seeds[4], (D, D), D ** -0.5, 0.1875, ((0, 8), (1, 2)))
    w_key = bell_draw(seeds[5], (D, D), D ** -0.5, 0.1875, ((0, 8), (1, 2)))
    w_value = bell_draw(seeds[6], (D, D), D ** -0.5, 0.1875, ((0, 8), (1, 2)))
    w_gate = bell_draw(seeds[7], (D, D), D ** -0.5, 0.1875, ((0, 8), (1, 2)))
    w_out = bell_draw(seeds[8], (D, D), (D // 4) ** -0.5, 0.375, ((0, 8), (1, 2)))
    w_ffn_gate = bell_draw(seeds[9], (D, FF), D ** -0.5, 0.1875, ((0, 8), (1, 2)))
    w_ffn_up = bell_draw(seeds[10], (D, FF), D ** -0.5, 0.1875, ((0, 8), (1, 2)))
    w_ffn_down = bell_draw(seeds[11], (FF, D), FF ** -0.5, 0.109375, ((0, 8), (1, 2)))
    persist_key = bell_draw(seeds[12], (P_SIZE, D), 1.0, 6.0, ((1, 16),))
    persist_value = bell_draw(seeds[13], (P_SIZE, D), 1.0, 6.0, ((1, 16),))
    mem_rate = jnp.clip(jnp.exp(math.log(0.5) - 2.3025851 * jax.random.uniform(seeds[14], (NTAB, H), jnp.float32) ** block_scale(seeds[14], (NTAB, H), ((1, 2),), -0.2, 0.2)), 0.05, 0.5)
    mem_momentum = jnp.clip(0.2 + 0.7 * jax.random.uniform(seeds[15], (NTAB, H), jnp.float32) ** block_scale(seeds[15], (NTAB, H), ((1, 2),), -0.2, 0.2), 0.2, 0.9)
    mem_forget = jnp.clip(jnp.exp(math.log(0.5) - 5.521461 * jax.random.uniform(seeds[16], (NTAB, H), jnp.float32) ** block_scale(seeds[16], (NTAB, H), ((1, 2),), -0.2, 0.2)), 0.002, 0.5)
    segment_ids = draw_segment_ids(jax.random.fold_in(seeds[19], 71), 0)
    decay_index = with_ends(jax.random.randint(seeds[18], (NCHUNK,), 0, NTAB), jax.random.fold_in(seeds[18], 1), 0, NTAB - 1).astype(jnp.int32)
    return dict(tokens_in=tokens_in, grad_out=grad_out, gain_attn=gain_attn, gain_ffn=gain_ffn, w_query=w_query, w_key=w_key, w_value=w_value, w_gate=w_gate, w_out=w_out, w_ffn_gate=w_ffn_gate, w_ffn_up=w_ffn_up, w_ffn_down=w_ffn_down, persist_key=persist_key, persist_value=persist_value, mem_rate=mem_rate, mem_momentum=mem_momentum, mem_forget=mem_forget, segment_ids=segment_ids, decay_index=decay_index)


EPS = 1e-06
NEG = -1e+30
HIGH = lax.Precision.HIGHEST

@jax.custom_vjp
def low(v):
    return lax.optimization_barrier(v.astype(jnp.bfloat16)).astype(jnp.float32)

@jax.custom_vjp
def low_back(v):
    return v

def low_keep(v):
    return (low(v), None)

def low_pass(kept, grad):
    return (grad,)

def back_keep(v):
    return (v, None)

def back_low(kept, grad):
    return (low(grad),)
low.defvjp(low_keep, low_pass)
low_back.defvjp(back_keep, back_low)

def matmul(first_op, second_op):
    return jnp.dot(first_op, second_op, precision=HIGH, preferred_element_type=jnp.float32)

def rms_norm(values, gain_vec):
    inverse = lax.rsqrt(lax.optimization_barrier(jnp.mean(values * values, axis=-1, keepdims=True)) + EPS)
    return values * inverse * gain_vec

def attend(inputs, fixed_keys, fixed_values):
    query_rows, key_rows, value_rows, seg_ids = inputs
    score_scale = HD ** (-0.5)
    tok_scores = low_back(jnp.einsum('qhd,khd->hqk', query_rows, key_rows, precision=HIGH) * score_scale)
    per_scores = low_back(jnp.einsum('qhd,phd->hqp', query_rows, fixed_keys, precision=HIGH) * score_scale)
    places = jnp.arange(SEG)
    allowed = (places[None, :] <= places[:, None]) & (seg_ids[None, :] == seg_ids[:, None])
    tok_scores = jnp.where(allowed[None, :, :], tok_scores, NEG)
    row_top = jnp.maximum(lax.optimization_barrier(jnp.max(tok_scores, axis=-1, keepdims=True)), lax.optimization_barrier(jnp.max(per_scores, axis=-1, keepdims=True)))
    tok_exp = jnp.exp(tok_scores - row_top)
    per_exp = jnp.exp(per_scores - row_top)
    row_total = lax.optimization_barrier(jnp.sum(tok_exp, axis=-1, keepdims=True)) + lax.optimization_barrier(jnp.sum(per_exp, axis=-1, keepdims=True))
    tok_prob = low(tok_exp / row_total)
    per_prob = low(per_exp / row_total)
    return jnp.einsum('hqk,khd->qhd', tok_prob, value_rows, precision=HIGH) + jnp.einsum('hqp,phd->qhd', per_prob, fixed_values, precision=HIGH)

def memory_read(query_rows, key_rows, value_rows, rate_rows, moment_rows, forget_rows, keep_flags):

    def advance(carry, inputs):
        memory, moment = carry
        span_query, span_key, span_value, span_rate, span_moment, span_forget, span_keep = inputs
        keep_now = span_keep[:, None, None, None]
        memory = memory * keep_now
        moment = moment * keep_now
        span_read = jnp.einsum('bchd,bhde->bche', span_query, memory, precision=HIGH)
        misfit = jnp.einsum('bchd,bhde->bche', span_key, memory, precision=HIGH) - span_value
        span_slope = jnp.einsum('bchd,bche->bhde', span_key, misfit, precision=HIGH)
        moment = span_moment[:, :, None, None] * moment - span_rate[:, :, None, None] * span_slope
        memory = (1.0 - span_forget[:, :, None, None]) * memory + moment
        return ((memory, moment), span_read)
    batch_size = query_rows.shape[1]
    empty_state = jnp.zeros((batch_size, H, HD, HD), jnp.float32)
    ignored, memory_reads = lax.scan(advance, (empty_state, empty_state), (query_rows, key_rows, value_rows, rate_rows, moment_rows, forget_rows, keep_flags))
    return memory_reads

def block_forward(params, tokens, seg_ids, span_index, tables):
    gain_attn, gain_ffn, w_query, w_key, w_value, w_gate, w_out, w_ffn_gate, w_ffn_up, w_ffn_down, persist_key, persist_value = params
    mem_rate, mem_momentum, mem_forget = tables
    row_count = tokens.shape[0]
    segments = row_count // SEG
    sequences = row_count // SEQ
    per_seq = SEQ // CH
    score_scale = HD ** (-0.5)
    normed = low(rms_norm(tokens, gain_attn))
    query_rows = low_back(low(matmul(normed, w_query)))
    key_rows = low_back(low(matmul(normed, w_key)))
    value_rows = low_back(low(matmul(normed, w_value)))
    gate_rows = low_back(low(matmul(normed, w_gate)))
    fixed_keys = persist_key.reshape(P_SIZE, H, HD)
    fixed_values = persist_value.reshape(P_SIZE, H, HD)

    def split_seg(values):
        return values.reshape(segments, SEG, H, HD)

    def attend_one(inputs):
        return attend(inputs, fixed_keys, fixed_values)
    attention = lax.map(jax.checkpoint(attend_one), (split_seg(query_rows), split_seg(key_rows), split_seg(value_rows), seg_ids.reshape(segments, SEG))).reshape(row_count, D)

    def to_scan(values):
        return values.reshape(sequences, per_seq, CH, H, HD).transpose(1, 0, 2, 3, 4)

    def table_rows(decay_table):
        return decay_table[span_index].reshape(sequences, per_seq, H).transpose(1, 0, 2)
    span_segs = seg_ids.reshape(sequences, per_seq, CH)
    same_doc = (span_segs[:, 1:, 0] == span_segs[:, :-1, CH - 1]).astype(jnp.float32)
    keep_flags = jnp.concatenate([jnp.zeros((sequences, 1), jnp.float32), same_doc], axis=1).T
    memory_reads = memory_read(to_scan(query_rows) * score_scale, to_scan(key_rows) * score_scale, to_scan(value_rows), table_rows(mem_rate), table_rows(mem_momentum), table_rows(mem_forget), keep_flags)
    memory_reads = memory_reads.transpose(1, 0, 2, 3, 4).reshape(row_count, D)
    combined = low_back(low(attention + jax.nn.sigmoid(gate_rows) * memory_reads))
    branch = low_back(matmul(combined, w_out))
    middle = tokens + branch
    normed2 = low(rms_norm(middle, gain_ffn))
    ffn_gate = low_back(matmul(normed2, w_ffn_gate))
    ffn_up = low_back(matmul(normed2, w_ffn_up))
    hidden = low(jax.nn.silu(ffn_gate) * ffn_up)
    ffn_out = low_back(matmul(hidden, w_ffn_down))
    final_rows = middle + ffn_out
    square_sums = jnp.stack([jnp.sum(tokens * tokens), jnp.sum(branch * branch), jnp.sum(final_rows * final_rows)])
    return (final_rows, square_sums)

def reference(tokens_in, grad_out, gain_attn, gain_ffn, w_query, w_key, w_value, w_gate, w_out, w_ffn_gate, w_ffn_up, w_ffn_down, persist_key, persist_value, mem_rate, mem_momentum, mem_forget, segment_ids, decay_index):
    params = tuple((weight.astype(jnp.float32) for weight in (gain_attn, gain_ffn, w_query, w_key, w_value, w_gate, w_out, w_ffn_gate, w_ffn_up, w_ffn_down, persist_key, persist_value)))
    tables = (mem_rate, mem_momentum, mem_forget)
    block_len = 2 * SEQ
    block_count = TOKENS // block_len
    tokens = tokens_in.astype(jnp.float32).reshape(block_count, block_len, D)
    seg_blocks = segment_ids.reshape(block_count, block_len)
    index_blocks = decay_index.reshape(block_count, block_len // CH)

    def whole_layer(layer_params, layer_tokens):

        def scan_step(running, inputs):
            part_tokens, part_segs, part_index = inputs
            result, square_sums = jax.checkpoint(block_forward)(layer_params, part_tokens, part_segs, part_index, tables)
            return (running + square_sums, result)
        square_sums, results = lax.scan(scan_step, jnp.zeros((3,), jnp.float32), (layer_tokens, seg_blocks, index_blocks))
        return (results, square_sums)
    results, pullback, square_sums = jax.vjp(whole_layer, params, tokens, has_aux=True)
    grads, grad_tokens = pullback(grad_out.astype(jnp.float32).reshape(block_count, block_len, D))
    rms_stats = jnp.sqrt(square_sums / (TOKENS * D))
    return (results.reshape(TOKENS, D).astype(jnp.bfloat16), grad_tokens.reshape(TOKENS, D).astype(jnp.bfloat16), grads[2], grads[3], grads[4], grads[5], grads[6], grads[7], grads[8], grads[9], grads[0], grads[1], grads[10], grads[11], rms_stats)
```

```python
import functools
import jax
import jax.numpy as jnp
from jax import lax
from jax.experimental import pallas as pl
from jax.experimental.pallas import tpu as pltpu
from jax.sharding import PartitionSpec as P

HD = 128
P_SIZE = 16
SEG = 1024
CH = 64
SEQ = 2048
TILE = 256
TPS = SEG // TILE
EPS = 1e-06
NEG = -1e30
SCALE = HD ** (-0.5)
LOG2E = 1.4426950408889634
VMEM_MAX = 60 * 1024 * 1024
F32 = jnp.float32
BF = jnp.bfloat16
HIGH = lax.Precision.HIGHEST
MESH = pl.DeviceIdType.MESH


def nn(a, b):
    return lax.dot_general(a, b, (((1,), (0,)), ((), ())), preferred_element_type=F32)


def nt(a, b):
    return lax.dot_general(a, b, (((1,), (1,)), ((), ())), preferred_element_type=F32)


def tn(a, b):
    return lax.dot_general(a, b, (((0,), (0,)), ((), ())), preferred_element_type=F32)


def token_bias(segc, segr, part):
    width = (part + 1) * TILE
    same = segc == segr[:, :width]
    qpos = lax.broadcasted_iota(jnp.int32, (TILE, width), 0) + part * TILE
    kpos = lax.broadcasted_iota(jnp.int32, (TILE, width), 1)
    return jnp.where(same & (kpos <= qpos), 0.0, NEG).astype(F32)


def mix_forward_tile(heads, part, tile, q_ref, k_ref, v_ref, g_ref, pk_ref, pv_ref, segc_ref,
                     segr_ref, coef_ref, comb_ref, lse_ref, reads_ref, m0_ref, err_ref, mem, mom):
    width = (part + 1) * TILE
    base = part * TILE
    bias = token_bias(segc_ref[...], segr_ref[...], part)
    pcol = lax.broadcasted_iota(jnp.int32, (TILE, HD), 1)
    lane = lax.broadcasted_iota(jnp.int32, (TILE, HD), 1)
    lse_all = jnp.zeros((TILE, HD), F32)
    blocks = TILE // CH
    for head in range(heads):
        cols = slice(head * HD, (head + 1) * HD)
        query = q_ref[:, cols]
        state = mem[head]
        speed = mom[head]
        reads = []
        for step in range(blocks):
            rows = slice(step * CH, (step + 1) * CH)
            at = tile * blocks + step
            keep = coef_ref[0, at * heads + head]
            rate = coef_ref[1, at * heads + head]
            moment = coef_ref[2, at * heads + head]
            stay = coef_ref[3, at * heads + head]
            start = state * keep
            low_start = start.astype(BF)
            m0_ref[step, head] = low_start
            rest = (start - low_start.astype(F32)).astype(BF)
            key = k_ref[base + step * CH:base + (step + 1) * CH, cols]
            value = v_ref[base + step * CH:base + (step + 1) * CH, cols]
            both = jnp.concatenate([query[rows], key], axis=0)
            got = nn(both, low_start) + nn(both, rest)
            reads.append(got[:CH] * SCALE)
            err = (got[CH:] * SCALE - value.astype(F32)).astype(BF)
            err_ref[rows, cols] = err
            slope = tn(key, err)
            speed = (moment * keep) * speed - (rate * SCALE) * slope
            state = stay * start + speed
        mem[head] = state
        mom[head] = speed
        read = jnp.concatenate(reads, axis=0)
        reads_ref[:, cols] = read.astype(BF)
        tok = nt(query, k_ref[:width, cols]) * (SCALE * LOG2E) + bias
        per = nt(query, pk_ref[:, cols]) * (SCALE * LOG2E)
        per = jnp.where(pcol < P_SIZE, per, NEG)
        top = jnp.maximum(jnp.max(tok, axis=1, keepdims=True), jnp.max(per, axis=1, keepdims=True))
        tok_e = jnp.exp2(tok - top)
        per_e = jnp.exp2(per - top)
        total = jnp.sum(tok_e, axis=1, keepdims=True) + jnp.sum(per_e, axis=1, keepdims=True)
        att = nn(tok_e.astype(BF), v_ref[:width, cols]) + nn(per_e.astype(BF), pv_ref[:, cols])
        att = att / total
        lse_all = jnp.where(lane == head, top + jnp.log2(total), lse_all)
        gate = jax.nn.sigmoid(g_ref[:, cols].astype(F32))
        comb_ref[:, cols] = (att + gate * read).astype(BF)
    lse_ref[...] = lse_all


def mix_forward_kernel(heads, q_ref, k_ref, v_ref, g_ref, pk_ref, pv_ref, segc_ref, segr_ref,
                       coef_ref, comb_ref, lse_ref, reads_ref, m0_ref, err_ref, mem, mom):
    tile = pl.program_id(0)

    @pl.when(tile == 0)
    def clear():
        mem[...] = jnp.zeros_like(mem)
        mom[...] = jnp.zeros_like(mom)

    for part in range(TPS):
        @pl.when(lax.rem(tile, TPS) == part)
        def work():
            mix_forward_tile(heads, part, tile, q_ref, k_ref, v_ref, g_ref, pk_ref, pv_ref,
                             segc_ref, segr_ref, coef_ref, comb_ref, lse_ref, reads_ref, m0_ref,
                             err_ref, mem, mom)


def mix_forward(qkvg, pkey, pvalue, segc, segr, coef, heads):
    total = qkvg.shape[0]
    width = heads * HD
    tiles = total // TILE
    per = TILE // CH
    return pl.pallas_call(
        functools.partial(mix_forward_kernel, heads),
        grid=(tiles,),
        in_specs=[
            pl.BlockSpec((TILE, width), lambda t: (t, 0)),
            pl.BlockSpec((SEG, width), lambda t: (t // TPS, 1)),
            pl.BlockSpec((SEG, width), lambda t: (t // TPS, 2)),
            pl.BlockSpec((TILE, width), lambda t: (t, 3)),
            pl.BlockSpec((HD, width), lambda t: (0, 0)),
            pl.BlockSpec((HD, width), lambda t: (0, 0)),
            pl.BlockSpec((TILE, 1), lambda t: (t, 0)),
            pl.BlockSpec((1, SEG), lambda t: (0, t // TPS)),
            pl.BlockSpec(memory_space=pltpu.SMEM),
        ],
        out_specs=[
            pl.BlockSpec((TILE, width), lambda t: (t, 0)),
            pl.BlockSpec((TILE, HD), lambda t: (t, 0)),
            pl.BlockSpec((TILE, width), lambda t: (t, 0)),
            pl.BlockSpec((per, heads, HD, HD), lambda t: (t, 0, 0, 0)),
            pl.BlockSpec((TILE, width), lambda t: (t, 0)),
        ],
        out_shape=[
            jax.ShapeDtypeStruct((total, width), BF),
            jax.ShapeDtypeStruct((total, HD), F32),
            jax.ShapeDtypeStruct((total, width), BF),
            jax.ShapeDtypeStruct((total // CH, heads, HD, HD), BF),
            jax.ShapeDtypeStruct((total, width), BF),
        ],
        scratch_shapes=[pltpu.VMEM((heads, HD, HD), F32), pltpu.VMEM((heads, HD, HD), F32)],
        compiler_params=pltpu.CompilerParams(vmem_limit_bytes=VMEM_MAX),
        name="mix_forward",
    )(qkvg, qkvg, qkvg, qkvg, pkey, pvalue, segc, segr, coef)


def mix_backward_tile(heads, part, tile, q_ref, k_ref, v_ref, g_ref, dc_ref, pk_ref, pv_ref,
                      segc_ref, segr_ref, coef_ref, lse_ref, reads_ref, m0_ref, err_ref, dout_ref,
                      dmem, dmom, dk_acc, dv_acc, dpk_acc, dpv_acc):
    width = (part + 1) * TILE
    base = part * TILE
    wide = heads * HD
    bias = token_bias(segc_ref[...], segr_ref[...], part)
    pcol = lax.broadcasted_iota(jnp.int32, (TILE, HD), 1)
    blocks = TILE // CH
    lse_all = lse_ref[...]
    for head in range(heads):
        cols = slice(head * HD, (head + 1) * HD)
        query = q_ref[:, cols]
        up = dc_ref[:, cols]
        upf = up.astype(F32)
        gate = jax.nn.sigmoid(g_ref[:, cols].astype(F32))
        dread = (upf * gate).astype(BF)
        dgate = upf * reads_ref[:, cols].astype(F32) * gate * (1.0 - gate)
        dout_ref[:, 3 * wide + head * HD:3 * wide + (head + 1) * HD] = dgate.astype(BF)
        dstate = dmem[head]
        dspeed = dmom[head]
        dq_mem, dk_mem, dv_mem = [None] * blocks, [None] * blocks, [None] * blocks
        for step in reversed(range(blocks)):
            rows = slice(step * CH, (step + 1) * CH)
            at = tile * blocks + step
            keep = coef_ref[0, at * heads + head]
            rate = coef_ref[1, at * heads + head]
            moment = coef_ref[2, at * heads + head]
            stay = coef_ref[3, at * heads + head]
            key = k_ref[base + step * CH:base + (step + 1) * CH, cols]
            start = m0_ref[step, head]
            err = err_ref[rows, cols]
            dspeed = dspeed + dstate
            dslope = (dspeed * (-rate)).astype(BF)
            derr = nn(key, dslope) * SCALE
            derr_low = derr.astype(BF)
            top = jnp.concatenate([dread[rows], derr_low], axis=0)
            both = jnp.concatenate([query[rows], key], axis=0)
            dstart = stay * dstate + SCALE * tn(both, top)
            back = nt(top, start)
            dq_mem[step] = back[:CH]
            dk_mem[step] = back[CH:] + nt(err, dslope)
            dv_mem[step] = derr
            dspeed = (moment * keep) * dspeed
            dstate = keep * dstart
        dmem[head] = dstate
        dmom[head] = dspeed
        tok = nt(query, k_ref[:width, cols]) * (SCALE * LOG2E) + bias
        per = nt(query, pk_ref[:, cols]) * (SCALE * LOG2E)
        per = jnp.where(pcol < P_SIZE, per, NEG)
        lse = lse_all[:, head:head + 1]
        tok_p = jnp.exp2(tok - lse)
        per_p = jnp.exp2(per - lse)
        tok_dp = nt(up, v_ref[:width, cols])
        per_dp = nt(up, pv_ref[:, cols])
        inner = jnp.sum(tok_p * tok_dp, axis=1, keepdims=True) + jnp.sum(
            per_p * per_dp, axis=1, keepdims=True)
        tok_ds = (tok_p * (tok_dp - inner)).astype(BF)
        per_ds = (per_p * (per_dp - inner)).astype(BF)
        dquery = nn(tok_ds, k_ref[:width, cols]) + nn(per_ds, pk_ref[:, cols])
        dquery = (dquery + jnp.concatenate(dq_mem, axis=0)) * SCALE
        dout_ref[:, cols] = dquery.astype(BF)
        dkey = tn(tok_ds, query)
        dval = tn(tok_p.astype(BF), up)
        dpk_acc[:, cols] += tn(per_ds, query) * SCALE
        dpv_acc[:, cols] += tn(per_p.astype(BF), up)
        own = slice(base, base + TILE)
        if part == TPS - 1:
            dk_acc[:base, cols] = dkey[:base]
            dv_acc[:base, cols] = dval[:base]
            dk_own, dv_own = dkey[base:], dval[base:]
        else:
            if part:
                dk_acc[:base, cols] += dkey[:base]
                dv_acc[:base, cols] += dval[:base]
            dk_own = dk_acc[own, cols] + dkey[base:]
            dv_own = dv_acc[own, cols] + dval[base:]
        dout_ref[:, wide + head * HD:wide + (head + 1) * HD] = (
            (dk_own + jnp.concatenate(dk_mem, axis=0)) * SCALE).astype(BF)
        dout_ref[:, 2 * wide + head * HD:2 * wide + (head + 1) * HD] = (
            dv_own - jnp.concatenate(dv_mem, axis=0)).astype(BF)


def mix_backward_kernel(heads, tiles, q_ref, k_ref, v_ref, g_ref, dc_ref, pk_ref, pv_ref, segc_ref,
                        segr_ref, coef_ref, lse_ref, reads_ref, m0_ref, err_ref, dout_ref, dpk_ref,
                        dpv_ref, dmem, dmom, dk_acc, dv_acc):
    turn = pl.program_id(0)
    tile = tiles - 1 - turn

    @pl.when(turn == 0)
    def clear():
        dmem[...] = jnp.zeros_like(dmem)
        dmom[...] = jnp.zeros_like(dmom)
        dpk_ref[...] = jnp.zeros_like(dpk_ref)
        dpv_ref[...] = jnp.zeros_like(dpv_ref)

    for part in range(TPS):
        @pl.when(lax.rem(tile, TPS) == part)
        def work():
            mix_backward_tile(heads, part, tile, q_ref, k_ref, v_ref, g_ref, dc_ref, pk_ref, pv_ref,
                              segc_ref, segr_ref, coef_ref, lse_ref, reads_ref, m0_ref, err_ref,
                              dout_ref, dmem, dmom, dk_acc, dv_acc, dpk_ref, dpv_ref)


def mix_backward(qkvg, dcomb, pkey, pvalue, segc, segr, coef, lse, reads, m0, err, heads):
    total = qkvg.shape[0]
    width = heads * HD
    tiles = total // TILE
    per = TILE // CH
    last = tiles - 1
    return pl.pallas_call(
        functools.partial(mix_backward_kernel, heads, tiles),
        grid=(tiles,),
        in_specs=[
            pl.BlockSpec((TILE, width), lambda t: (last - t, 0)),
            pl.BlockSpec((SEG, width), lambda t: ((last - t) // TPS, 1)),
            pl.BlockSpec((SEG, width), lambda t: ((last - t) // TPS, 2)),
            pl.BlockSpec((TILE, width), lambda t: (last - t, 3)),
            pl.BlockSpec((TILE, width), lambda t: (last - t, 0)),
            pl.BlockSpec((HD, width), lambda t: (0, 0)),
            pl.BlockSpec((HD, width), lambda t: (0, 0)),
            pl.BlockSpec((TILE, 1), lambda t: (last - t, 0)),
            pl.BlockSpec((1, SEG), lambda t: (0, (last - t) // TPS)),
            pl.BlockSpec(memory_space=pltpu.SMEM),
            pl.BlockSpec((TILE, HD), lambda t: (last - t, 0)),
            pl.BlockSpec((TILE, width), lambda t: (last - t, 0)),
            pl.BlockSpec((per, heads, HD, HD), lambda t: (last - t, 0, 0, 0)),
            pl.BlockSpec((TILE, width), lambda t: (last - t, 0)),
        ],
        out_specs=[
            pl.BlockSpec((TILE, 4 * width), lambda t: (last - t, 0)),
            pl.BlockSpec((HD, width), lambda t: (0, 0)),
            pl.BlockSpec((HD, width), lambda t: (0, 0)),
        ],
        out_shape=[
            jax.ShapeDtypeStruct((total, 4 * width), BF),
            jax.ShapeDtypeStruct((HD, width), F32),
            jax.ShapeDtypeStruct((HD, width), F32),
        ],
        scratch_shapes=[
            pltpu.VMEM((heads, HD, HD), F32),
            pltpu.VMEM((heads, HD, HD), F32),
            pltpu.VMEM((SEG, width), F32),
            pltpu.VMEM((SEG, width), F32),
        ],
        compiler_params=pltpu.CompilerParams(vmem_limit_bytes=VMEM_MAX),
        name="mix_backward",
    )(qkvg, qkvg, qkvg, qkvg, dcomb, pkey, pvalue, segc, segr, coef, lse, reads, m0, err)


def ffn_kernel(tiles, comb_ref, x_ref, dy_ref, wo_ref, wg_ref, wu_ref, wd_ref, gain_ref, out_ref,
               dmid_ref, dcomb_ref, go_ref, gg_ref, gu_ref, gd_ref, dgain_ref, sums_ref, n2, n2t,
               mid, acc_out, acc_dn, hid_all, pair_all):
    turn = pl.program_id(0)
    rows_all, dim = x_ref.shape
    steps = rows_all // TILE
    ft = wg_ref.shape[1]
    gain = gain_ref[...]

    @pl.when(turn == 0)
    def first():
        sums_ref[...] = jnp.zeros_like(sums_ref)
        dgain_ref[...] = jnp.zeros_like(dgain_ref)
        for i in range(steps):
            rows = slice(i * TILE, (i + 1) * TILE)
            xf = x_ref[rows, :].astype(F32)
            branch = nn(comb_ref[rows, :], wo_ref[...])
            middle = xf + branch
            mid[rows, :] = middle
            acc_out[rows, :] = middle
            inv = lax.rsqrt(jnp.mean(middle * middle, axis=1, keepdims=True) + EPS)
            normed = (middle * inv * gain).astype(BF)
            n2[rows, :] = normed
            n2t[:, rows] = normed.T
            acc_dn[rows, :] = jnp.zeros((TILE, dim), F32)
            sums_ref[0:1, :] += jnp.sum(xf * xf, axis=0, keepdims=True)
            sums_ref[1:2, :] += jnp.sum(branch * branch, axis=0, keepdims=True)

    wd = wd_ref[...]
    both = jnp.concatenate([wg_ref[...], wu_ref[...]], axis=1)
    for i in range(steps):
        rows = slice(i * TILE, (i + 1) * TILE)
        gateup = nn(n2[rows, :], both)
        gate, up = gateup[:, :ft], gateup[:, ft:]
        dh = nt(dy_ref[rows, :], wd)
        sig = jax.nn.sigmoid(gate)
        silu = gate * sig
        hid = (silu * up).astype(BF)
        dg = (dh * up * (sig * (1.0 + gate * (1.0 - sig)))).astype(BF)
        du = (dh * silu).astype(BF)
        hid_all[rows, :] = hid
        pair = jnp.concatenate([dg, du], axis=1)
        pair_all[rows, :] = pair
        acc_out[rows, :] += nn(hid, wd)
        acc_dn[rows, :] += nt(pair, both)
    gd_ref[...] = tn(hid_all[...], dy_ref[...]).astype(BF)
    grads = nn(n2t[...], pair_all[...])
    gg_ref[...] = grads[:, :ft].astype(BF)
    gu_ref[...] = grads[:, ft:].astype(BF)

    @pl.when(turn == tiles - 1)
    def last():
        for i in range(steps):
            rows = slice(i * TILE, (i + 1) * TILE)
            final = acc_out[rows, :]
            out_ref[rows, :] = final.astype(BF)
            sums_ref[2:3, :] += jnp.sum(final * final, axis=0, keepdims=True)
            middle = mid[rows, :]
            inv = lax.rsqrt(jnp.mean(middle * middle, axis=1, keepdims=True) + EPS)
            dnorm = acc_dn[rows, :]
            weighted = dnorm * gain
            inner = jnp.mean(weighted * middle, axis=1, keepdims=True)
            dgain_ref[...] += jnp.sum(dnorm * middle * inv, axis=0, keepdims=True)
            dmid = dy_ref[rows, :].astype(F32) + weighted * inv - middle * (inv * inv * inv) * inner
            low = dmid.astype(BF)
            dmid_ref[rows, :] = low
            dcomb_ref[rows, :] = nt(low, wo_ref[...]).astype(BF)
        for i in range(dim // TILE):
            part = slice(i * TILE, (i + 1) * TILE)
            go_ref[part, :] = tn(comb_ref[:, part], dmid_ref[...]).astype(BF)


def whole(shape):
    return pl.BlockSpec(shape, lambda t: (0,) * len(shape), pipeline_mode=pl.Buffered(1))


def ffn_block(comb, x, dy, w_out, w_gate, w_up, w_down, gain):
    rows, dim = x.shape
    hidden = w_gate.shape[1]
    tiles = hidden // TILE
    full = (rows, dim)
    return pl.pallas_call(
        functools.partial(ffn_kernel, tiles),
        grid=(tiles,),
        in_specs=[
            whole(full),
            whole(full),
            whole(full),
            whole((dim, dim)),
            pl.BlockSpec((dim, TILE), lambda t: (0, t)),
            pl.BlockSpec((dim, TILE), lambda t: (0, t)),
            pl.BlockSpec((TILE, dim), lambda t: (t, 0)),
            whole((1, dim)),
        ],
        out_specs=[
            whole(full),
            whole(full),
            whole(full),
            whole((dim, dim)),
            pl.BlockSpec((dim, TILE), lambda t: (0, t)),
            pl.BlockSpec((dim, TILE), lambda t: (0, t)),
            pl.BlockSpec((TILE, dim), lambda t: (t, 0)),
            whole((1, dim)),
            whole((8, dim)),
        ],
        out_shape=[
            jax.ShapeDtypeStruct(full, BF),
            jax.ShapeDtypeStruct(full, BF),
            jax.ShapeDtypeStruct(full, BF),
            jax.ShapeDtypeStruct((dim, dim), BF),
            jax.ShapeDtypeStruct((dim, hidden), BF),
            jax.ShapeDtypeStruct((dim, hidden), BF),
            jax.ShapeDtypeStruct((hidden, dim), BF),
            jax.ShapeDtypeStruct((1, dim), F32),
            jax.ShapeDtypeStruct((8, dim), F32),
        ],
        scratch_shapes=[
            pltpu.VMEM(full, BF),
            pltpu.VMEM((dim, rows), BF),
            pltpu.VMEM(full, F32),
            pltpu.VMEM(full, F32),
            pltpu.VMEM(full, F32),
            pltpu.VMEM((rows, TILE), BF),
            pltpu.VMEM((rows, 2 * TILE), BF),
        ],
        compiler_params=pltpu.CompilerParams(vmem_limit_bytes=VMEM_MAX),
        name="ffn_block",
    )(comb, x, dy, w_out, w_gate, w_up, w_down, gain)


def ring_place(row, n):
    return jnp.where(lax.rem(row, 2) == 0, row // 2, n - 1 - row // 2)


def ring_row(place, n):
    return jnp.where(place < n // 2, 2 * place, 2 * (n - place) - 1)


def split_cols(width, flip):
    tiles = width // HD
    first = (tiles + (0 if flip else 1)) // 2 * HD
    return ((0, first), (first, width - first))


def mod(value, n):
    return lax.rem(value + n, n)


def neighbours(n):
    me = ring_place(lax.axis_index("row"), n)
    return me, ring_row(mod(me + 1, n), n), ring_row(mod(me - 1, n), n)


def greet(n, right, left, use_col, use_dp):
    barrier = pltpu.get_barrier_semaphore()
    count = 2
    for target in (right, left):
        pl.semaphore_signal(barrier, inc=1, device_id={"row": target}, device_id_type=MESH)
    if use_col:
        other = 1 - lax.axis_index("col")
        pl.semaphore_signal(barrier, inc=1, device_id={"col": other}, device_id_type=MESH)
        count += 1
    if use_dp:
        twin = 1 - lax.axis_index("dp")
        pl.semaphore_signal(barrier, inc=1, device_id={"dp": twin}, device_id_type=MESH)
        count += 1
    pl.semaphore_wait(barrier, count)


class Gather:
    def __init__(self, n, items, sems):
        self.n = n
        self.items = items
        self.send, self.recv, self.local, self.csend, self.crecv = sems
        self.me, self.right, self.left = neighbours(n)
        self.row = lax.axis_index("row")
        self.other = 1 - lax.axis_index("col")

    def hop(self, m, d, s):
        block, whole_ref, base, share = self.items[m]
        place = mod(self.me - s, self.n) if d == 0 else mod(self.me + s, self.n)
        owner = ring_row(place, self.n)
        start, size = split_cols(block.shape[1], m % 2)[d]
        spot = whole_ref.at[owner, :, pl.ds(base + start, size)]
        return owner, start, size, spot

    def ring(self, m, d, s, first=False):
        block = self.items[m][0]
        owner, start, size, spot = self.hop(m, d, s)
        source = block.at[:, pl.ds(start, size)] if first else spot
        return pltpu.make_async_remote_copy(
            src_ref=source, dst_ref=spot, send_sem=self.send.at[m, d, s], recv_sem=self.recv.at[m, d, s],
            device_id={"row": self.right if d == 0 else self.left}, device_id_type=MESH)

    def across(self, m, source, spot):
        return pltpu.make_async_remote_copy(
            src_ref=source, dst_ref=spot, send_sem=self.csend.at[m], recv_sem=self.crecv.at[m],
            device_id={"col": self.other}, device_id_type=MESH)

    def keep(self, m):
        block, whole_ref, base, share = self.items[m]
        return pltpu.make_async_copy(
            block, whole_ref.at[self.row, :, pl.ds(base, block.shape[1])], self.local.at[m])

    def begin(self, ms):
        for m in ms:
            for d in (0, 1):
                self.ring(m, d, 0, first=True).start()
        for m in ms:
            block, whole_ref, base, share = self.items[m]
            self.keep(m).start()
            if share:
                self.across(m, block, whole_ref.at[self.row, :, pl.ds(base, block.shape[1])]).start()

    def advance(self, m, s):
        for d in (0, 1):
            self.ring(m, d, s).wait_recv()

            @pl.when(s < self.n - 2)
            def on():
                self.ring(m, d, s + 1).start()

            if self.items[m][3]:
                spot = self.hop(m, d, s + 1)[3]
                self.across(m, spot, spot).start()

    def finish(self, ms):
        for m in ms:
            block, whole_ref, base, share = self.items[m]
            self.keep(m).wait()
            if share:
                spot = whole_ref.at[:, :, pl.ds(base, block.shape[1])]
                theirs = whole_ref.at[:, :, pl.ds(self.other * block.shape[1], block.shape[1])]
                self.across(m, spot, theirs).wait_recv()
                self.across(m, spot, theirs).wait_send()

            def sent(s, carry):
                for d in (0, 1):
                    self.ring(m, d, s).wait_send()
                return carry

            lax.fori_loop(0, self.n - 1, sent, 0)


def gather_sems(n, count):
    return [
        pltpu.SemaphoreType.DMA((count, 2, n - 1)),
        pltpu.SemaphoreType.DMA((count, 2, n - 1)),
        pltpu.SemaphoreType.DMA((count,)),
        pltpu.SemaphoreType.DMA((count,)),
        pltpu.SemaphoreType.DMA((count,)),
    ]


def gather_kernel(n, first, *refs):
    blocks = refs[:8]
    x_ref = refs[8]
    wide, w_out, w_gate, w_up, w_down, pair = refs[9:15]
    sems = refs[15:20]
    xsems = refs[20]
    core = lax.axis_index("col")
    items = [(blocks[m], wide, m * blocks[m].shape[1], False) for m in range(4)]
    items += [(blocks[m], ref, core * blocks[m].shape[1], True)
              for m, ref in zip(range(4, 8), (w_out, w_gate, w_up, w_down))]
    g = Gather(n, items, sems)
    greet(n, g.right, g.left, True, False)
    g.begin(range(4))
    mine = pltpu.make_async_copy(x_ref, pair.at[core], xsems.at[0])
    mine.start()
    theirs = pltpu.make_async_remote_copy(
        src_ref=x_ref, dst_ref=pair.at[core], send_sem=xsems.at[1], recv_sem=xsems.at[2],
        device_id={"col": 1 - core}, device_id_type=MESH)
    theirs.start()
    g.begin(range(4, 8))

    def step(s, carry):
        for m in range(8):
            g.advance(m, s)
        return carry

    lax.fori_loop(0, n - 1, step, 0)
    g.finish(range(8))
    mine.wait()
    theirs.wait()


def gather_all(n, blocks, x):
    rows = [block.shape[0] for block in blocks]
    width = blocks[0].shape[1]
    any_spec = pl.BlockSpec(memory_space=pl.ANY)
    shapes = [(n, rows[0], 4 * width)] + [(n, rows[m], 2 * blocks[m].shape[1]) for m in range(4, 8)]
    shapes.append((2,) + x.shape)
    return pl.pallas_call(
        functools.partial(gather_kernel, n, 4),
        in_specs=[any_spec] * 9,
        out_specs=[any_spec] * 6,
        out_shape=[jax.ShapeDtypeStruct(shape, BF) for shape in shapes],
        scratch_shapes=gather_sems(n, 8) + [pltpu.SemaphoreType.DMA((3,))],
        compiler_params=pltpu.CompilerParams(collective_id=1, has_side_effects=True),
        name="gather_all",
    )(*blocks, x)


class Scatter:
    def __init__(self, n, items, sems):
        self.n = n
        self.items = items
        self.send, self.recv, self.local, self.csend, self.crecv, self.dsend, self.drecv = sems
        self.me, self.right, self.left = neighbours(n)
        self.row = lax.axis_index("row")
        self.core = lax.axis_index("col")
        self.twin = 1 - lax.axis_index("dp")

    def load(self, m):
        whole_ref, base, width, share, own = self.items[m][:5]
        return pltpu.make_async_copy(whole_ref.at[:, :, pl.ds(base, width)], own, self.local.at[m])

    def across(self, m):
        whole_ref, base, width, share, own, sib = self.items[m][:6]
        return pltpu.make_async_remote_copy(
            src_ref=whole_ref.at[:, :, pl.ds((1 - self.core) * width, width)], dst_ref=sib,
            send_sem=self.csend.at[m], recv_sem=self.crecv.at[m],
            device_id={"col": 1 - self.core}, device_id_type=MESH)

    def begin(self, ms):
        for m in ms:
            if self.items[m][3]:
                self.across(m).start()
            self.load(m).start()

    def ready(self, m):
        self.load(m).wait()
        if self.items[m][3]:
            self.across(m).wait_recv()

    def part(self, m, d, s):
        place = mod(self.me - 1 - s, self.n) if d == 0 else mod(self.me + 1 + s, self.n)
        start, size = split_cols(self.items[m][2], m % 2)[d]
        return ring_row(mod(place, self.n), self.n), slice(start, start + size)

    def ring(self, m, d, s):
        own, ring = self.items[m][4], self.items[m][6]
        owner, cols = self.part(m, d, s)
        return pltpu.make_async_remote_copy(
            src_ref=own.at[owner, :, cols], dst_ref=ring.at[s, :, cols],
            send_sem=self.send.at[m, d, s], recv_sem=self.recv.at[m, d, s],
            device_id={"row": self.right if d == 0 else self.left}, device_id_type=MESH)

    def total(self, m, d, s, arrived):
        whole_ref, base, width, share, own, sib, ring = self.items[m][:7]
        owner, cols = self.part(m, d, s)
        value = own[owner, :, cols].astype(F32)
        if share:
            value = value + sib[owner, :, cols].astype(F32)
        if arrived:
            value = value + ring[s - 1, :, cols].astype(F32)
        return owner, cols, value

    def start(self, m):
        for d in (0, 1):
            owner, cols, value = self.total(m, d, 0, False)
            if self.items[m][3]:
                self.items[m][4][owner, :, cols] = value.astype(BF)
            self.ring(m, d, 0).start()

    def advance(self, m, s):
        for d in (0, 1):
            self.ring(m, d, s - 1).wait_recv()
            owner, cols, value = self.total(m, d, s, True)
            self.items[m][4][owner, :, cols] = value.astype(BF)
            self.ring(m, d, s).start()

    def swap(self, m):
        low, twin = self.items[m][7:9]
        return pltpu.make_async_remote_copy(
            src_ref=low, dst_ref=twin, send_sem=self.dsend.at[m], recv_sem=self.drecv.at[m],
            device_id={"dp": self.twin}, device_id_type=MESH)

    def settle(self, m):
        for d in (0, 1):
            self.ring(m, d, self.n - 2).wait_recv()
            owner, cols, value = self.total(m, d, self.n - 1, True)
            self.items[m][7][:, cols] = value.astype(BF)
        self.swap(m).start()

    def finish(self, m):
        low, twin, out = self.items[m][7:10]
        self.swap(m).wait_recv()
        out[...] = low[...].astype(F32) + twin[...].astype(F32)
        self.swap(m).wait_send()
        if self.items[m][3]:
            self.across(m).wait_send()

        def sent(s, carry):
            for d in (0, 1):
                self.ring(m, d, s).wait_send()
            return carry

        lax.fori_loop(0, self.n - 1, sent, 0)


def scatter_sems(n, count):
    return [
        pltpu.SemaphoreType.DMA((count, 2, n - 1)),
        pltpu.SemaphoreType.DMA((count, 2, n - 1)),
    ] + [pltpu.SemaphoreType.DMA((count,))] * 5


def scatter_plan(arrays):
    scratch = []
    for array, width, share in arrays:
        n, rows, full = array.shape
        scratch.append(pltpu.VMEM((n, rows, width), BF))
        scratch.append(pltpu.VMEM((n, rows, width) if share else (1, 16, HD), BF))
        scratch.append(pltpu.VMEM((n - 1, rows, width), BF))
        scratch.append(pltpu.VMEM((rows, width), BF))
        scratch.append(pltpu.VMEM((rows, width), BF))
    return scratch


def scatter_kernel(n, count, *refs):
    wide, go, gg, gu, gd = refs[:5]
    outs = refs[5:5 + count]
    scratch = refs[5 + count:5 + 6 * count]
    sems = refs[5 + 6 * count:]
    core = lax.axis_index("col")
    items = []
    for m in range(count):
        ref = wide if m < 4 else (go, gg, gu, gd)[m - 4]
        width = outs[m].shape[1]
        base = m * width if m < 4 else core * width
        items.append((ref, base, width, m >= 4) + tuple(scratch[5 * m:5 * m + 5]) + (outs[m],))
    g = Scatter(n, items, sems)
    greet(n, g.right, g.left, True, True)
    order = (5, 6, 7, 4, 0, 1, 2, 3)
    g.begin(order)
    for m in order:
        g.ready(m)
        g.start(m)

    def step(s, carry):
        for m in order:
            g.advance(m, s)
        return carry

    lax.fori_loop(1, n - 1, step, 0)
    for m in order:
        g.settle(m)
    for m in order:
        g.finish(m)


def scatter_all(n, wide, go, gg, gu, gd):
    width = wide.shape[2] // 4
    arrays = [(wide, width, False)] * 4 + [(a, a.shape[2] // 2, True) for a in (go, gg, gu, gd)]
    count = len(arrays)
    any_spec = pl.BlockSpec(memory_space=pl.ANY)
    return pl.pallas_call(
        functools.partial(scatter_kernel, n, count),
        in_specs=[any_spec] * 5,
        out_specs=[pl.BlockSpec(memory_space=pltpu.VMEM)] * count,
        out_shape=[jax.ShapeDtypeStruct((a.shape[1], w), F32) for a, w, share in arrays],
        scratch_shapes=scatter_plan(arrays) + scatter_sems(n, count),
        compiler_params=pltpu.CompilerParams(
            collective_id=2, has_side_effects=True, vmem_limit_bytes=VMEM_MAX),
        name="scatter_all",
    )(wide, go, gg, gu, gd)


def local(
    tokens_in,
    grad_out,
    gain_attn,
    gain_ffn,
    w_query,
    w_key,
    w_value,
    w_gate,
    w_out,
    w_ffn_gate,
    w_ffn_up,
    w_ffn_down,
    persist_key,
    persist_value,
    mem_rate,
    mem_momentum,
    mem_forget,
    segment_ids,
    decay_index,
):
    n = lax.axis_size("row")
    core = lax.axis_index("col")
    local_tok, dim = tokens_in.shape
    heads = mem_rate.shape[1]
    width = heads * HD
    piece = gain_attn.shape[0]
    small = jnp.concatenate(
        [persist_key, persist_value, gain_attn[None, :], gain_ffn[None, :]], axis=0)
    small_all = lax.all_gather(small, ("row", "col"), axis=1, tiled=True)
    gain_a = small_all[2 * P_SIZE][None, :].astype(F32)
    gain_f = small_all[2 * P_SIZE + 1][None, :].astype(F32)
    own_small = lax.dynamic_slice_in_dim(small_all, core * width, width, 1)
    pad = ((0, HD - P_SIZE), (0, 0))
    pkey = jnp.pad(own_small[:P_SIZE], pad)
    pvalue = jnp.pad(own_small[P_SIZE:2 * P_SIZE], pad)

    blocks = (w_query, w_key, w_value, w_gate, w_out, w_ffn_gate, w_ffn_up, w_ffn_down)
    wide, full_out, full_gate, full_up, full_down, pair = gather_all(n, blocks, tokens_in)
    wide = wide.reshape(dim, 4 * width)
    full_out, full_gate, full_up = [a.reshape(dim, -1) for a in (full_out, full_gate, full_up)]
    full_down = full_down.reshape(-1, dim)

    inputs = pair.reshape(2 * local_tok, dim).astype(F32)
    inverse_a = lax.rsqrt(jnp.mean(inputs * inputs, axis=-1, keepdims=True) + EPS)
    normed = (inputs * inverse_a * gain_a).astype(BF)
    qkvg = nn(normed, wide).astype(BF)

    total = qkvg.shape[0]
    spans = total // CH
    span_ids = segment_ids.reshape(total // SEQ, SEQ // CH, CH)
    same = (span_ids[:, 1:, 0] == span_ids[:, :-1, CH - 1]).astype(F32)
    keep = jnp.concatenate([jnp.zeros((total // SEQ, 1), F32), same], axis=1).reshape(spans, 1)
    choose = (decay_index[:, None] == jnp.arange(mem_rate.shape[0])[None, :]).astype(F32)
    tables = jnp.concatenate([mem_rate, mem_momentum, 1.0 - mem_forget], axis=1)
    picked = jnp.dot(choose, tables, precision=HIGH)
    coef = jnp.stack(
        [jnp.broadcast_to(keep, (spans, heads))] + [picked[:, i * heads:(i + 1) * heads] for i in range(3)]
    ).reshape(4, spans * heads)
    segc, segr = segment_ids[:, None], segment_ids[None, :]

    comb, lse, reads, m0, err = mix_forward(qkvg, pkey, pvalue, segc, segr, coef, heads)
    comb_tok = lax.all_to_all(comb, "col", split_axis=0, concat_axis=1, tiled=True)
    result, dmid, dcomb_tok, go, gg, gu, gd, dgain_f, sums = ffn_block(
        comb_tok, tokens_in, grad_out, full_out, full_gate, full_up, full_down, gain_f)
    dcomb = lax.all_to_all(dcomb_tok, "col", split_axis=1, concat_axis=0, tiled=True)
    dqkvg, dpk, dpv = mix_backward(
        qkvg, dcomb, pkey, pvalue, segc, segr, coef, lse, reads, m0, err, heads)

    g_wide = tn(normed, dqkvg).astype(BF)
    back = nt(dqkvg, wide).astype(BF)
    mine = lax.dynamic_slice_in_dim(back, core * local_tok, local_tok, 0)
    theirs = lax.dynamic_slice_in_dim(back, (1 - core) * local_tok, local_tok, 0)
    theirs = lax.ppermute(theirs, "col", [(0, 1), (1, 0)])
    dnorm = mine.astype(F32) + theirs.astype(F32)
    xf = tokens_in.astype(F32)
    inv = lax.rsqrt(jnp.mean(xf * xf, axis=-1, keepdims=True) + EPS)
    weighted = dnorm * gain_a
    inner = jnp.mean(weighted * xf, axis=-1, keepdims=True)
    grad_in = (dmid.astype(F32) + weighted * inv - xf * (inv * inv * inv) * inner).astype(BF)
    dgain_a = jnp.sum(dnorm * xf * inv, axis=0)

    rows = dim // n
    hidden_rows = full_down.shape[0] // n
    grads = scatter_all(
        n,
        g_wide.reshape(n, rows, 4 * width),
        go.reshape(n, rows, dim),
        gg.reshape(n, rows, -1),
        gu.reshape(n, rows, -1),
        gd.reshape(n, hidden_rows, dim),
    )

    place = jnp.zeros((2 * P_SIZE, dim), F32)
    place = lax.dynamic_update_slice_in_dim(
        place, jnp.concatenate([dpk[:P_SIZE], dpv[:P_SIZE]], axis=0), core * width, 1)
    packed = jnp.concatenate([place, dgain_a[None, :], dgain_f, sums[:3]], axis=0)
    summed = lax.psum(packed, ("dp", "row", "col"))
    entry_count = local_tok * dim * lax.axis_size("dp") * n * lax.axis_size("col")
    rms_stats = jnp.sqrt(jnp.sum(summed[2 * P_SIZE + 2:], axis=1) / entry_count)
    slot = lax.axis_index("row") * 2 + core
    part = lax.dynamic_slice_in_dim(summed, slot * piece, piece, 1)
    return (
        result,
        grad_in,
        grads[0],
        grads[1],
        grads[2],
        grads[3],
        grads[4],
        grads[5],
        grads[6],
        grads[7],
        part[2 * P_SIZE],
        part[2 * P_SIZE + 1],
        part[:P_SIZE],
        part[P_SIZE:2 * P_SIZE],
        rms_stats,
    )


def solution(mesh):
    tokens = P(("dp", "row", "col"), None)
    vector = P(("row", "col"))
    weight = P("row", "col")
    persist = P(None, ("row", "col"))
    table = P(None, "col")
    ids = P(("dp", "row"))
    return jax.shard_map(
        local,
        mesh=mesh,
        in_specs=(tokens, tokens, vector, vector) + (weight,) * 8 + (persist,) * 2 + (table,) * 3 + (ids,) * 2,
        out_specs=(tokens, tokens) + (weight,) * 8 + (vector,) * 2 + (persist,) * 2 + (P(),),
        check_vma=False,
    )
```

```python
import functools
import jax
import jax.numpy as jnp
from jax import lax
from jax.experimental import pallas as pl
from jax.experimental.pallas import tpu as pltpu
from jax.sharding import PartitionSpec as P

HD = 128
P_SIZE = 16
SEG = 1024
CH = 64
SEQ = 2048
TILE = 256
TPS = SEG // TILE
EPS = 1e-06
NEG = -1e30
SCALE = HD ** (-0.5)
LOG2E = 1.4426950408889634
VMEM_MAX = 60 * 1024 * 1024
F32 = jnp.float32
BF = jnp.bfloat16
HIGH = lax.Precision.HIGHEST
MESH = pl.DeviceIdType.MESH


def nn(a, b):
    return lax.dot_general(a, b, (((1,), (0,)), ((), ())), preferred_element_type=F32)


def nt(a, b):
    return lax.dot_general(a, b, (((1,), (1,)), ((), ())), preferred_element_type=F32)


def tn(a, b):
    return lax.dot_general(a, b, (((0,), (0,)), ((), ())), preferred_element_type=F32)


def token_bias(segc, segr, part):
    width = (part + 1) * TILE
    same = segc == segr[:, :width]
    qpos = lax.broadcasted_iota(jnp.int32, (TILE, width), 0) + part * TILE
    kpos = lax.broadcasted_iota(jnp.int32, (TILE, width), 1)
    return jnp.where(same & (kpos <= qpos), 0.0, NEG).astype(F32)


def mix_forward_tile(heads, part, tile, q_ref, k_ref, v_ref, g_ref, pk_ref, pv_ref, segc_ref,
                     segr_ref, coef_ref, comb_ref, lse_ref, reads_ref, m0_ref, err_ref, mem, mom):
    width = (part + 1) * TILE
    base = part * TILE
    bias = token_bias(segc_ref[...], segr_ref[...], part)
    pcol = lax.broadcasted_iota(jnp.int32, (TILE, HD), 1)
    lane = lax.broadcasted_iota(jnp.int32, (TILE, HD), 1)
    lse_all = jnp.zeros((TILE, HD), F32)
    blocks = TILE // CH
    for head in range(heads):
        cols = slice(head * HD, (head + 1) * HD)
        query = q_ref[:, cols]
        state = mem[head]
        speed = mom[head]
        reads = []
        for step in range(blocks):
            rows = slice(step * CH, (step + 1) * CH)
            at = tile * blocks + step
            keep = coef_ref[0, at * heads + head]
            rate = coef_ref[1, at * heads + head]
            moment = coef_ref[2, at * heads + head]
            stay = coef_ref[3, at * heads + head]
            start = state * keep
            low_start = start.astype(BF)
            m0_ref[step, head] = low_start
            rest = (start - low_start.astype(F32)).astype(BF)
            key = k_ref[base + step * CH:base + (step + 1) * CH, cols]
            value = v_ref[base + step * CH:base + (step + 1) * CH, cols]
            both = jnp.concatenate([query[rows], key], axis=0)
            got = nn(both, low_start) + nn(both, rest)
            reads.append(got[:CH] * SCALE)
            err = (got[CH:] * SCALE - value.astype(F32)).astype(BF)
            err_ref[rows, cols] = err
            slope = tn(key, err)
            speed = (moment * keep) * speed - (rate * SCALE) * slope
            state = stay * start + speed
        mem[head] = state
        mom[head] = speed
        read = jnp.concatenate(reads, axis=0)
        reads_ref[:, cols] = read.astype(BF)
        tok = nt(query, k_ref[:width, cols]) * (SCALE * LOG2E) + bias
        per = nt(query, pk_ref[:, cols]) * (SCALE * LOG2E)
        per = jnp.where(pcol < P_SIZE, per, NEG)
        top = jnp.maximum(jnp.max(tok, axis=1, keepdims=True), jnp.max(per, axis=1, keepdims=True))
        tok_e = jnp.exp2(tok - top)
        per_e = jnp.exp2(per - top)
        total = jnp.sum(tok_e, axis=1, keepdims=True) + jnp.sum(per_e, axis=1, keepdims=True)
        att = nn(tok_e.astype(BF), v_ref[:width, cols]) + nn(per_e.astype(BF), pv_ref[:, cols])
        att = att / total
        lse_all = jnp.where(lane == head, top + jnp.log2(total), lse_all)
        gate = jax.nn.sigmoid(g_ref[:, cols].astype(F32))
        comb_ref[:, cols] = (att + gate * read).astype(BF)
    lse_ref[...] = lse_all


def hop_bound(turn, tiles, hops):
    return (turn * hops) // tiles


def mix_forward_kernel(heads, n, tiles, q_ref, k_ref, v_ref, g_ref, pk_ref, pv_ref, segc_ref,
                       segr_ref, coef_ref, b0, b1, b2, b3, lse_ref, reads_ref, m0_ref, err_ref,
                       comb_out, w0, w1, w2, w3, mem, mom, comb_all, csems, *sems):
    tile = pl.program_id(0)
    core = lax.axis_index("col")
    blocks, wholes = (b0, b1, b2, b3), (w0, w1, w2, w3)
    items = [(blk, ref, core * blk.shape[1], True) for blk, ref in zip(blocks, wholes)]
    g = Gather(n, items, sems)
    each = range(len(items))
    width = heads * HD
    per_core = tiles // 2

    def hops(low, high):
        def one(s, carry):
            for m in each:
                g.advance(m, s)
            return carry

        lax.fori_loop(low, high, one, 0)

    def place(device, index):
        return comb_out.at[pl.ds(index * TILE, TILE), pl.ds(device * width, width)]

    @pl.when(tile == 0)
    def clear():
        greet(n, g.right, g.left, True, False)
        g.begin(each)
        mem[...] = jnp.zeros_like(mem)
        mom[...] = jnp.zeros_like(mom)

    @pl.when(tile > 0)
    def pass_on():
        hops(hop_bound(tile - 1, tiles, n - 1), hop_bound(tile, tiles, n - 1))

    for part in range(TPS):
        @pl.when(lax.rem(tile, TPS) == part)
        def work():
            mix_forward_tile(heads, part, tile, q_ref, k_ref, v_ref, g_ref, pk_ref, pv_ref,
                             segc_ref, segr_ref, coef_ref, comb_all.at[tile], lse_ref, reads_ref,
                             m0_ref, err_ref, mem, mom)

    def stay(index):
        return pltpu.make_async_copy(
            comb_all.at[core * per_core + index], place(core, index), csems.at[0, index])

    def leave(index):
        return pltpu.make_async_remote_copy(
            src_ref=comb_all.at[(1 - core) * per_core + index], dst_ref=place(core, index),
            send_sem=csems.at[1, index], recv_sem=csems.at[2, index],
            device_id={"col": 1 - core}, device_id_type=MESH)

    index = lax.rem(tile, per_core)

    @pl.when(tile // per_core == core)
    def mine():
        stay(index).start()

    @pl.when(tile // per_core != core)
    def theirs():
        leave(index).start()

    @pl.when(tile == tiles - 1)
    def end():
        hops(hop_bound(tiles - 1, tiles, n - 1), n - 1)
        g.finish(each)
        for i in range(per_core):
            stay(i).wait()
            leave(i).wait()


def mix_forward(n, qkvg, pkey, pvalue, segc, segr, coef, heads, blocks):
    total = qkvg.shape[0]
    width = heads * HD
    tiles = total // TILE
    per = TILE // CH
    any_spec = pl.BlockSpec(memory_space=pl.ANY)
    return pl.pallas_call(
        functools.partial(mix_forward_kernel, heads, n, tiles),
        grid=(tiles,),
        in_specs=[
            pl.BlockSpec((TILE, width), lambda t: (t, 0)),
            pl.BlockSpec((SEG, width), lambda t: (t // TPS, 1)),
            pl.BlockSpec((SEG, width), lambda t: (t // TPS, 2)),
            pl.BlockSpec((TILE, width), lambda t: (t, 3)),
            pl.BlockSpec((HD, width), lambda t: (0, 0)),
            pl.BlockSpec((HD, width), lambda t: (0, 0)),
            pl.BlockSpec((TILE, 1), lambda t: (t, 0)),
            pl.BlockSpec((1, SEG), lambda t: (0, t // TPS)),
            pl.BlockSpec(memory_space=pltpu.SMEM),
        ] + [any_spec] * 4,
        out_specs=[
            pl.BlockSpec((TILE, HD), lambda t: (t, 0)),
            pl.BlockSpec((TILE, width), lambda t: (t, 0)),
            pl.BlockSpec((per, heads, HD, HD), lambda t: (t, 0, 0, 0)),
            pl.BlockSpec((TILE, width), lambda t: (t, 0)),
        ] + [any_spec] * 5,
        out_shape=[
            jax.ShapeDtypeStruct((total, HD), F32),
            jax.ShapeDtypeStruct((total, width), BF),
            jax.ShapeDtypeStruct((total // CH, heads, HD, HD), BF),
            jax.ShapeDtypeStruct((total, width), BF),
            jax.ShapeDtypeStruct((total // 2, 2 * width), BF),
        ] + [jax.ShapeDtypeStruct((n, b.shape[0], 2 * b.shape[1]), BF) for b in blocks],
        scratch_shapes=[
            pltpu.VMEM((heads, HD, HD), F32),
            pltpu.VMEM((heads, HD, HD), F32),
            pltpu.VMEM((tiles, TILE, width), BF),
            pltpu.SemaphoreType.DMA((3, tiles // 2)),
        ] + gather_sems(n, 4),
        compiler_params=pltpu.CompilerParams(
            collective_id=3, has_side_effects=True, vmem_limit_bytes=VMEM_MAX),
        name="mix_forward",
    )(qkvg, qkvg, qkvg, qkvg, pkey, pvalue, segc, segr, coef, *blocks)


def mix_backward_tile(heads, part, tile, q_ref, k_ref, v_ref, g_ref, dc_ref, pk_ref, pv_ref,
                      segc_ref, segr_ref, coef_ref, lse_ref, reads_ref, m0_ref, err_ref, dout_ref,
                      dmem, dmom, dk_acc, dv_acc, dpk_acc, dpv_acc):
    width = (part + 1) * TILE
    base = part * TILE
    wide = heads * HD
    bias = token_bias(segc_ref[...], segr_ref[...], part)
    pcol = lax.broadcasted_iota(jnp.int32, (TILE, HD), 1)
    blocks = TILE // CH
    lse_all = lse_ref[...]
    for head in range(heads):
        cols = slice(head * HD, (head + 1) * HD)
        query = q_ref[:, cols]
        up = dc_ref[:, cols]
        upf = up.astype(F32)
        gate = jax.nn.sigmoid(g_ref[:, cols].astype(F32))
        dread = (upf * gate).astype(BF)
        dgate = upf * reads_ref[:, cols].astype(F32) * gate * (1.0 - gate)
        dout_ref[:, 3 * wide + head * HD:3 * wide + (head + 1) * HD] = dgate.astype(BF)
        dstate = dmem[head]
        dspeed = dmom[head]
        dq_mem, dk_mem, dv_mem = [None] * blocks, [None] * blocks, [None] * blocks
        for step in reversed(range(blocks)):
            rows = slice(step * CH, (step + 1) * CH)
            at = tile * blocks + step
            keep = coef_ref[0, at * heads + head]
            rate = coef_ref[1, at * heads + head]
            moment = coef_ref[2, at * heads + head]
            stay = coef_ref[3, at * heads + head]
            key = k_ref[base + step * CH:base + (step + 1) * CH, cols]
            start = m0_ref[step, head]
            err = err_ref[rows, cols]
            dspeed = dspeed + dstate
            dslope = (dspeed * (-rate)).astype(BF)
            derr = nn(key, dslope) * SCALE
            derr_low = derr.astype(BF)
            top = jnp.concatenate([dread[rows], derr_low], axis=0)
            both = jnp.concatenate([query[rows], key], axis=0)
            dstart = stay * dstate + SCALE * tn(both, top)
            back = nt(top, start)
            dq_mem[step] = back[:CH]
            dk_mem[step] = back[CH:] + nt(err, dslope)
            dv_mem[step] = derr
            dspeed = (moment * keep) * dspeed
            dstate = keep * dstart
        dmem[head] = dstate
        dmom[head] = dspeed
        tok = nt(query, k_ref[:width, cols]) * (SCALE * LOG2E) + bias
        per = nt(query, pk_ref[:, cols]) * (SCALE * LOG2E)
        per = jnp.where(pcol < P_SIZE, per, NEG)
        lse = lse_all[:, head:head + 1]
        tok_p = jnp.exp2(tok - lse)
        per_p = jnp.exp2(per - lse)
        tok_dp = nt(up, v_ref[:width, cols])
        per_dp = nt(up, pv_ref[:, cols])
        inner = jnp.sum(tok_p * tok_dp, axis=1, keepdims=True) + jnp.sum(
            per_p * per_dp, axis=1, keepdims=True)
        tok_ds = (tok_p * (tok_dp - inner)).astype(BF)
        per_ds = (per_p * (per_dp - inner)).astype(BF)
        dquery = nn(tok_ds, k_ref[:width, cols]) + nn(per_ds, pk_ref[:, cols])
        dquery = (dquery + jnp.concatenate(dq_mem, axis=0)) * SCALE
        dout_ref[:, cols] = dquery.astype(BF)
        dkey = tn(tok_ds, query)
        dval = tn(tok_p.astype(BF), up)
        dpk_acc[:, cols] += tn(per_ds, query) * SCALE
        dpv_acc[:, cols] += tn(per_p.astype(BF), up)
        own = slice(base, base + TILE)
        if part == TPS - 1:
            dk_acc[:base, cols] = dkey[:base]
            dv_acc[:base, cols] = dval[:base]
            dk_own, dv_own = dkey[base:], dval[base:]
        else:
            if part:
                dk_acc[:base, cols] += dkey[:base]
                dv_acc[:base, cols] += dval[:base]
            dk_own = dk_acc[own, cols] + dkey[base:]
            dv_own = dv_acc[own, cols] + dval[base:]
        dout_ref[:, wide + head * HD:wide + (head + 1) * HD] = (
            (dk_own + jnp.concatenate(dk_mem, axis=0)) * SCALE).astype(BF)
        dout_ref[:, 2 * wide + head * HD:2 * wide + (head + 1) * HD] = (
            dv_own - jnp.concatenate(dv_mem, axis=0)).astype(BF)


def mix_backward_kernel(heads, n, tiles, q_ref, k_ref, v_ref, g_ref, dc_ref, pk_ref, pv_ref,
                        segc_ref, segr_ref, coef_ref, lse_ref, reads_ref, m0_ref, err_ref, *refs):
    own_refs, sib_refs = refs[:4], refs[4:8]
    dout_ref, dpk_ref, dpv_ref = refs[8:11]
    outs = refs[11:15]
    dmem, dmom, dk_acc, dv_acc = refs[15:19]
    scratch = refs[19:39]
    sems = refs[39:]
    turn = pl.program_id(0)
    tile = tiles - 1 - turn
    items = [
        (own_refs[m], 0, outs[m].shape[1], sib_refs[m]) + tuple(scratch[5 * m:5 * m + 5]) + (outs[m],)
        for m in range(4)
    ]
    g = Scatter(n, items, sems)
    order = (1, 2, 3, 0)

    def hops(low, high):
        def one(s, carry):
            for m in order:
                g.advance(m, s)
            return carry

        lax.fori_loop(low, high, one, 0)

    @pl.when(turn == 0)
    def clear():
        greet(n, g.right, g.left, False, True)
        g.begin(order)
        dmem[...] = jnp.zeros_like(dmem)
        dmom[...] = jnp.zeros_like(dmom)
        dpk_ref[...] = jnp.zeros_like(dpk_ref)
        dpv_ref[...] = jnp.zeros_like(dpv_ref)
        for m in order:
            g.ready(m)
            g.start(m)

    @pl.when(turn > 0)
    def pass_on():
        hops(1 + hop_bound(turn - 1, tiles - 1, n - 2), 1 + hop_bound(turn, tiles - 1, n - 2))

    for part in range(TPS):
        @pl.when(lax.rem(tile, TPS) == part)
        def work():
            mix_backward_tile(heads, part, tile, q_ref, k_ref, v_ref, g_ref, dc_ref, pk_ref, pv_ref,
                              segc_ref, segr_ref, coef_ref, lse_ref, reads_ref, m0_ref, err_ref,
                              dout_ref, dmem, dmom, dk_acc, dv_acc, dpk_ref, dpv_ref)

    @pl.when(turn == tiles - 1)
    def end():
        for m in order:
            g.settle(m)
        for m in order:
            g.finish(m)


def mix_backward(n, qkvg, dcomb, pkey, pvalue, segc, segr, coef, lse, reads, m0, err, heads, owns, sibs):
    total = qkvg.shape[0]
    width = heads * HD
    tiles = total // TILE
    per = TILE // CH
    last = tiles - 1
    any_spec = pl.BlockSpec(memory_space=pl.ANY)
    arrays = [(a, a.shape[2], True) for a in owns]
    return pl.pallas_call(
        functools.partial(mix_backward_kernel, heads, n, tiles),
        grid=(tiles,),
        in_specs=[
            pl.BlockSpec((TILE, width), lambda t: (last - t, 0)),
            pl.BlockSpec((SEG, width), lambda t: ((last - t) // TPS, 1)),
            pl.BlockSpec((SEG, width), lambda t: ((last - t) // TPS, 2)),
            pl.BlockSpec((TILE, width), lambda t: (last - t, 3)),
            pl.BlockSpec((TILE, width), lambda t: (last - t, 0)),
            pl.BlockSpec((HD, width), lambda t: (0, 0)),
            pl.BlockSpec((HD, width), lambda t: (0, 0)),
            pl.BlockSpec((TILE, 1), lambda t: (last - t, 0)),
            pl.BlockSpec((1, SEG), lambda t: (0, (last - t) // TPS)),
            pl.BlockSpec(memory_space=pltpu.SMEM),
            pl.BlockSpec((TILE, HD), lambda t: (last - t, 0)),
            pl.BlockSpec((TILE, width), lambda t: (last - t, 0)),
            pl.BlockSpec((per, heads, HD, HD), lambda t: (last - t, 0, 0, 0)),
            pl.BlockSpec((TILE, width), lambda t: (last - t, 0)),
        ] + [any_spec] * 8,
        out_specs=[
            pl.BlockSpec((TILE, 4 * width), lambda t: (last - t, 0)),
            pl.BlockSpec((HD, width), lambda t: (0, 0)),
            pl.BlockSpec((HD, width), lambda t: (0, 0)),
        ] + [whole((a.shape[1], w)) for a, w, share in arrays],
        out_shape=[
            jax.ShapeDtypeStruct((total, 4 * width), BF),
            jax.ShapeDtypeStruct((HD, width), F32),
            jax.ShapeDtypeStruct((HD, width), F32),
        ] + [jax.ShapeDtypeStruct((a.shape[1], w), F32) for a, w, share in arrays],
        scratch_shapes=[
            pltpu.VMEM((heads, HD, HD), F32),
            pltpu.VMEM((heads, HD, HD), F32),
            pltpu.VMEM((SEG, width), F32),
            pltpu.VMEM((SEG, width), F32),
        ] + scatter_plan(arrays) + scatter_sems(n, 4),
        compiler_params=pltpu.CompilerParams(
            collective_id=4, has_side_effects=True, vmem_limit_bytes=VMEM_MAX),
        name="mix_backward",
    )(qkvg, qkvg, qkvg, qkvg, dcomb, pkey, pvalue, segc, segr, coef, lse, reads, m0, err, *owns, *sibs)


def whole(shape):
    return pl.BlockSpec(shape, lambda t: (0,) * len(shape), pipeline_mode=pl.Buffered(1))


def ffn_kernel(tiles, comb_ref, x_ref, dy_ref, wo_ref, wg0, wg1, wu0, wu1, wd0, wd1, gain_ref,
               out_ref, dmid_ref, dgain_ref, sums_ref, dcomb_out, go_own, go_sib, gg_own, gg_sib,
               gu_own, gu_sib, gd_own, gd_sib, n2, n2t, mid, acc_out, acc_dn, hid_all, pair_all,
               dcomb_v, go_v, gbuf, ubuf, dbuf, keep_sem, send_sem, recv_sem, end_sem):
    turn = pl.program_id(0)
    core = lax.axis_index("col")
    other = 1 - core
    rows_all, dim = x_ref.shape
    half = dim // 2
    steps = rows_all // TILE
    ft = 2 * HD
    gain = gain_ref[...]
    slot = lax.rem(turn, 2)
    hidden_half = gg_own.shape[1]

    def push(src, dst, sem, rsem):
        return pltpu.make_async_remote_copy(
            src_ref=src, dst_ref=dst, send_sem=sem, recv_sem=rsem,
            device_id={"col": other}, device_id_type=MESH)

    def moves(t, s):
        stay, leave = [], []
        for i, (buf, own, sib) in enumerate(((gbuf, gg_own, gg_sib), (ubuf, gu_own, gu_sib))):
            cols = pl.ds(pl.multiple_of(t * HD, HD), HD)
            stay.append(pltpu.make_async_copy(
                buf.at[s, core], own.at[:, cols], keep_sem.at[i, s]))
            leave.append(push(buf.at[s, other], sib.at[:, cols], send_sem.at[i, s], recv_sem.at[i]))
        for i in range(2):
            rows = pl.ds(pl.multiple_of(i * hidden_half + t * HD, HD), HD)
            stay.append(pltpu.make_async_copy(
                dbuf.at[s, core, pl.ds(i * HD, HD)], gd_own.at[rows, :], keep_sem.at[2 + i, s]))
            leave.append(push(dbuf.at[s, other, pl.ds(i * HD, HD)], gd_sib.at[rows, :],
                              send_sem.at[2 + i, s], recv_sem.at[2 + i]))
        return stay, leave

    def settle(t, s):
        stay, leave = moves(t, s)
        for copy in stay:
            copy.wait()
        for copy in leave:
            copy.wait_send()

    @pl.when(turn == 0)
    def first():
        barrier = pltpu.get_barrier_semaphore()
        pl.semaphore_signal(barrier, inc=1, device_id={"col": other}, device_id_type=MESH)
        pl.semaphore_wait(barrier, 1)
        sums_ref[...] = jnp.zeros_like(sums_ref)
        dgain_ref[...] = jnp.zeros_like(dgain_ref)
        for i in range(steps):
            rows = slice(i * TILE, (i + 1) * TILE)
            xf = x_ref[rows, :].astype(F32)
            branch = nn(comb_ref[rows, :], wo_ref[...])
            middle = xf + branch
            mid[rows, :] = middle
            acc_out[rows, :] = middle
            inv = lax.rsqrt(jnp.mean(middle * middle, axis=1, keepdims=True) + EPS)
            normed = (middle * inv * gain).astype(BF)
            n2[rows, :] = normed
            n2t[:, rows] = normed.T
            acc_dn[rows, :] = jnp.zeros((TILE, dim), F32)
            sums_ref[0:1, :] += jnp.sum(xf * xf, axis=0, keepdims=True)
            sums_ref[1:2, :] += jnp.sum(branch * branch, axis=0, keepdims=True)

    wd = jnp.concatenate([wd0[...], wd1[...]], axis=0)
    both = jnp.concatenate([wg0[...], wg1[...], wu0[...], wu1[...]], axis=1)
    for i in range(steps):
        rows = slice(i * TILE, (i + 1) * TILE)
        gateup = nn(n2[rows, :], both)
        gate, up = gateup[:, :ft], gateup[:, ft:]
        dh = nt(dy_ref[rows, :], wd)
        sig = jax.nn.sigmoid(gate)
        silu = gate * sig
        hid = (silu * up).astype(BF)
        dg = (dh * up * (sig * (1.0 + gate * (1.0 - sig)))).astype(BF)
        du = (dh * silu).astype(BF)
        hid_all[rows, :] = hid
        pair = jnp.concatenate([dg, du], axis=1)
        pair_all[rows, :] = pair
        acc_out[rows, :] += nn(hid, wd)
        acc_dn[rows, :] += nt(pair, both)

    @pl.when(turn >= 2)
    def reuse():
        settle(turn - 2, slot)

    down = tn(hid_all[...], dy_ref[...]).astype(BF)
    grads = nn(n2t[...], pair_all[...]).astype(BF)
    for i in range(2):
        gbuf[slot, i] = grads[:, i * HD:(i + 1) * HD]
        ubuf[slot, i] = grads[:, ft + i * HD:ft + (i + 1) * HD]
        dbuf[slot, i] = down[:, i * half:(i + 1) * half]
    stay, leave = moves(turn, slot)
    for copy in stay + leave:
        copy.start()

    @pl.when(turn == tiles - 1)
    def last():
        for i in range(steps):
            rows = slice(i * TILE, (i + 1) * TILE)
            final = acc_out[rows, :]
            out_ref[rows, :] = final.astype(BF)
            sums_ref[2:3, :] += jnp.sum(final * final, axis=0, keepdims=True)
            middle = mid[rows, :]
            inv = lax.rsqrt(jnp.mean(middle * middle, axis=1, keepdims=True) + EPS)
            dnorm = acc_dn[rows, :]
            weighted = dnorm * gain
            inner = jnp.mean(weighted * middle, axis=1, keepdims=True)
            dgain_ref[...] += jnp.sum(dnorm * middle * inv, axis=0, keepdims=True)
            dmid = dy_ref[rows, :].astype(F32) + weighted * inv - middle * (inv * inv * inv) * inner
            low = dmid.astype(BF)
            dmid_ref[rows, :] = low
            dcomb = nt(low, wo_ref[...]).astype(BF)
            dcomb_v[0, rows, :] = dcomb[:, :half]
            dcomb_v[1, rows, :] = dcomb[:, half:]
        home = pl.ds(pl.multiple_of(core * rows_all, TILE), rows_all)
        stay_c = pltpu.make_async_copy(dcomb_v.at[core], dcomb_out.at[home, :], end_sem.at[0])
        leave_c = push(dcomb_v.at[other], dcomb_out.at[home, :], end_sem.at[1], end_sem.at[2])
        stay_c.start()
        leave_c.start()
        for i in range(dim // TILE):
            part = slice(i * TILE, (i + 1) * TILE)
            go = tn(comb_ref[:, part], dmid_ref[...]).astype(BF)
            go_v[0, part, :] = go[:, :half]
            go_v[1, part, :] = go[:, half:]
        stay_o = pltpu.make_async_copy(go_v.at[core], go_own, end_sem.at[3])
        leave_o = push(go_v.at[other], go_sib, end_sem.at[4], end_sem.at[5])
        stay_o.start()
        leave_o.start()
        settle(turn - 1, 1 - slot)
        settle(turn, slot)
        for i, sib in enumerate((gg_sib, gu_sib)):
            push(sib, sib, send_sem.at[i, 0], recv_sem.at[i]).wait_recv()
        for i in range(2):
            part = gd_sib.at[pl.ds(i * hidden_half, hidden_half), :]
            push(part, part, send_sem.at[2 + i, 0], recv_sem.at[2 + i]).wait_recv()
        stay_c.wait()
        stay_o.wait()
        leave_c.wait()
        leave_o.wait()


def ffn_block(comb, x, dy, w_out, w_gate, w_up, w_down, gain):
    rows, dim = x.shape
    hidden = w_gate.shape[1]
    tiles = hidden // (2 * HD)
    full = (rows, dim)
    half = dim // 2
    any_spec = pl.BlockSpec(memory_space=pl.ANY)
    front = pl.BlockSpec((dim, HD), lambda t: (0, t))
    rear = pl.BlockSpec((dim, HD), lambda t: (0, t + tiles))
    dma = pltpu.SemaphoreType.DMA
    return pl.pallas_call(
        functools.partial(ffn_kernel, tiles),
        grid=(tiles,),
        in_specs=[
            whole(full),
            whole(full),
            whole(full),
            whole((dim, dim)),
            front,
            rear,
            front,
            rear,
            pl.BlockSpec((HD, dim), lambda t: (t, 0)),
            pl.BlockSpec((HD, dim), lambda t: (t + tiles, 0)),
            whole((1, dim)),
        ],
        out_specs=[whole(full), whole(full), whole((1, dim)), whole((8, dim))] + [any_spec] * 9,
        out_shape=[
            jax.ShapeDtypeStruct(full, BF),
            jax.ShapeDtypeStruct(full, BF),
            jax.ShapeDtypeStruct((1, dim), F32),
            jax.ShapeDtypeStruct((8, dim), F32),
            jax.ShapeDtypeStruct((2 * rows, half), BF),
        ]
        + [jax.ShapeDtypeStruct((dim, half), BF)] * 2
        + [jax.ShapeDtypeStruct((dim, hidden // 2), BF)] * 4
        + [jax.ShapeDtypeStruct((hidden, half), BF)] * 2,
        scratch_shapes=[
            pltpu.VMEM(full, BF),
            pltpu.VMEM((dim, rows), BF),
            pltpu.VMEM(full, F32),
            pltpu.VMEM(full, F32),
            pltpu.VMEM(full, F32),
            pltpu.VMEM((rows, 2 * HD), BF),
            pltpu.VMEM((rows, 4 * HD), BF),
            pltpu.VMEM((2, rows, half), BF),
            pltpu.VMEM((2, dim, half), BF),
            pltpu.VMEM((2, 2, dim, HD), BF),
            pltpu.VMEM((2, 2, dim, HD), BF),
            pltpu.VMEM((2, 2, 2 * HD, half), BF),
            dma((4, 2)),
            dma((4, 2)),
            dma((4,)),
            dma((6,)),
        ],
        compiler_params=pltpu.CompilerParams(
            collective_id=5, has_side_effects=True, vmem_limit_bytes=VMEM_MAX),
        name="ffn_block",
    )(comb, x, dy, w_out, w_gate, w_gate, w_up, w_up, w_down, w_down, gain)


def ring_place(row, n):
    return jnp.where(lax.rem(row, 2) == 0, row // 2, n - 1 - row // 2)


def ring_row(place, n):
    return jnp.where(place < n // 2, 2 * place, 2 * (n - place) - 1)


def split_cols(width, flip):
    tiles = width // HD
    if tiles == 1:
        return ((0, width),)
    first = (tiles + (0 if flip else 1)) // 2 * HD
    return ((0, first), (first, width - first))


def mod(value, n):
    return lax.rem(value + n, n)


def neighbours(n):
    me = ring_place(lax.axis_index("row"), n)
    return me, ring_row(mod(me + 1, n), n), ring_row(mod(me - 1, n), n)


def greet(n, right, left, use_col, use_dp):
    barrier = pltpu.get_barrier_semaphore()
    count = 2
    for target in (right, left):
        pl.semaphore_signal(barrier, inc=1, device_id={"row": target}, device_id_type=MESH)
    if use_col:
        other = 1 - lax.axis_index("col")
        pl.semaphore_signal(barrier, inc=1, device_id={"col": other}, device_id_type=MESH)
        count += 1
    if use_dp:
        twin = 1 - lax.axis_index("dp")
        pl.semaphore_signal(barrier, inc=1, device_id={"dp": twin}, device_id_type=MESH)
        count += 1
    pl.semaphore_wait(barrier, count)


class Gather:
    def __init__(self, n, items, sems):
        self.n = n
        self.items = items
        self.send, self.recv, self.local, self.csend, self.crecv = sems
        self.me, self.right, self.left = neighbours(n)
        self.row = lax.axis_index("row")
        self.other = 1 - lax.axis_index("col")

    def ways(self, m):
        return range(len(split_cols(self.items[m][0].shape[1], m % 2)))

    def hop(self, m, d, s):
        block, whole_ref, base, share = self.items[m]
        place = mod(self.me - s, self.n) if d == 0 else mod(self.me + s, self.n)
        owner = ring_row(place, self.n)
        start, size = split_cols(block.shape[1], m % 2)[d]
        spot = whole_ref.at[owner, :, pl.ds(base + start, size)]
        return owner, start, size, spot

    def ring(self, m, d, s, first=False):
        block = self.items[m][0]
        owner, start, size, spot = self.hop(m, d, s)
        source = block.at[:, pl.ds(start, size)] if first else spot
        return pltpu.make_async_remote_copy(
            src_ref=source, dst_ref=spot, send_sem=self.send.at[m, d, s], recv_sem=self.recv.at[m, d, s],
            device_id={"row": self.right if d == 0 else self.left}, device_id_type=MESH)

    def across(self, m, source, spot):
        return pltpu.make_async_remote_copy(
            src_ref=source, dst_ref=spot, send_sem=self.csend.at[m], recv_sem=self.crecv.at[m],
            device_id={"col": self.other}, device_id_type=MESH)

    def keep(self, m):
        block, whole_ref, base, share = self.items[m]
        return pltpu.make_async_copy(
            block, whole_ref.at[self.row, :, pl.ds(base, block.shape[1])], self.local.at[m])

    def begin(self, ms):
        for m in ms:
            for d in self.ways(m):
                self.ring(m, d, 0, first=True).start()
        for m in ms:
            block, whole_ref, base, share = self.items[m]
            self.keep(m).start()
            if share:
                self.across(m, block, whole_ref.at[self.row, :, pl.ds(base, block.shape[1])]).start()

    def advance(self, m, s):
        for d in self.ways(m):
            self.ring(m, d, s).wait_recv()

            @pl.when(s < self.n - 2)
            def on():
                self.ring(m, d, s + 1).start()

            if self.items[m][3]:
                spot = self.hop(m, d, s + 1)[3]
                self.across(m, spot, spot).start()

    def finish(self, ms):
        for m in ms:
            block, whole_ref, base, share = self.items[m]
            self.keep(m).wait()
            if share:
                spot = whole_ref.at[:, :, pl.ds(base, block.shape[1])]
                theirs = whole_ref.at[:, :, pl.ds(self.other * block.shape[1], block.shape[1])]
                self.across(m, spot, theirs).wait_recv()
                self.across(m, spot, theirs).wait_send()

            def sent(s, carry):
                for d in self.ways(m):
                    self.ring(m, d, s).wait_send()
                return carry

            lax.fori_loop(0, self.n - 1, sent, 0)


def gather_sems(n, count):
    return [
        pltpu.SemaphoreType.DMA((count, 2, n - 1)),
        pltpu.SemaphoreType.DMA((count, 2, n - 1)),
        pltpu.SemaphoreType.DMA((count,)),
        pltpu.SemaphoreType.DMA((count,)),
        pltpu.SemaphoreType.DMA((count,)),
    ]


def gather_kernel(n, *refs):
    blocks = refs[:5]
    x_ref = refs[5]
    wide, small, pair = refs[6:9]
    sems = refs[9:14]
    xsems = refs[14]
    core = lax.axis_index("col")
    items = [(blocks[m], wide, m * blocks[m].shape[1], False) for m in range(4)]
    items.append((blocks[4], small, core * blocks[4].shape[1], True))
    g = Gather(n, items, sems)
    greet(n, g.right, g.left, True, False)
    g.begin(range(5))
    mine = pltpu.make_async_copy(x_ref, pair.at[core], xsems.at[0])
    mine.start()
    theirs = pltpu.make_async_remote_copy(
        src_ref=x_ref, dst_ref=pair.at[core], send_sem=xsems.at[1], recv_sem=xsems.at[2],
        device_id={"col": 1 - core}, device_id_type=MESH)
    theirs.start()

    def step(s, carry):
        for m in range(5):
            g.advance(m, s)
        return carry

    lax.fori_loop(0, n - 1, step, 0)
    g.finish(range(5))
    mine.wait()
    theirs.wait()


def gather_first(n, blocks, small, x):
    rows, width = blocks[0].shape
    any_spec = pl.BlockSpec(memory_space=pl.ANY)
    shapes = [(n, rows, 4 * width), (n, small.shape[0], 2 * small.shape[1]), (2,) + x.shape]
    return pl.pallas_call(
        functools.partial(gather_kernel, n),
        in_specs=[any_spec] * 6,
        out_specs=[any_spec] * 3,
        out_shape=[jax.ShapeDtypeStruct(shape, BF) for shape in shapes],
        scratch_shapes=gather_sems(n, 5) + [pltpu.SemaphoreType.DMA((3,))],
        compiler_params=pltpu.CompilerParams(collective_id=1, has_side_effects=True),
        name="gather_first",
    )(*blocks, small, x)


class Scatter:
    def __init__(self, n, items, sems):
        self.n = n
        self.items = items
        self.send, self.recv, self.local, self.sib, self.dsend, self.drecv = sems
        self.me, self.right, self.left = neighbours(n)
        self.twin = 1 - lax.axis_index("dp")

    def ways(self, m):
        return range(len(split_cols(self.items[m][2], m % 2)))

    def loads(self, m):
        ref, base, width, other, own, sib = self.items[m][:6]
        copies = [pltpu.make_async_copy(ref.at[:, :, pl.ds(base, width)], own, self.local.at[m])]
        if other is not None:
            copies.append(pltpu.make_async_copy(other, sib, self.sib.at[m]))
        return copies

    def begin(self, ms):
        for m in ms:
            for copy in self.loads(m):
                copy.start()

    def ready(self, m):
        for copy in self.loads(m):
            copy.wait()

    def part(self, m, d, s):
        place = mod(self.me - 1 - s, self.n) if d == 0 else mod(self.me + 1 + s, self.n)
        start, size = split_cols(self.items[m][2], m % 2)[d]
        return ring_row(mod(place, self.n), self.n), slice(start, start + size)

    def ring(self, m, d, s):
        own, ring = self.items[m][4], self.items[m][6]
        owner, cols = self.part(m, d, s)
        return pltpu.make_async_remote_copy(
            src_ref=own.at[owner, :, cols], dst_ref=ring.at[s, :, cols],
            send_sem=self.send.at[m, d, s], recv_sem=self.recv.at[m, d, s],
            device_id={"row": self.right if d == 0 else self.left}, device_id_type=MESH)

    def total(self, m, d, s, arrived):
        other, own, sib, ring = self.items[m][3:7]
        owner, cols = self.part(m, d, s)
        value = own[owner, :, cols].astype(F32)
        if other is not None:
            value = value + sib[owner, :, cols].astype(F32)
        if arrived:
            value = value + ring[s - 1, :, cols].astype(F32)
        return owner, cols, value.astype(own.dtype)

    def start(self, m):
        for d in self.ways(m):
            if self.items[m][3] is not None:
                owner, cols, value = self.total(m, d, 0, False)
                self.items[m][4][owner, :, cols] = value
            self.ring(m, d, 0).start()

    def advance(self, m, s):
        for d in self.ways(m):
            self.ring(m, d, s - 1).wait_recv()
            owner, cols, value = self.total(m, d, s, True)
            self.items[m][4][owner, :, cols] = value
            self.ring(m, d, s).start()

    def swap(self, m):
        low, twin = self.items[m][7:9]
        return pltpu.make_async_remote_copy(
            src_ref=low, dst_ref=twin, send_sem=self.dsend.at[m], recv_sem=self.drecv.at[m],
            device_id={"dp": self.twin}, device_id_type=MESH)

    def settle(self, m):
        for d in self.ways(m):
            self.ring(m, d, self.n - 2).wait_recv()
            owner, cols, value = self.total(m, d, self.n - 1, True)
            self.items[m][7][:, cols] = value
        self.swap(m).start()

    def finish(self, m):
        low, twin, out = self.items[m][7:10]
        self.swap(m).wait_recv()
        out[...] = low[...].astype(F32) + twin[...].astype(F32)
        self.swap(m).wait_send()

        def sent(s, carry):
            for d in self.ways(m):
                self.ring(m, d, s).wait_send()
            return carry

        lax.fori_loop(0, self.n - 1, sent, 0)


def scatter_sems(n, count):
    return [
        pltpu.SemaphoreType.DMA((count, 2, n - 1)),
        pltpu.SemaphoreType.DMA((count, 2, n - 1)),
    ] + [pltpu.SemaphoreType.DMA((count,))] * 4


def scatter_plan(arrays):
    scratch = []
    for array, width, share in arrays:
        n, rows, full = array.shape
        kind = array.dtype
        scratch.append(pltpu.VMEM((n, rows, width), kind))
        scratch.append(pltpu.VMEM((n, rows, width) if share else (1, 16, HD), kind))
        scratch.append(pltpu.VMEM((n - 1, rows, width), kind))
        scratch.append(pltpu.VMEM((rows, width), kind))
        scratch.append(pltpu.VMEM((rows, width), kind))
    return scratch


def scatter_kernel(n, count, *refs):
    wide, small = refs[:2]
    outs = refs[2:2 + count]
    scratch = refs[2 + count:2 + 6 * count]
    small_sib, small_sems = refs[2 + 6 * count:4 + 6 * count]
    sems = refs[4 + 6 * count:]
    core = lax.axis_index("col")
    items = []
    for m in range(count):
        width = outs[m].shape[1]
        ref, base, other = (wide, m * width, None) if m < 4 else (small, core * width, small_sib)
        items.append((ref, base, width, other) + tuple(scratch[5 * m:5 * m + 5]) + (outs[m],))
    g = Scatter(n, items, sems)
    greet(n, g.right, g.left, True, True)
    width = outs[4].shape[1]
    cross = pltpu.make_async_remote_copy(
        src_ref=small.at[:, :, pl.ds((1 - core) * width, width)], dst_ref=small_sib,
        send_sem=small_sems.at[0], recv_sem=small_sems.at[1],
        device_id={"col": 1 - core}, device_id_type=MESH)
    cross.start()
    order = range(4)
    g.begin(order)
    for m in order:
        g.ready(m)
        g.start(m)
    cross.wait()
    g.begin((4,))
    g.ready(4)
    g.start(4)

    def step(s, carry):
        for m in range(count):
            g.advance(m, s)
        return carry

    lax.fori_loop(1, n - 1, step, 0)
    for m in range(count):
        g.settle(m)
    for m in range(count):
        g.finish(m)


def scatter_last(n, wide, small):
    width = wide.shape[2] // 4
    arrays = [(wide, width, False)] * 4 + [(small, HD, True)]
    count = len(arrays)
    any_spec = pl.BlockSpec(memory_space=pl.ANY)
    return pl.pallas_call(
        functools.partial(scatter_kernel, n, count),
        in_specs=[any_spec] * 2,
        out_specs=[pl.BlockSpec(memory_space=pltpu.VMEM)] * count,
        out_shape=[jax.ShapeDtypeStruct((a.shape[1], w), F32) for a, w, share in arrays],
        scratch_shapes=scatter_plan(arrays)
        + [pltpu.VMEM((n, small.shape[1], HD), F32), pltpu.SemaphoreType.DMA((2,))]
        + scatter_sems(n, count),
        compiler_params=pltpu.CompilerParams(
            collective_id=2, has_side_effects=True, vmem_limit_bytes=VMEM_MAX),
        name="scatter_last",
    )(wide, small)


def local(
    tokens_in,
    grad_out,
    gain_attn,
    gain_ffn,
    w_query,
    w_key,
    w_value,
    w_gate,
    w_out,
    w_ffn_gate,
    w_ffn_up,
    w_ffn_down,
    persist_key,
    persist_value,
    mem_rate,
    mem_momentum,
    mem_forget,
    segment_ids,
    decay_index,
):
    n = lax.axis_size("row")
    core = lax.axis_index("col")
    local_tok, dim = tokens_in.shape
    heads = mem_rate.shape[1]
    width = heads * HD
    piece = gain_attn.shape[0]
    small = jnp.concatenate(
        [persist_key, persist_value, gain_attn[None, :], gain_ffn[None, :]], axis=0)
    small = jnp.pad(small, ((0, 48 - small.shape[0]), (0, HD - piece)))
    wide, small_all, pair = gather_first(n, (w_query, w_key, w_value, w_gate), small, tokens_in)
    wide = wide.reshape(dim, 4 * width)
    small_all = small_all.reshape(n, 48, 2, HD)[:, :, :, :piece].transpose(1, 0, 2, 3).reshape(48, dim)
    gain_a = small_all[2 * P_SIZE][None, :].astype(F32)
    gain_f = small_all[2 * P_SIZE + 1][None, :].astype(F32)
    own_small = lax.dynamic_slice_in_dim(small_all, core * width, width, 1)
    pad = ((0, HD - P_SIZE), (0, 0))
    pkey = jnp.pad(own_small[:P_SIZE], pad)
    pvalue = jnp.pad(own_small[P_SIZE:2 * P_SIZE], pad)

    inputs = pair.reshape(2 * local_tok, dim).astype(F32)
    inverse_a = lax.rsqrt(jnp.mean(inputs * inputs, axis=-1, keepdims=True) + EPS)
    normed = (inputs * inverse_a * gain_a).astype(BF)
    qkvg = nn(normed, wide).astype(BF)

    total = qkvg.shape[0]
    spans = total // CH
    span_ids = segment_ids.reshape(total // SEQ, SEQ // CH, CH)
    same = (span_ids[:, 1:, 0] == span_ids[:, :-1, CH - 1]).astype(F32)
    keep = jnp.concatenate([jnp.zeros((total // SEQ, 1), F32), same], axis=1).reshape(spans, 1)
    choose = (decay_index[:, None] == jnp.arange(mem_rate.shape[0])[None, :]).astype(F32)
    tables = jnp.concatenate([mem_rate, mem_momentum, 1.0 - mem_forget], axis=1)
    picked = jnp.dot(choose, tables, precision=HIGH)
    coef = jnp.stack(
        [jnp.broadcast_to(keep, (spans, heads))] + [picked[:, i * heads:(i + 1) * heads] for i in range(3)]
    ).reshape(4, spans * heads)
    segc, segr = segment_ids[:, None], segment_ids[None, :]

    later = (w_out, w_ffn_gate, w_ffn_up, w_ffn_down)
    lse, reads, m0, err, comb_tok, full_out, full_gate, full_up, full_down = mix_forward(
        n, qkvg, pkey, pvalue, segc, segr, coef, heads, later)
    full_out, full_gate, full_up = [a.reshape(dim, -1) for a in (full_out, full_gate, full_up)]
    full_down = full_down.reshape(-1, dim)
    result, dmid, dgain_f, sums, dcomb, *parts = ffn_block(
        comb_tok, tokens_in, grad_out, full_out, full_gate, full_up, full_down, gain_f)
    parts = [a.reshape(n, a.shape[0] // n, a.shape[1]) for a in parts]
    dqkvg, dpk, dpv, *grads_late = mix_backward(
        n, qkvg, dcomb, pkey, pvalue, segc, segr, coef, lse, reads, m0, err, heads,
        parts[0::2], parts[1::2])

    g_wide = tn(normed, dqkvg).astype(BF)
    back = nt(dqkvg, wide).astype(BF)
    mine = lax.dynamic_slice_in_dim(back, core * local_tok, local_tok, 0)
    theirs = lax.dynamic_slice_in_dim(back, (1 - core) * local_tok, local_tok, 0)
    theirs = lax.ppermute(theirs, "col", [(0, 1), (1, 0)])
    dnorm = mine.astype(F32) + theirs.astype(F32)
    xf = tokens_in.astype(F32)
    inv = lax.rsqrt(jnp.mean(xf * xf, axis=-1, keepdims=True) + EPS)
    weighted = dnorm * gain_a
    inner = jnp.mean(weighted * xf, axis=-1, keepdims=True)
    grad_in = (dmid.astype(F32) + weighted * inv - xf * (inv * inv * inv) * inner).astype(BF)
    dgain_a = jnp.sum(dnorm * xf * inv, axis=0)

    place = jnp.zeros((2 * P_SIZE, dim), F32)
    place = lax.dynamic_update_slice_in_dim(
        place, jnp.concatenate([dpk[:P_SIZE], dpv[:P_SIZE]], axis=0), core * width, 1)
    packed = jnp.concatenate([place, dgain_a[None, :], dgain_f], axis=0)
    packed = packed.reshape(2 * P_SIZE + 2, n, 2, piece).transpose(1, 0, 2, 3)
    packed = jnp.pad(packed, ((0, 0), (0, 0), (0, 0), (0, HD - piece)))
    stats = jnp.sum(sums.reshape(8, dim // HD, HD), axis=1)[:6]
    stats = jnp.broadcast_to(stats[None, :, None, :], (n, 6, 2, HD))
    packed = jnp.concatenate([packed, stats], axis=1).reshape(n, 2 * P_SIZE + 8, 2 * HD)
    *grads, part = scatter_last(n, g_wide.reshape(n, dim // n, 4 * width), packed)
    grads = grads + grads_late
    entry_count = local_tok * dim * lax.axis_size("dp") * n * lax.axis_size("col")
    rms_stats = jnp.sqrt(jnp.sum(part[2 * P_SIZE + 2:2 * P_SIZE + 5], axis=1) / entry_count)
    part = part[:, :piece]
    return (
        result,
        grad_in,
        grads[0],
        grads[1],
        grads[2],
        grads[3],
        grads[4],
        grads[5],
        grads[6],
        grads[7],
        part[2 * P_SIZE],
        part[2 * P_SIZE + 1],
        part[:P_SIZE],
        part[P_SIZE:2 * P_SIZE],
        rms_stats,
    )


def solution(mesh):
    tokens = P(("dp", "row", "col"), None)
    vector = P(("row", "col"))
    weight = P("row", "col")
    persist = P(None, ("row", "col"))
    table = P(None, "col")
    ids = P(("dp", "row"))
    return jax.shard_map(
        local,
        mesh=mesh,
        in_specs=(tokens, tokens, vector, vector) + (weight,) * 8 + (persist,) * 2 + (table,) * 3 + (ids,) * 2,
        out_specs=(tokens, tokens) + (weight,) * 8 + (vector,) * 2 + (persist,) * 2 + (P(),),
        check_vma=False,
    )
```

```python
import functools
import jax
import jax.numpy as jnp
from jax import lax
from jax.experimental import pallas as pl
from jax.experimental.pallas import tpu as pltpu
from jax.sharding import PartitionSpec as P

HD = 128
P_SIZE = 16
SEG = 1024
CH = 64
SEQ = 2048
TILE = 256
TPS = SEG // TILE
EPS = 1e-06
NEG = -1e30
SCALE = HD ** (-0.5)
LOG2E = 1.4426950408889634
VMEM_MAX = 60 * 1024 * 1024
F32 = jnp.float32
BF = jnp.bfloat16
HIGH = lax.Precision.HIGHEST
MESH = pl.DeviceIdType.MESH


def nn(a, b):
    return lax.dot_general(a, b, (((1,), (0,)), ((), ())), preferred_element_type=F32)


def nt(a, b):
    return lax.dot_general(a, b, (((1,), (1,)), ((), ())), preferred_element_type=F32)


def tn(a, b):
    return lax.dot_general(a, b, (((0,), (0,)), ((), ())), preferred_element_type=F32)


def token_bias(segc, segr, part):
    width = (part + 1) * TILE
    same = segc == segr[:, :width]
    qpos = lax.broadcasted_iota(jnp.int32, (TILE, width), 0) + part * TILE
    kpos = lax.broadcasted_iota(jnp.int32, (TILE, width), 1)
    return jnp.where(same & (kpos <= qpos), 0.0, NEG).astype(F32)


def mix_forward_tile(heads, part, tile, q_ref, k_ref, v_ref, g_ref, pk_ref, pv_ref, segc_ref,
                     segr_ref, coef_ref, comb_ref, lse_ref, reads_ref, m0_ref, err_ref, mem, mom):
    width = (part + 1) * TILE
    base = part * TILE
    bias = token_bias(segc_ref[...], segr_ref[...], part)
    pcol = lax.broadcasted_iota(jnp.int32, (TILE, HD), 1)
    lane = lax.broadcasted_iota(jnp.int32, (TILE, HD), 1)
    lse_all = jnp.zeros((TILE, HD), F32)
    blocks = TILE // CH
    for head in range(heads):
        cols = slice(head * HD, (head + 1) * HD)
        query = q_ref[:, cols]
        state = mem[head]
        speed = mom[head]
        reads = []
        for step in range(blocks):
            rows = slice(step * CH, (step + 1) * CH)
            at = tile * blocks + step
            keep = coef_ref[0, at * heads + head]
            rate = coef_ref[1, at * heads + head]
            moment = coef_ref[2, at * heads + head]
            stay = coef_ref[3, at * heads + head]
            start = state * keep
            low_start = start.astype(BF)
            m0_ref[step, head] = low_start
            rest = (start - low_start.astype(F32)).astype(BF)
            key = k_ref[base + step * CH:base + (step + 1) * CH, cols]
            value = v_ref[base + step * CH:base + (step + 1) * CH, cols]
            both = jnp.concatenate([query[rows], key], axis=0)
            got = nn(both, low_start) + nn(both, rest)
            reads.append(got[:CH] * SCALE)
            err = (got[CH:] * SCALE - value.astype(F32)).astype(BF)
            err_ref[rows, cols] = err
            slope = tn(key, err)
            speed = (moment * keep) * speed - (rate * SCALE) * slope
            state = stay * start + speed
        mem[head] = state
        mom[head] = speed
        read = jnp.concatenate(reads, axis=0)
        reads_ref[:, cols] = read.astype(BF)
        tok = nt(query, k_ref[:width, cols]) * (SCALE * LOG2E) + bias
        per = nt(query, pk_ref[:, cols]) * (SCALE * LOG2E)
        per = jnp.where(pcol < P_SIZE, per, NEG)
        top = jnp.maximum(jnp.max(tok, axis=1, keepdims=True), jnp.max(per, axis=1, keepdims=True))
        tok_e = jnp.exp2(tok - top)
        per_e = jnp.exp2(per - top)
        total = jnp.sum(tok_e, axis=1, keepdims=True) + jnp.sum(per_e, axis=1, keepdims=True)
        att = nn(tok_e.astype(BF), v_ref[:width, cols]) + nn(per_e.astype(BF), pv_ref[:, cols])
        att = att / total
        lse_all = jnp.where(lane == head, top + jnp.log2(total), lse_all)
        gate = jax.nn.sigmoid(g_ref[:, cols].astype(F32))
        comb_ref[:, cols] = (att + gate * read).astype(BF)
    lse_ref[...] = lse_all


def hop_bound(turn, tiles, hops):
    return (turn * hops) // tiles


def mix_forward_kernel(heads, n, tiles, q_ref, k_ref, v_ref, g_ref, pk_ref, pv_ref, segc_ref,
                       segr_ref, coef_ref, b0, b1, b2, b3, lse_ref, reads_ref, m0_ref, err_ref,
                       comb_out, w0, w1, w2, w3, mem, mom, comb_all, csems, *sems):
    tile = pl.program_id(0)
    core = lax.axis_index("col")
    blocks, wholes = (b0, b1, b2, b3), (w0, w1, w2, w3)
    planes = (None, 0, 1, None)
    items = [(blk, ref, core * blk.shape[1], True, plane)
             for blk, ref, plane in zip(blocks, wholes, planes)]
    g = Gather(n, items, sems)
    each = range(len(items))
    width = heads * HD
    per_core = tiles // 2

    def hops(low, high):
        def one(s, carry):
            for m in each:
                g.advance(m, s)
            return carry

        lax.fori_loop(low, high, one, 0)

    def place(device, index):
        return comb_out.at[pl.ds(index * TILE, TILE), pl.ds(device * width, width)]

    @pl.when(tile == 0)
    def clear():
        greet(n, g.right, g.left, True, True)
        g.begin(each)
        mem[...] = jnp.zeros_like(mem)
        mom[...] = jnp.zeros_like(mom)

    @pl.when(tile > 0)
    def pass_on():
        hops(hop_bound(tile - 1, tiles, n - 1), hop_bound(tile, tiles, n - 1))

    for part in range(TPS):
        @pl.when(lax.rem(tile, TPS) == part)
        def work():
            mix_forward_tile(heads, part, tile, q_ref, k_ref, v_ref, g_ref, pk_ref, pv_ref,
                             segc_ref, segr_ref, coef_ref, comb_all.at[tile], lse_ref, reads_ref,
                             m0_ref, err_ref, mem, mom)

    def stay(index):
        return pltpu.make_async_copy(
            comb_all.at[core * per_core + index], place(core, index), csems.at[0, index])

    def leave(index):
        return pltpu.make_async_remote_copy(
            src_ref=comb_all.at[(1 - core) * per_core + index], dst_ref=place(core, index),
            send_sem=csems.at[1, index], recv_sem=csems.at[2, index],
            device_id={"col": 1 - core}, device_id_type=MESH)

    index = lax.rem(tile, per_core)

    @pl.when(tile // per_core == core)
    def mine():
        stay(index).start()

    @pl.when(tile // per_core != core)
    def theirs():
        leave(index).start()

    @pl.when(tile == tiles - 1)
    def end():
        hops(hop_bound(tiles - 1, tiles, n - 1), n - 1)
        g.finish(each)
        for i in range(per_core):
            stay(i).wait()
            leave(i).wait()


def mix_forward(n, qkvg, pkey, pvalue, segc, segr, coef, heads, blocks):
    total = qkvg.shape[0]
    width = heads * HD
    tiles = total // TILE
    per = TILE // CH
    any_spec = pl.BlockSpec(memory_space=pl.ANY)
    return pl.pallas_call(
        functools.partial(mix_forward_kernel, heads, n, tiles),
        grid=(tiles,),
        in_specs=[
            pl.BlockSpec((TILE, width), lambda t: (t, 0)),
            pl.BlockSpec((SEG, width), lambda t: (t // TPS, 1)),
            pl.BlockSpec((SEG, width), lambda t: (t // TPS, 2)),
            pl.BlockSpec((TILE, width), lambda t: (t, 3)),
            pl.BlockSpec((HD, width), lambda t: (0, 0)),
            pl.BlockSpec((HD, width), lambda t: (0, 0)),
            pl.BlockSpec((TILE, 1), lambda t: (t, 0)),
            pl.BlockSpec((1, SEG), lambda t: (0, t // TPS)),
            pl.BlockSpec(memory_space=pltpu.SMEM),
        ] + [whole(b.shape) for b in blocks],
        out_specs=[
            pl.BlockSpec((TILE, HD), lambda t: (t, 0)),
            pl.BlockSpec((TILE, width), lambda t: (t, 0)),
            pl.BlockSpec((per, heads, HD, HD), lambda t: (t, 0, 0, 0)),
            pl.BlockSpec((TILE, width), lambda t: (t, 0)),
        ] + [any_spec] * 5,
        out_shape=[
            jax.ShapeDtypeStruct((total, HD), F32),
            jax.ShapeDtypeStruct((total, width), BF),
            jax.ShapeDtypeStruct((total // CH, heads, HD, HD), BF),
            jax.ShapeDtypeStruct((total, width), BF),
            jax.ShapeDtypeStruct((total // 2, 2 * width), BF),
        ] + [jax.ShapeDtypeStruct((n, b.shape[0], 2 * b.shape[1]), BF) for b in blocks],
        scratch_shapes=[
            pltpu.VMEM((heads, HD, HD), F32),
            pltpu.VMEM((heads, HD, HD), F32),
            pltpu.VMEM((tiles, TILE, width), BF),
            pltpu.SemaphoreType.DMA((3, tiles // 2)),
        ] + gather_sems(n, 4),
        compiler_params=pltpu.CompilerParams(
            collective_id=3, has_side_effects=True, vmem_limit_bytes=VMEM_MAX),
        name="mix_forward",
    )(qkvg, qkvg, qkvg, qkvg, pkey, pvalue, segc, segr, coef, *blocks)


def mix_backward_tile(heads, part, tile, q_ref, k_ref, v_ref, g_ref, dc_ref, pk_ref, pv_ref,
                      segc_ref, segr_ref, coef_ref, lse_ref, reads_ref, m0_ref, err_ref, dout_ref,
                      dmem, dmom, dk_acc, dv_acc, dpk_acc, dpv_acc):
    width = (part + 1) * TILE
    base = part * TILE
    wide = heads * HD
    bias = token_bias(segc_ref[...], segr_ref[...], part)
    pcol = lax.broadcasted_iota(jnp.int32, (TILE, HD), 1)
    blocks = TILE // CH
    lse_all = lse_ref[...]
    for head in range(heads):
        cols = slice(head * HD, (head + 1) * HD)
        query = q_ref[:, cols]
        up = dc_ref[:, cols]
        upf = up.astype(F32)
        gate = jax.nn.sigmoid(g_ref[:, cols].astype(F32))
        dread = (upf * gate).astype(BF)
        dgate = upf * reads_ref[:, cols].astype(F32) * gate * (1.0 - gate)
        dout_ref[:, 3 * wide + head * HD:3 * wide + (head + 1) * HD] = dgate.astype(BF)
        dstate = dmem[head]
        dspeed = dmom[head]
        dq_mem, dk_mem, dv_mem = [None] * blocks, [None] * blocks, [None] * blocks
        for step in reversed(range(blocks)):
            rows = slice(step * CH, (step + 1) * CH)
            at = tile * blocks + step
            keep = coef_ref[0, at * heads + head]
            rate = coef_ref[1, at * heads + head]
            moment = coef_ref[2, at * heads + head]
            stay = coef_ref[3, at * heads + head]
            key = k_ref[base + step * CH:base + (step + 1) * CH, cols]
            start = m0_ref[step, head]
            err = err_ref[rows, cols]
            dspeed = dspeed + dstate
            dslope = (dspeed * (-rate)).astype(BF)
            derr = nn(key, dslope) * SCALE
            derr_low = derr.astype(BF)
            top = jnp.concatenate([dread[rows], derr_low], axis=0)
            both = jnp.concatenate([query[rows], key], axis=0)
            dstart = stay * dstate + SCALE * tn(both, top)
            back = nt(top, start)
            dq_mem[step] = back[:CH]
            dk_mem[step] = back[CH:] + nt(err, dslope)
            dv_mem[step] = derr
            dspeed = (moment * keep) * dspeed
            dstate = keep * dstart
        dmem[head] = dstate
        dmom[head] = dspeed
        tok = nt(query, k_ref[:width, cols]) * (SCALE * LOG2E) + bias
        per = nt(query, pk_ref[:, cols]) * (SCALE * LOG2E)
        per = jnp.where(pcol < P_SIZE, per, NEG)
        lse = lse_all[:, head:head + 1]
        tok_p = jnp.exp2(tok - lse)
        per_p = jnp.exp2(per - lse)
        tok_dp = nt(up, v_ref[:width, cols])
        per_dp = nt(up, pv_ref[:, cols])
        inner = jnp.sum(tok_p * tok_dp, axis=1, keepdims=True) + jnp.sum(
            per_p * per_dp, axis=1, keepdims=True)
        tok_ds = (tok_p * (tok_dp - inner)).astype(BF)
        per_ds = (per_p * (per_dp - inner)).astype(BF)
        dquery = nn(tok_ds, k_ref[:width, cols]) + nn(per_ds, pk_ref[:, cols])
        dquery = (dquery + jnp.concatenate(dq_mem, axis=0)) * SCALE
        dout_ref[:, cols] = dquery.astype(BF)
        dkey = tn(tok_ds, query)
        dval = tn(tok_p.astype(BF), up)
        dpk_acc[:, cols] += tn(per_ds, query) * SCALE
        dpv_acc[:, cols] += tn(per_p.astype(BF), up)
        own = slice(base, base + TILE)
        if part == TPS - 1:
            dk_acc[:base, cols] = dkey[:base]
            dv_acc[:base, cols] = dval[:base]
            dk_own, dv_own = dkey[base:], dval[base:]
        else:
            if part:
                dk_acc[:base, cols] += dkey[:base]
                dv_acc[:base, cols] += dval[:base]
            dk_own = dk_acc[own, cols] + dkey[base:]
            dv_own = dv_acc[own, cols] + dval[base:]
        dout_ref[:, wide + head * HD:wide + (head + 1) * HD] = (
            (dk_own + jnp.concatenate(dk_mem, axis=0)) * SCALE).astype(BF)
        dout_ref[:, 2 * wide + head * HD:2 * wide + (head + 1) * HD] = (
            dv_own - jnp.concatenate(dv_mem, axis=0)).astype(BF)


def mix_backward_kernel(heads, n, tiles, q_ref, k_ref, v_ref, g_ref, dc_ref, pk_ref, pv_ref,
                        segc_ref, segr_ref, coef_ref, lse_ref, reads_ref, m0_ref, err_ref, *refs):
    own_refs, sib_refs = refs[:4], refs[4:8]
    dout_ref, dpk_ref, dpv_ref = refs[8:11]
    outs = refs[11:15]
    dmem, dmom, dk_acc, dv_acc = refs[15:19]
    scratch = refs[19:31]
    sems = refs[31:]
    turn = pl.program_id(0)
    tile = tiles - 1 - turn
    items = [
        (own_refs[m], 0, outs[m].shape[1], sib_refs[m]) + tuple(scratch[3 * m:3 * m + 3]) + (outs[m], None, None)
        for m in range(4)
    ]
    g = Scatter(n, items, sems)
    order = (1, 2, 3, 0)

    def hops(low, high):
        def one(s, carry):
            for m in order:
                g.advance(m, s)
            return carry

        lax.fori_loop(low, high, one, 0)

    @pl.when(turn == 0)
    def clear():
        greet(n, g.right, g.left, False, False)
        g.begin(order)
        dmem[...] = jnp.zeros_like(dmem)
        dmom[...] = jnp.zeros_like(dmom)
        dpk_ref[...] = jnp.zeros_like(dpk_ref)
        dpv_ref[...] = jnp.zeros_like(dpv_ref)
        for m in order:
            g.ready(m)
            g.start(m)

    @pl.when(turn > 0)
    def pass_on():
        hops(1 + hop_bound(turn - 1, tiles - 1, n - 2), 1 + hop_bound(turn, tiles - 1, n - 2))

    for part in range(TPS):
        @pl.when(lax.rem(tile, TPS) == part)
        def work():
            mix_backward_tile(heads, part, tile, q_ref, k_ref, v_ref, g_ref, dc_ref, pk_ref, pv_ref,
                              segc_ref, segr_ref, coef_ref, lse_ref, reads_ref, m0_ref, err_ref,
                              dout_ref, dmem, dmom, dk_acc, dv_acc, dpk_ref, dpv_ref)

    @pl.when(turn == tiles - 1)
    def end():
        for m in order:
            g.settle(m)
        for m in order:
            g.drain(m)


def mix_backward(n, qkvg, dcomb, pkey, pvalue, segc, segr, coef, lse, reads, m0, err, heads, owns, sibs):
    total = qkvg.shape[0]
    width = heads * HD
    tiles = total // TILE
    per = TILE // CH
    last = tiles - 1
    any_spec = pl.BlockSpec(memory_space=pl.ANY)
    arrays = [(a, a.shape[2], True) for a in owns]
    return pl.pallas_call(
        functools.partial(mix_backward_kernel, heads, n, tiles),
        grid=(tiles,),
        in_specs=[
            pl.BlockSpec((TILE, width), lambda t: (last - t, 0)),
            pl.BlockSpec((SEG, width), lambda t: ((last - t) // TPS, 1)),
            pl.BlockSpec((SEG, width), lambda t: ((last - t) // TPS, 2)),
            pl.BlockSpec((TILE, width), lambda t: (last - t, 3)),
            pl.BlockSpec((TILE, width), lambda t: (last - t, 0)),
            pl.BlockSpec((HD, width), lambda t: (0, 0)),
            pl.BlockSpec((HD, width), lambda t: (0, 0)),
            pl.BlockSpec((TILE, 1), lambda t: (last - t, 0)),
            pl.BlockSpec((1, SEG), lambda t: (0, (last - t) // TPS)),
            pl.BlockSpec(memory_space=pltpu.SMEM),
            pl.BlockSpec((TILE, HD), lambda t: (last - t, 0)),
            pl.BlockSpec((TILE, width), lambda t: (last - t, 0)),
            pl.BlockSpec((per, heads, HD, HD), lambda t: (last - t, 0, 0, 0)),
            pl.BlockSpec((TILE, width), lambda t: (last - t, 0)),
        ] + [any_spec] * 8,
        out_specs=[
            pl.BlockSpec((TILE, 4 * width), lambda t: (last - t, 0)),
            pl.BlockSpec((HD, width), lambda t: (0, 0)),
            pl.BlockSpec((HD, width), lambda t: (0, 0)),
        ] + [whole((a.shape[1], w)) for a, w, share in arrays],
        out_shape=[
            jax.ShapeDtypeStruct((total, 4 * width), BF),
            jax.ShapeDtypeStruct((HD, width), F32),
            jax.ShapeDtypeStruct((HD, width), F32),
        ] + [jax.ShapeDtypeStruct((a.shape[1], w), BF) for a, w, share in arrays],
        scratch_shapes=[
            pltpu.VMEM((heads, HD, HD), F32),
            pltpu.VMEM((heads, HD, HD), F32),
            pltpu.VMEM((SEG, width), F32),
            pltpu.VMEM((SEG, width), F32),
        ] + scatter_plan(arrays, False) + scatter_sems(n, 4),
        compiler_params=pltpu.CompilerParams(
            collective_id=4, has_side_effects=True, vmem_limit_bytes=VMEM_MAX),
        name="mix_backward",
    )(qkvg, qkvg, qkvg, qkvg, dcomb, pkey, pvalue, segc, segr, coef, lse, reads, m0, err, *owns, *sibs)


def whole(shape):
    return pl.BlockSpec(shape, lambda t: (0,) * len(shape), pipeline_mode=pl.Buffered(1))


def ffn_kernel(tiles, comb_ref, x_ref, dy_ref, wo_ref, wg0, wg1, wu0, wu1, wd0, wd1, gain_ref,
               out_ref, dmid_ref, dgain_ref, sums_ref, dcomb_out, go_own, go_sib, gg_own, gg_sib,
               gu_own, gu_sib, gd_own, gd_sib, n2, n2t, mid, acc_out, acc_dn, hid_all, pair_all,
               dcomb_v, go_v, gbuf, ubuf, dbuf, keep_sem, send_sem, recv_sem, end_sem):
    turn = pl.program_id(0)
    core = lax.axis_index("col")
    other = 1 - core
    rows_all, dim = x_ref.shape
    half = dim // 2
    steps = rows_all // TILE
    ft = 2 * HD
    gain = gain_ref[...]
    slot = lax.rem(turn, 2)
    hidden_half = gg_own.shape[1]

    def push(src, dst, sem, rsem):
        return pltpu.make_async_remote_copy(
            src_ref=src, dst_ref=dst, send_sem=sem, recv_sem=rsem,
            device_id={"col": other}, device_id_type=MESH)

    def moves(t, s):
        stay, leave = [], []
        for i, (buf, own, sib) in enumerate(((gbuf, gg_own, gg_sib), (ubuf, gu_own, gu_sib))):
            cols = pl.ds(pl.multiple_of(t * HD, HD), HD)
            stay.append(pltpu.make_async_copy(
                buf.at[s, core], own.at[:, cols], keep_sem.at[i, s]))
            leave.append(push(buf.at[s, other], sib.at[:, cols], send_sem.at[i, s], recv_sem.at[i]))
        for i in range(2):
            rows = pl.ds(pl.multiple_of(i * hidden_half + t * HD, HD), HD)
            stay.append(pltpu.make_async_copy(
                dbuf.at[s, core, pl.ds(i * HD, HD)], gd_own.at[rows, :], keep_sem.at[2 + i, s]))
            leave.append(push(dbuf.at[s, other, pl.ds(i * HD, HD)], gd_sib.at[rows, :],
                              send_sem.at[2 + i, s], recv_sem.at[2 + i]))
        return stay, leave

    def settle(t, s):
        stay, leave = moves(t, s)
        for copy in stay:
            copy.wait()
        for copy in leave:
            copy.wait_send()

    @pl.when(turn == 0)
    def first():
        barrier = pltpu.get_barrier_semaphore()
        pl.semaphore_signal(barrier, inc=1, device_id={"col": other}, device_id_type=MESH)
        pl.semaphore_wait(barrier, 1)
        sums_ref[...] = jnp.zeros_like(sums_ref)
        dgain_ref[...] = jnp.zeros_like(dgain_ref)
        for i in range(steps):
            rows = slice(i * TILE, (i + 1) * TILE)
            xf = x_ref[rows, :].astype(F32)
            branch = nn(comb_ref[rows, :], wo_ref[...])
            middle = xf + branch
            mid[rows, :] = middle
            acc_out[rows, :] = middle
            inv = lax.rsqrt(jnp.mean(middle * middle, axis=1, keepdims=True) + EPS)
            normed = (middle * inv * gain).astype(BF)
            n2[rows, :] = normed
            n2t[:, rows] = normed.T
            acc_dn[rows, :] = jnp.zeros((TILE, dim), F32)
            sums_ref[0:1, :] += jnp.sum(xf * xf, axis=0, keepdims=True)
            sums_ref[1:2, :] += jnp.sum(branch * branch, axis=0, keepdims=True)

    wd = jnp.concatenate([wd0[...], wd1[...]], axis=0)
    both = jnp.concatenate([wg0[...], wg1[...], wu0[...], wu1[...]], axis=1)
    for i in range(steps):
        rows = slice(i * TILE, (i + 1) * TILE)
        gateup = nn(n2[rows, :], both)
        gate, up = gateup[:, :ft], gateup[:, ft:]
        dh = nt(dy_ref[rows, :], wd)
        sig = jax.nn.sigmoid(gate)
        silu = gate * sig
        hid = (silu * up).astype(BF)
        dg = (dh * up * (sig * (1.0 + gate * (1.0 - sig)))).astype(BF)
        du = (dh * silu).astype(BF)
        hid_all[rows, :] = hid
        pair = jnp.concatenate([dg, du], axis=1)
        pair_all[rows, :] = pair
        acc_out[rows, :] += nn(hid, wd)
        acc_dn[rows, :] += nt(pair, both)

    @pl.when(turn >= 2)
    def reuse():
        settle(turn - 2, slot)

    down = tn(hid_all[...], dy_ref[...]).astype(BF)
    grads = nn(n2t[...], pair_all[...]).astype(BF)
    for i in range(2):
        gbuf[slot, i] = grads[:, i * HD:(i + 1) * HD]
        ubuf[slot, i] = grads[:, ft + i * HD:ft + (i + 1) * HD]
        dbuf[slot, i] = down[:, i * half:(i + 1) * half]
    stay, leave = moves(turn, slot)
    for copy in stay + leave:
        copy.start()

    @pl.when(turn == tiles - 1)
    def last():
        for i in range(steps):
            rows = slice(i * TILE, (i + 1) * TILE)
            final = acc_out[rows, :]
            out_ref[rows, :] = final.astype(BF)
            sums_ref[2:3, :] += jnp.sum(final * final, axis=0, keepdims=True)
            middle = mid[rows, :]
            inv = lax.rsqrt(jnp.mean(middle * middle, axis=1, keepdims=True) + EPS)
            dnorm = acc_dn[rows, :]
            weighted = dnorm * gain
            inner = jnp.mean(weighted * middle, axis=1, keepdims=True)
            dgain_ref[...] += jnp.sum(dnorm * middle * inv, axis=0, keepdims=True)
            dmid = dy_ref[rows, :].astype(F32) + weighted * inv - middle * (inv * inv * inv) * inner
            low = dmid.astype(BF)
            dmid_ref[rows, :] = low
            dcomb = nt(low, wo_ref[...]).astype(BF)
            dcomb_v[0, rows, :] = dcomb[:, :half]
            dcomb_v[1, rows, :] = dcomb[:, half:]
        home = pl.ds(pl.multiple_of(core * rows_all, TILE), rows_all)
        stay_c = pltpu.make_async_copy(dcomb_v.at[core], dcomb_out.at[home, :], end_sem.at[0])
        leave_c = push(dcomb_v.at[other], dcomb_out.at[home, :], end_sem.at[1], end_sem.at[2])
        stay_c.start()
        leave_c.start()
        for i in range(dim // TILE):
            part = slice(i * TILE, (i + 1) * TILE)
            go = tn(comb_ref[:, part], dmid_ref[...]).astype(BF)
            go_v[0, part, :] = go[:, :half]
            go_v[1, part, :] = go[:, half:]
        stay_o = pltpu.make_async_copy(go_v.at[core], go_own, end_sem.at[3])
        leave_o = push(go_v.at[other], go_sib, end_sem.at[4], end_sem.at[5])
        stay_o.start()
        leave_o.start()
        settle(turn - 1, 1 - slot)
        settle(turn, slot)
        for i, sib in enumerate((gg_sib, gu_sib)):
            push(sib, sib, send_sem.at[i, 0], recv_sem.at[i]).wait_recv()
        for i in range(2):
            part = gd_sib.at[pl.ds(i * hidden_half, hidden_half), :]
            push(part, part, send_sem.at[2 + i, 0], recv_sem.at[2 + i]).wait_recv()
        stay_c.wait()
        stay_o.wait()
        leave_c.wait()
        leave_o.wait()


def ffn_block(comb, x, dy, w_out, w_gate, w_up, w_down, gain):
    rows, dim = x.shape
    hidden = w_gate.shape[1]
    tiles = hidden // (2 * HD)
    full = (rows, dim)
    half = dim // 2
    any_spec = pl.BlockSpec(memory_space=pl.ANY)
    front = pl.BlockSpec((dim, HD), lambda t: (0, t))
    rear = pl.BlockSpec((dim, HD), lambda t: (0, t + tiles))
    dma = pltpu.SemaphoreType.DMA
    return pl.pallas_call(
        functools.partial(ffn_kernel, tiles),
        grid=(tiles,),
        in_specs=[
            whole(full),
            whole(full),
            whole(full),
            whole((dim, dim)),
            front,
            rear,
            front,
            rear,
            pl.BlockSpec((HD, dim), lambda t: (t, 0)),
            pl.BlockSpec((HD, dim), lambda t: (t + tiles, 0)),
            whole((1, dim)),
        ],
        out_specs=[whole(full), whole(full), whole((1, dim)), whole((8, dim))] + [any_spec] * 9,
        out_shape=[
            jax.ShapeDtypeStruct(full, BF),
            jax.ShapeDtypeStruct(full, BF),
            jax.ShapeDtypeStruct((1, dim), F32),
            jax.ShapeDtypeStruct((8, dim), F32),
            jax.ShapeDtypeStruct((2 * rows, half), BF),
        ]
        + [jax.ShapeDtypeStruct((dim, half), BF)] * 2
        + [jax.ShapeDtypeStruct((dim, hidden // 2), BF)] * 4
        + [jax.ShapeDtypeStruct((hidden, half), BF)] * 2,
        scratch_shapes=[
            pltpu.VMEM(full, BF),
            pltpu.VMEM((dim, rows), BF),
            pltpu.VMEM(full, F32),
            pltpu.VMEM(full, F32),
            pltpu.VMEM(full, F32),
            pltpu.VMEM((rows, 2 * HD), BF),
            pltpu.VMEM((rows, 4 * HD), BF),
            pltpu.VMEM((2, rows, half), BF),
            pltpu.VMEM((2, dim, half), BF),
            pltpu.VMEM((2, 2, dim, HD), BF),
            pltpu.VMEM((2, 2, dim, HD), BF),
            pltpu.VMEM((2, 2, 2 * HD, half), BF),
            dma((4, 2)),
            dma((4, 2)),
            dma((4,)),
            dma((6,)),
        ],
        compiler_params=pltpu.CompilerParams(
            collective_id=5, has_side_effects=True, vmem_limit_bytes=VMEM_MAX),
        name="ffn_block",
    )(comb, x, dy, w_out, w_gate, w_gate, w_up, w_up, w_down, w_down, gain)


def ring_place(row, n):
    return jnp.where(lax.rem(row, 2) == 0, row // 2, n - 1 - row // 2)


def ring_row(place, n):
    return jnp.where(place < n // 2, 2 * place, 2 * (n - place) - 1)


def split_cols(width, flip):
    tiles = width // HD
    if tiles == 1:
        return ((0, width),)
    first = (tiles + (0 if flip else 1)) // 2 * HD
    return ((0, first), (first, width - first))


def mod(value, n):
    return lax.rem(value + n, n)


def neighbours(n):
    me = ring_place(lax.axis_index("row"), n)
    return me, ring_row(mod(me + 1, n), n), ring_row(mod(me - 1, n), n)


def greet(n, right, left, use_col, use_dp):
    barrier = pltpu.get_barrier_semaphore()
    count = 2
    for target in (right, left):
        pl.semaphore_signal(barrier, inc=1, device_id={"row": target}, device_id_type=MESH)
    if use_col:
        other = 1 - lax.axis_index("col")
        pl.semaphore_signal(barrier, inc=1, device_id={"col": other}, device_id_type=MESH)
        count += 1
    if use_dp:
        twin = 1 - lax.axis_index("dp")
        pl.semaphore_signal(barrier, inc=1, device_id={"dp": twin}, device_id_type=MESH)
        count += 1
    pl.semaphore_wait(barrier, count)


class Gather:
    def __init__(self, n, items, sems):
        self.n = n
        self.items = items
        self.send, self.recv, self.local, self.csend, self.crecv, self.xsend = sems
        self.me, self.right, self.left = neighbours(n)
        self.row = lax.axis_index("row")
        self.other = 1 - lax.axis_index("col")
        self.plane = lax.axis_index("dp")

    def ways(self, m):
        return range(len(split_cols(self.items[m][0].shape[1], m % 2)))

    def hop(self, m, d, s):
        block, whole_ref, base = self.items[m][:3]
        place = mod(self.me - s, self.n) if d == 0 else mod(self.me + s, self.n)
        owner = ring_row(place, self.n)
        start, size = split_cols(block.shape[1], m % 2)[d]
        return start, size, whole_ref.at[owner, :, pl.ds(base + start, size)]

    def ring(self, m, d, s, first=False):
        start, size, spot = self.hop(m, d, s)
        source = self.items[m][0].at[:, pl.ds(start, size)] if first else spot
        return pltpu.make_async_remote_copy(
            src_ref=source, dst_ref=spot, send_sem=self.send.at[m, d, s], recv_sem=self.recv.at[m, d, s],
            device_id={"row": self.right if d == 0 else self.left}, device_id_type=MESH)

    def over(self, m, d, s):
        spot = self.hop(m, d, s + 1)[2]
        return pltpu.make_async_remote_copy(
            src_ref=spot, dst_ref=spot, send_sem=self.xsend.at[m, d, s], recv_sem=self.recv.at[m, d, s],
            device_id={"dp": 1 - self.plane}, device_id_type=MESH)

    def across(self, m, source, spot):
        return pltpu.make_async_remote_copy(
            src_ref=source, dst_ref=spot, send_sem=self.csend.at[m], recv_sem=self.crecv.at[m],
            device_id={"col": self.other}, device_id_type=MESH)

    def keep(self, m):
        block, whole_ref, base = self.items[m][:3]
        return pltpu.make_async_copy(
            block, whole_ref.at[self.row, :, pl.ds(base, block.shape[1])], self.local.at[m])

    def when(self, m, inside, action):
        plane = self.items[m][4]
        if plane is None:
            if inside:
                action()
        else:
            pl.when((self.plane == plane) if inside else (self.plane != plane))(action)

    def begin(self, ms):
        for m in ms:
            def launch(m=m):
                for d in self.ways(m):
                    self.ring(m, d, 0, first=True).start()

            self.when(m, True, launch)
        for m in ms:
            block, whole_ref, base, share = self.items[m][:4]
            self.keep(m).start()
            if share:
                self.across(m, block, whole_ref.at[self.row, :, pl.ds(base, block.shape[1])]).start()

    def hand(self, m, d, s):
        if self.items[m][3]:
            spot = self.hop(m, d, s + 1)[2]
            self.across(m, spot, spot).start()

    def arrive(self, m, s):
        for d in self.ways(m):
            self.over(m, d, s).wait_recv()
            self.hand(m, d, s)

    def advance(self, m, s):
        def inside():
            for d in self.ways(m):
                self.ring(m, d, s).wait_recv()

                @pl.when(s < self.n - 2)
                def on():
                    self.ring(m, d, s + 1).start()

                if self.items[m][4] is not None:
                    self.over(m, d, s).start()
                self.hand(m, d, s)

        def outside():
            @pl.when(s > 0)
            def late():
                self.arrive(m, s - 1)

        self.when(m, True, inside)
        self.when(m, False, outside)

    def finish(self, ms):
        for m in ms:
            self.when(m, False, functools.partial(self.arrive, m, self.n - 2))
        for m in ms:
            block, whole_ref, base, share, plane = self.items[m]
            self.keep(m).wait()
            if share:
                spot = whole_ref.at[:, :, pl.ds(base, block.shape[1])]
                theirs = whole_ref.at[:, :, pl.ds(self.other * block.shape[1], block.shape[1])]
                self.across(m, spot, theirs).wait_recv()
                self.across(m, spot, theirs).wait_send()

            def drain(m=m, plane=plane):
                def sent(s, carry):
                    for d in self.ways(m):
                        self.ring(m, d, s).wait_send()
                        if plane is not None:
                            self.over(m, d, s).wait_send()
                    return carry

                lax.fori_loop(0, self.n - 1, sent, 0)

            self.when(m, True, drain)


def gather_sems(n, count):
    dma = pltpu.SemaphoreType.DMA
    return [dma((count, 2, n - 1))] * 2 + [dma((count,))] * 3 + [dma((count, 2, n - 1))]


def gather_kernel(n, *refs):
    blocks = refs[:5]
    x_ref = refs[5]
    wide, small, pair = refs[6:9]
    sems = refs[9:15]
    xsems = refs[15]
    core = lax.axis_index("col")
    items = [(blocks[m], wide, m * blocks[m].shape[1], False, None) for m in range(4)]
    items.append((blocks[4], small, core * blocks[4].shape[1], True, None))
    g = Gather(n, items, sems)
    greet(n, g.right, g.left, True, False)
    g.begin(range(5))
    mine = pltpu.make_async_copy(x_ref, pair.at[core], xsems.at[0])
    mine.start()
    theirs = pltpu.make_async_remote_copy(
        src_ref=x_ref, dst_ref=pair.at[core], send_sem=xsems.at[1], recv_sem=xsems.at[2],
        device_id={"col": 1 - core}, device_id_type=MESH)
    theirs.start()

    def step(s, carry):
        for m in range(5):
            g.advance(m, s)
        return carry

    lax.fori_loop(0, n - 1, step, 0)
    g.finish(range(5))
    mine.wait()
    theirs.wait()


def gather_first(n, blocks, small, x):
    rows, width = blocks[0].shape
    any_spec = pl.BlockSpec(memory_space=pl.ANY)
    vmem_spec = pl.BlockSpec(memory_space=pltpu.VMEM)
    shapes = [(n, rows, 4 * width), (n, small.shape[0], 2 * small.shape[1]), (2,) + x.shape]
    return pl.pallas_call(
        functools.partial(gather_kernel, n),
        in_specs=[vmem_spec] * 6,
        out_specs=[any_spec] * 3,
        out_shape=[jax.ShapeDtypeStruct(shape, BF) for shape in shapes],
        scratch_shapes=gather_sems(n, 5) + [pltpu.SemaphoreType.DMA((3,))],
        compiler_params=pltpu.CompilerParams(
            collective_id=1, has_side_effects=True, vmem_limit_bytes=VMEM_MAX),
        name="gather_first",
    )(*blocks, small, x)


class Scatter:
    def __init__(self, n, items, sems):
        self.n = n
        self.items = items
        self.send, self.recv, self.local, self.sib, self.dsend, self.drecv = sems
        self.me, self.right, self.left = neighbours(n)
        self.twin = 1 - lax.axis_index("dp")

    def ways(self, m):
        return range(len(split_cols(self.items[m][2], m % 2)))

    def loads(self, m):
        ref, base, width, other, own, sib = self.items[m][:6]
        copies = [pltpu.make_async_copy(ref.at[:, :, pl.ds(base, width)], own, self.local.at[m])]
        if other is not None:
            copies.append(pltpu.make_async_copy(other, sib, self.sib.at[m]))
        return copies

    def begin(self, ms):
        for m in ms:
            for copy in self.loads(m):
                copy.start()

    def ready(self, m):
        for copy in self.loads(m):
            copy.wait()

    def part(self, m, d, s):
        place = mod(self.me - 1 - s, self.n) if d == 0 else mod(self.me + 1 + s, self.n)
        start, size = split_cols(self.items[m][2], m % 2)[d]
        return ring_row(mod(place, self.n), self.n), slice(start, start + size)

    def ring(self, m, d, s):
        own, ring = self.items[m][4], self.items[m][6]
        owner, cols = self.part(m, d, s)
        return pltpu.make_async_remote_copy(
            src_ref=own.at[owner, :, cols], dst_ref=ring.at[s, :, cols],
            send_sem=self.send.at[m, d, s], recv_sem=self.recv.at[m, d, s],
            device_id={"row": self.right if d == 0 else self.left}, device_id_type=MESH)

    def total(self, m, d, s, arrived):
        other, own, sib, ring = self.items[m][3:7]
        owner, cols = self.part(m, d, s)
        value = own[owner, :, cols].astype(F32)
        if other is not None:
            value = value + sib[owner, :, cols].astype(F32)
        if arrived:
            value = value + ring[s - 1, :, cols].astype(F32)
        return owner, cols, value.astype(own.dtype)

    def start(self, m):
        for d in self.ways(m):
            if self.items[m][3] is not None:
                owner, cols, value = self.total(m, d, 0, False)
                self.items[m][4][owner, :, cols] = value
            self.ring(m, d, 0).start()

    def advance(self, m, s):
        for d in self.ways(m):
            self.ring(m, d, s - 1).wait_recv()
            owner, cols, value = self.total(m, d, s, True)
            self.items[m][4][owner, :, cols] = value
            self.ring(m, d, s).start()

    def swap(self, m):
        low, twin = self.items[m][7:9]
        return pltpu.make_async_remote_copy(
            src_ref=low, dst_ref=twin, send_sem=self.dsend.at[m], recv_sem=self.drecv.at[m],
            device_id={"dp": self.twin}, device_id_type=MESH)

    def settle(self, m):
        for d in self.ways(m):
            self.ring(m, d, self.n - 2).wait_recv()
            owner, cols, value = self.total(m, d, self.n - 1, True)
            self.items[m][7][:, cols] = value
        if self.items[m][8] is not None:
            self.swap(m).start()

    def finish(self, m):
        low, twin, out = self.items[m][7:10]
        self.swap(m).wait_recv()
        out[...] = low[...].astype(F32) + twin[...].astype(F32)
        self.swap(m).wait_send()
        self.drain(m)

    def drain(self, m):
        def sent(s, carry):
            for d in self.ways(m):
                self.ring(m, d, s).wait_send()
            return carry

        lax.fori_loop(0, self.n - 1, sent, 0)


def scatter_sems(n, count):
    return [
        pltpu.SemaphoreType.DMA((count, 2, n - 1)),
        pltpu.SemaphoreType.DMA((count, 2, n - 1)),
    ] + [pltpu.SemaphoreType.DMA((count,))] * 4


def scatter_plan(arrays, swap=True):
    scratch = []
    for array, width, share in arrays:
        n, rows, full = array.shape
        kind = array.dtype
        scratch.append(pltpu.VMEM((n, rows, width), kind))
        scratch.append(pltpu.VMEM((n, rows, width) if share else (1, 16, HD), kind))
        scratch.append(pltpu.VMEM((n - 1, rows, width), kind))
        if swap:
            scratch.append(pltpu.VMEM((rows, width), kind))
            scratch.append(pltpu.VMEM((rows, width), kind))
    return scratch


def post_kernel(n, normed_ref, d_ref, w_ref, x_ref, dmid_ref, gain_ref, small, *refs):
    late = refs[:4]
    own_w = refs[4:8]
    gin_ref = refs[8]
    outs = refs[9:14]
    late_outs = refs[14:18]
    dgain_ref = refs[18]
    turned, back, leave, came, dg_own, dg_sib, small_sib = refs[19:26]
    late_in = refs[26:30]
    scratch = refs[30:55]
    side, late_send, late_recv = refs[55:58]
    sems = refs[58:]
    turn = pl.program_id(0)
    core = lax.axis_index("col")
    other = 1 - core
    rows_all, dim = x_ref.shape
    width = outs[0].shape[1]
    block = outs[0].shape[0]
    items = []
    for m in range(5):
        first, sib = (0, None) if m < 4 else (core * HD, small_sib)
        items.append((None if m < 4 else small, first, outs[m].shape[1], sib)
                     + tuple(scratch[5 * m:5 * m + 5]) + (outs[m],))
    g = Scatter(n, items, sems)
    steps = 2 * rows_all // TILE

    def push(src, dst, at):
        return pltpu.make_async_remote_copy(
            src_ref=src, dst_ref=dst, send_sem=side.at[2 * at], recv_sem=side.at[2 * at + 1],
            device_id={"col": other}, device_id_type=MESH)

    def late_swap(i):
        return pltpu.make_async_remote_copy(
            src_ref=late[i], dst_ref=late_in[i], send_sem=late_send.at[i], recv_sem=late_recv.at[i],
            device_id={"dp": g.twin}, device_id_type=MESH)

    cross = push(small.at[:, :, pl.ds(other * HD, HD)], small_sib, 0)
    swap_back = push(leave, came, 1)
    swap_gain = push(dg_own, dg_sib, 2)

    @pl.when(turn == 0)
    def first_turn():
        greet(n, g.right, g.left, True, True)
        cross.start()
        for i in range(4):
            late_swap(i).start()
        for i in range(steps):
            rows = slice(i * TILE, (i + 1) * TILE)
            turned[:, rows] = normed_ref[rows, :].T
            back[rows, :] = jnp.zeros((TILE, dim), F32)

    for m in range(4):
        @pl.when(turn == m)
        def this():
            grad = nn(turned[...], d_ref[...]).astype(BF)
            for q in range(n):
                items[m][4][q] = grad[q * block:(q + 1) * block]
            g.start(m)
            if m == 0:
                cross.wait()
                g.begin((4,))
                g.ready(4)
                g.start(4)
            for i in range(steps):
                rows = slice(i * TILE, (i + 1) * TILE)
                back[rows, :] += nt(d_ref[rows, :], w_ref[...])

    @pl.when(turn == 3)
    def rest():
        def step(low, high):
            def one(s, carry):
                for m in range(5):
                    g.advance(m, s)
                return carry

            lax.fori_loop(low, high, one, 0)

        hops = n - 2
        theirs = pl.multiple_of(other * rows_all, TILE)
        for i in range(rows_all // TILE):
            rows = slice(i * TILE, (i + 1) * TILE)
            leave[rows, :] = back[pl.ds(theirs + i * TILE, TILE), :].astype(BF)
        swap_back.start()
        step(1, 1 + hop_bound(1, 3, hops))
        swap_back.wait()
        mine = pl.multiple_of(core * rows_all, TILE)
        gain = gain_ref[...]
        for i in range(rows_all // TILE):
            rows = slice(i * TILE, (i + 1) * TILE)
            xf = x_ref[rows, :].astype(F32)
            inv = lax.rsqrt(jnp.mean(xf * xf, axis=1, keepdims=True) + EPS)
            weighted = (back[pl.ds(mine + i * TILE, TILE), :] + came[rows, :].astype(F32)) * gain
            inner = jnp.mean(weighted * xf, axis=1, keepdims=True)
            value = dmid_ref[rows, :].astype(F32) + weighted * inv - xf * (inv * inv * inv) * inner
            gin_ref[rows, :] = value.astype(BF)
            if i == 1:
                step(1 + hop_bound(1, 3, hops), 1 + hop_bound(2, 3, hops))
        step(1 + hop_bound(2, 3, hops), 1 + hops)
        for m in range(5):
            g.settle(m)
        for i in range(4):
            late_swap(i).wait()
            late_outs[i][...] = late[i][...].astype(F32) + late_in[i][...].astype(F32)
        total = jnp.zeros((block, 1), F32)
        for m in range(4):
            g.finish(m)
            total = total + jnp.sum(outs[m][...] * own_w[m][...].astype(F32), axis=1, keepdims=True)
        dg_own[...] = jnp.broadcast_to(total, (block, HD))
        swap_gain.start()
        g.finish(4)
        swap_gain.wait()
        dgain_ref[...] = dg_own[...] + dg_sib[...]


def post(n, normed, dqkvg, wide, x, dmid, gain, small, late, own_w):
    total, dim = normed.shape
    width = wide.shape[1] // 4
    rows = x.shape[0]
    block = dim // n
    arrays = [(jax.ShapeDtypeStruct((n, block, width), BF), width, False)] * 4 + [(small, HD, True)]
    any_spec = pl.BlockSpec(memory_space=pl.ANY)
    dma = pltpu.SemaphoreType.DMA
    outs = [((a.shape[1], w), F32) for a, w, share in arrays]
    late_outs = [(a.shape, F32) for a in late]
    shapes = [((rows, dim), BF)] + outs + late_outs + [((block, HD), F32)]
    return pl.pallas_call(
        functools.partial(post_kernel, n),
        grid=(4,),
        in_specs=[
            whole((total, dim)),
            pl.BlockSpec((total, width), lambda t: (0, t)),
            pl.BlockSpec((dim, width), lambda t: (0, t)),
            whole((rows, dim)),
            whole((rows, dim)),
            whole((1, dim)),
            any_spec,
        ] + [whole(a.shape) for a in late] + [whole(a.shape) for a in own_w],
        out_specs=[whole(shape) for shape, kind in shapes],
        out_shape=[jax.ShapeDtypeStruct(shape, kind) for shape, kind in shapes],
        scratch_shapes=[
            pltpu.VMEM((dim, total), BF),
            pltpu.VMEM((total, dim), F32),
            pltpu.VMEM((rows, dim), BF),
            pltpu.VMEM((rows, dim), BF),
            pltpu.VMEM((block, HD), F32),
            pltpu.VMEM((block, HD), F32),
            pltpu.VMEM((n, small.shape[1], HD), F32),
        ]
        + [pltpu.VMEM(a.shape, BF) for a in late]
        + scatter_plan(arrays)
        + [dma((6,)), dma((4,)), dma((4,))]
        + scatter_sems(n, 5),
        compiler_params=pltpu.CompilerParams(
            collective_id=2, has_side_effects=True, vmem_limit_bytes=VMEM_MAX),
        name="post",
    )(normed, dqkvg, wide, x, dmid, gain, small, *late, *own_w)


def local(
    tokens_in,
    grad_out,
    gain_attn,
    gain_ffn,
    w_query,
    w_key,
    w_value,
    w_gate,
    w_out,
    w_ffn_gate,
    w_ffn_up,
    w_ffn_down,
    persist_key,
    persist_value,
    mem_rate,
    mem_momentum,
    mem_forget,
    segment_ids,
    decay_index,
):
    n = lax.axis_size("row")
    core = lax.axis_index("col")
    local_tok, dim = tokens_in.shape
    heads = mem_rate.shape[1]
    width = heads * HD
    piece = gain_attn.shape[0]
    small = jnp.concatenate(
        [persist_key, persist_value, gain_attn[None, :], gain_ffn[None, :]], axis=0)
    small = jnp.pad(small, ((0, 48 - small.shape[0]), (0, HD - piece)))
    wide, small_all, pair = gather_first(n, (w_query, w_key, w_value, w_gate), small, tokens_in)
    wide = wide.reshape(dim, 4 * width)
    small_all = small_all.reshape(n, 48, 2, HD)[:, :, :, :piece].transpose(1, 0, 2, 3).reshape(48, dim)
    gain_a = small_all[2 * P_SIZE][None, :].astype(F32)
    gain_f = small_all[2 * P_SIZE + 1][None, :].astype(F32)
    own_small = lax.dynamic_slice_in_dim(small_all, core * width, width, 1)
    pad = ((0, HD - P_SIZE), (0, 0))
    pkey = jnp.pad(own_small[:P_SIZE], pad)
    pvalue = jnp.pad(own_small[P_SIZE:2 * P_SIZE], pad)

    inputs = pair.reshape(2 * local_tok, dim).astype(F32)
    inverse_a = lax.rsqrt(jnp.mean(inputs * inputs, axis=-1, keepdims=True) + EPS)
    normed = (inputs * inverse_a * gain_a).astype(BF)
    qkvg = nn(normed, wide).astype(BF)

    total = qkvg.shape[0]
    spans = total // CH
    span_ids = segment_ids.reshape(total // SEQ, SEQ // CH, CH)
    same = (span_ids[:, 1:, 0] == span_ids[:, :-1, CH - 1]).astype(F32)
    keep = jnp.concatenate([jnp.zeros((total // SEQ, 1), F32), same], axis=1).reshape(spans, 1)
    choose = (decay_index[:, None] == jnp.arange(mem_rate.shape[0])[None, :]).astype(F32)
    tables = jnp.concatenate([mem_rate, mem_momentum, 1.0 - mem_forget], axis=1)
    picked = jnp.dot(choose, tables, precision=HIGH)
    coef = jnp.stack(
        [jnp.broadcast_to(keep, (spans, heads))] + [picked[:, i * heads:(i + 1) * heads] for i in range(3)]
    ).reshape(4, spans * heads)
    segc, segr = segment_ids[:, None], segment_ids[None, :]

    later = (w_out, w_ffn_gate, w_ffn_up, w_ffn_down)
    lse, reads, m0, err, comb_tok, full_out, full_gate, full_up, full_down = mix_forward(
        n, qkvg, pkey, pvalue, segc, segr, coef, heads, later)
    full_out, full_gate, full_up = [a.reshape(dim, -1) for a in (full_out, full_gate, full_up)]
    full_down = full_down.reshape(-1, dim)
    result, dmid, dgain_f, sums, dcomb, *parts = ffn_block(
        comb_tok, tokens_in, grad_out, full_out, full_gate, full_up, full_down, gain_f)
    parts = [a.reshape(n, a.shape[0] // n, a.shape[1]) for a in parts]
    dqkvg, dpk, dpv, *grads_late = mix_backward(
        n, qkvg, dcomb, pkey, pvalue, segc, segr, coef, lse, reads, m0, err, heads,
        parts[0::2], parts[1::2])

    place = jnp.zeros((2 * P_SIZE, dim), F32)
    place = lax.dynamic_update_slice_in_dim(
        place, jnp.concatenate([dpk[:P_SIZE], dpv[:P_SIZE]], axis=0), core * width, 1)
    packed = jnp.concatenate([place, jnp.zeros((1, dim), F32), dgain_f], axis=0)
    packed = packed.reshape(2 * P_SIZE + 2, n, 2, piece).transpose(1, 0, 2, 3)
    packed = jnp.pad(packed, ((0, 0), (0, 0), (0, 0), (0, HD - piece)))
    stats = jnp.sum(sums.reshape(8, dim // HD, HD), axis=1)[:6]
    stats = jnp.broadcast_to(stats[None, :, None, :], (n, 6, 2, HD))
    packed = jnp.concatenate([packed, stats], axis=1).reshape(n, 2 * P_SIZE + 8, 2 * HD)
    grad_in, *rest = post(
        n, normed, dqkvg, wide, tokens_in, dmid, gain_a, packed, grads_late,
        (w_query, w_key, w_value, w_gate))
    grads, part, dgain_a = rest[:4] + rest[5:9], rest[4], rest[9]
    dgain_a = lax.dynamic_slice_in_dim(dgain_a[:, 0], core * piece, piece, 0) / gain_attn.astype(F32)
    entry_count = local_tok * dim * lax.axis_size("dp") * n * lax.axis_size("col")
    rms_stats = jnp.sqrt(jnp.sum(part[2 * P_SIZE + 2:2 * P_SIZE + 5], axis=1) / entry_count)
    part = part[:, :piece]
    return (
        result,
        grad_in,
        grads[0],
        grads[1],
        grads[2],
        grads[3],
        grads[4],
        grads[5],
        grads[6],
        grads[7],
        dgain_a,
        part[2 * P_SIZE + 1],
        part[:P_SIZE],
        part[P_SIZE:2 * P_SIZE],
        rms_stats,
    )


def solution(mesh):
    tokens = P(("dp", "row", "col"), None)
    vector = P(("row", "col"))
    weight = P("row", "col")
    persist = P(None, ("row", "col"))
    table = P(None, "col")
    ids = P(("dp", "row"))
    return jax.shard_map(
        local,
        mesh=mesh,
        in_specs=(tokens, tokens, vector, vector) + (weight,) * 8 + (persist,) * 2 + (table,) * 3 + (ids,) * 2,
        out_specs=(tokens, tokens) + (weight,) * 8 + (vector,) * 2 + (persist,) * 2 + (P(),),
        check_vma=False,
    )
```

```python
import functools
import jax
import jax.numpy as jnp
from jax import lax
from jax.experimental import pallas as pl
from jax.experimental.pallas import tpu as pltpu
from jax.sharding import PartitionSpec as P

HD = 128
P_SIZE = 16
SEG = 1024
CH = 64
SEQ = 2048
TILE = 256
TPS = SEG // TILE
EPS = 1e-06
NEG = -1e30
SCALE = HD ** (-0.5)
LOG2E = 1.4426950408889634
VMEM_MAX = 60 * 1024 * 1024
F32 = jnp.float32
BF = jnp.bfloat16
HIGH = lax.Precision.HIGHEST
MESH = pl.DeviceIdType.MESH


def nn(a, b):
    return lax.dot_general(a, b, (((1,), (0,)), ((), ())), preferred_element_type=F32)


def nt(a, b):
    return lax.dot_general(a, b, (((1,), (1,)), ((), ())), preferred_element_type=F32)


def tn(a, b):
    return lax.dot_general(a, b, (((0,), (0,)), ((), ())), preferred_element_type=F32)


def token_bias(segc, segr, part):
    width = (part + 1) * TILE
    same = segc == segr[:, :width]
    qpos = lax.broadcasted_iota(jnp.int32, (TILE, width), 0) + part * TILE
    kpos = lax.broadcasted_iota(jnp.int32, (TILE, width), 1)
    return jnp.where(same & (kpos <= qpos), 0.0, NEG).astype(F32)


def mix_forward_tile(heads, part, tile, q_ref, k_ref, v_ref, g_ref, pk_ref, pv_ref, segc_ref,
                     segr_ref, coef_ref, comb_ref, lse_ref, reads_ref, m0_ref, err_ref, mem, mom):
    width = (part + 1) * TILE
    base = part * TILE
    bias = token_bias(segc_ref[...], segr_ref[...], part)
    lane = lax.broadcasted_iota(jnp.int32, (TILE, HD), 1)
    lse_all = jnp.zeros((TILE, HD), F32)
    blocks = TILE // CH
    reads = [[None] * blocks for head in range(heads)]
    per_turn = -(-heads // blocks)
    attention = {}

    def memory(step, head):
        cols = slice(head * HD, (head + 1) * HD)
        rows = slice(step * CH, (step + 1) * CH)
        at = (tile * blocks + step) * heads + head
        keep = coef_ref[0, at]
        rate = coef_ref[1, at]
        moment = coef_ref[2, at]
        stay = coef_ref[3, at]
        start = mem[head] * keep
        low_start = start.astype(BF)
        m0_ref[step, head] = low_start
        key = k_ref[base + step * CH:base + (step + 1) * CH, cols]
        value = v_ref[base + step * CH:base + (step + 1) * CH, cols]
        both = jnp.concatenate([q_ref[rows, cols], key], axis=0)
        got = nn(both, low_start)
        reads[head][step] = got[:CH] * SCALE
        err = (got[CH:] * SCALE - value.astype(F32)).astype(BF)
        err_ref[rows, cols] = err
        speed = (moment * keep) * mom[head] - (rate * SCALE) * tn(key, err)
        mom[head] = speed
        mem[head] = stay * start + speed

    def attend(head):
        cols = slice(head * HD, (head + 1) * HD)
        query = q_ref[:, cols]
        tok = nt(query, k_ref[:width, cols]) * (SCALE * LOG2E) + bias
        per = nt(query, pk_ref[:, cols]) * (SCALE * LOG2E)
        per = jnp.where(lane < P_SIZE, per, NEG)
        top = jnp.maximum(jnp.max(tok, axis=1, keepdims=True), jnp.max(per, axis=1, keepdims=True))
        tok_e = jnp.exp2(tok - top)
        per_e = jnp.exp2(per - top)
        total = jnp.sum(tok_e, axis=1, keepdims=True) + jnp.sum(per_e, axis=1, keepdims=True)
        att = nn(tok_e.astype(BF), v_ref[:width, cols]) + nn(per_e.astype(BF), pv_ref[:, cols])
        attention[head] = att / total
        return top + jnp.log2(total)

    for step in range(blocks):
        for head in range(heads):
            memory(step, head)
        for head in range(step * per_turn, min(heads, (step + 1) * per_turn)):
            lse_all = jnp.where(lane == head, attend(head), lse_all)
    for head in range(heads):
        cols = slice(head * HD, (head + 1) * HD)
        read = jnp.concatenate(reads[head], axis=0)
        reads_ref[:, cols] = read.astype(BF)
        gate = jax.nn.sigmoid(g_ref[:, cols].astype(F32))
        comb_ref[:, cols] = (attention[head] + gate * read).astype(BF)
    lse_ref[...] = lse_all


def hop_bound(turn, tiles, hops):
    return (turn * hops) // tiles


def hop_early(turn, tiles, hops):
    return jnp.minimum(hops, (turn * hops + tiles - 1) // tiles)


def mix_forward_kernel(heads, n, tiles, q_ref, k_ref, v_ref, g_ref, pk_ref, pv_ref, segc_ref,
                       segr_ref, coef_ref, b0, b1, b2, b3, lse_ref, reads_ref, m0_ref, err_ref,
                       comb_out, w0, w1, w2, w3, mem, mom, comb_all, csems, *sems):
    tile = pl.program_id(0)
    core = lax.axis_index("col")
    blocks, wholes = (b0, b1, b2, b3), (w0, w1, w2, w3)
    planes = (None, 0, 1, None)
    items = [(blk, ref, core * blk.shape[1], True, plane)
             for blk, ref, plane in zip(blocks, wholes, planes)]
    g = Gather(n, items, sems)
    each = range(len(items))
    width = heads * HD
    per_core = tiles // 2

    def hops(low, high):
        def one(s, carry):
            for m in each:
                g.advance(m, s)
            return carry

        lax.fori_loop(low, high, one, 0)

    def place(device, index):
        return comb_out.at[pl.ds(index * TILE, TILE), pl.ds(device * width, width)]

    @pl.when(tile == 0)
    def clear():
        greet(n, g.right, g.left, True, True)
        g.begin(each)
        mem[...] = jnp.zeros_like(mem)
        mom[...] = jnp.zeros_like(mom)

    @pl.when(tile > 0)
    def pass_on():
        hops(hop_bound(tile - 1, tiles, n - 1), hop_bound(tile, tiles, n - 1))

    for part in range(TPS):
        @pl.when(lax.rem(tile, TPS) == part)
        def work():
            mix_forward_tile(heads, part, tile, q_ref, k_ref, v_ref, g_ref, pk_ref, pv_ref,
                             segc_ref, segr_ref, coef_ref, comb_all.at[tile], lse_ref, reads_ref,
                             m0_ref, err_ref, mem, mom)

    def stay(index):
        return pltpu.make_async_copy(
            comb_all.at[core * per_core + index], place(core, index), csems.at[0, index])

    def leave(index):
        return pltpu.make_async_remote_copy(
            src_ref=comb_all.at[(1 - core) * per_core + index], dst_ref=place(core, index),
            send_sem=csems.at[1, index], recv_sem=csems.at[2, index],
            device_id={"col": 1 - core}, device_id_type=MESH)

    index = lax.rem(tile, per_core)

    @pl.when(tile // per_core == core)
    def mine():
        stay(index).start()

    @pl.when(tile // per_core != core)
    def theirs():
        leave(index).start()

    @pl.when(tile == tiles - 1)
    def end():
        hops(hop_bound(tiles - 1, tiles, n - 1), n - 1)
        g.finish(each)
        for i in range(per_core):
            stay(i).wait()
            leave(i).wait()


def mix_forward(n, qkvg, pkey, pvalue, segc, segr, coef, heads, blocks):
    total = qkvg.shape[0]
    width = heads * HD
    tiles = total // TILE
    per = TILE // CH
    any_spec = pl.BlockSpec(memory_space=pl.ANY)
    return pl.pallas_call(
        functools.partial(mix_forward_kernel, heads, n, tiles),
        grid=(tiles,),
        in_specs=[
            pl.BlockSpec((TILE, width), lambda t: (t, 0)),
            pl.BlockSpec((SEG, width), lambda t: (t // TPS, 1)),
            pl.BlockSpec((SEG, width), lambda t: (t // TPS, 2)),
            pl.BlockSpec((TILE, width), lambda t: (t, 3)),
            pl.BlockSpec((HD, width), lambda t: (0, 0)),
            pl.BlockSpec((HD, width), lambda t: (0, 0)),
            pl.BlockSpec((TILE, 1), lambda t: (t, 0)),
            pl.BlockSpec((1, SEG), lambda t: (0, t // TPS)),
            pl.BlockSpec(memory_space=pltpu.SMEM),
        ] + [whole(b.shape) for b in blocks],
        out_specs=[
            pl.BlockSpec((TILE, HD), lambda t: (t, 0)),
            pl.BlockSpec((TILE, width), lambda t: (t, 0)),
            pl.BlockSpec((per, heads, HD, HD), lambda t: (t, 0, 0, 0)),
            pl.BlockSpec((TILE, width), lambda t: (t, 0)),
        ] + [any_spec] * 5,
        out_shape=[
            jax.ShapeDtypeStruct((total, HD), F32),
            jax.ShapeDtypeStruct((total, width), BF),
            jax.ShapeDtypeStruct((total // CH, heads, HD, HD), BF),
            jax.ShapeDtypeStruct((total, width), BF),
            jax.ShapeDtypeStruct((total // 2, 2 * width), BF),
        ] + [jax.ShapeDtypeStruct((n, b.shape[0], 2 * b.shape[1]), BF) for b in blocks],
        scratch_shapes=[
            pltpu.VMEM((heads, HD, HD), F32),
            pltpu.VMEM((heads, HD, HD), F32),
            pltpu.VMEM((tiles, TILE, width), BF),
            pltpu.SemaphoreType.DMA((3, tiles // 2)),
        ] + gather_sems(n, 4),
        compiler_params=pltpu.CompilerParams(
            collective_id=3, has_side_effects=True, vmem_limit_bytes=VMEM_MAX),
        name="mix_forward",
    )(qkvg, qkvg, qkvg, qkvg, pkey, pvalue, segc, segr, coef, *blocks)


def mix_backward_tile(heads, part, tile, q_ref, k_ref, v_ref, g_ref, dc_ref, pk_ref, pv_ref,
                      segc_ref, segr_ref, coef_ref, lse_ref, reads_ref, m0_ref, err_ref, dout_ref,
                      dmem, dmom, dk_acc, dv_acc, dpk_acc, dpv_acc):
    width = (part + 1) * TILE
    base = part * TILE
    wide = heads * HD
    bias = token_bias(segc_ref[...], segr_ref[...], part)
    pcol = lax.broadcasted_iota(jnp.int32, (TILE, HD), 1)
    blocks = TILE // CH
    lse_all = lse_ref[...]
    dreads = {}
    mem_q, mem_k, mem_v = {}, {}, {}

    def gates(head):
        cols = slice(head * HD, (head + 1) * HD)
        upf = dc_ref[:, cols].astype(F32)
        gate = jax.nn.sigmoid(g_ref[:, cols].astype(F32))
        dreads[head] = (upf * gate).astype(BF)
        dgate = upf * reads_ref[:, cols].astype(F32) * gate * (1.0 - gate)
        dout_ref[:, 3 * wide + head * HD:3 * wide + (head + 1) * HD] = dgate.astype(BF)

    def memory(step, head):
        cols = slice(head * HD, (head + 1) * HD)
        rows = slice(step * CH, (step + 1) * CH)
        at = (tile * blocks + step) * heads + head
        keep = coef_ref[0, at]
        rate = coef_ref[1, at]
        moment = coef_ref[2, at]
        stay = coef_ref[3, at]
        key = k_ref[base + step * CH:base + (step + 1) * CH, cols]
        start = m0_ref[step, head]
        err = err_ref[rows, cols]
        dstate = dmem[head]
        dspeed = dmom[head] + dstate
        dslope = (dspeed * (-rate)).astype(BF)
        derr = nn(key, dslope) * SCALE
        top = jnp.concatenate([dreads[head][rows], derr.astype(BF)], axis=0)
        both = jnp.concatenate([q_ref[rows, cols], key], axis=0)
        dmem[head] = keep * (stay * dstate + SCALE * tn(both, top))
        dmom[head] = (moment * keep) * dspeed
        back = nt(top, start)
        mem_q[head, step] = back[:CH]
        mem_k[head, step] = back[CH:] + nt(err, dslope)
        mem_v[head, step] = derr

    def attend(head):
        cols = slice(head * HD, (head + 1) * HD)
        query = q_ref[:, cols]
        up = dc_ref[:, cols]
        tok = nt(query, k_ref[:width, cols]) * (SCALE * LOG2E) + bias
        per = nt(query, pk_ref[:, cols]) * (SCALE * LOG2E)
        per = jnp.where(pcol < P_SIZE, per, NEG)
        lse = lse_all[:, head:head + 1]
        tok_p = jnp.exp2(tok - lse)
        per_p = jnp.exp2(per - lse)
        tok_dp = nt(up, v_ref[:width, cols])
        per_dp = nt(up, pv_ref[:, cols])
        inner = jnp.sum(tok_p * tok_dp, axis=1, keepdims=True) + jnp.sum(
            per_p * per_dp, axis=1, keepdims=True)
        tok_ds = (tok_p * (tok_dp - inner)).astype(BF)
        per_ds = (per_p * (per_dp - inner)).astype(BF)
        dquery = nn(tok_ds, k_ref[:width, cols]) + nn(per_ds, pk_ref[:, cols])
        dpk_acc[:, cols] += tn(per_ds, query) * SCALE
        dpv_acc[:, cols] += tn(per_p.astype(BF), up)
        dkey = tn(tok_ds, query)
        dval = tn(tok_p.astype(BF), up)
        own = slice(base, base + TILE)
        if part == TPS - 1:
            dk_acc[:, cols] = dkey
            dv_acc[:, cols] = dval
        else:
            dk_acc[:base + TILE, cols] += dkey
            dv_acc[:base + TILE, cols] += dval
        return dquery

    def finish(head, dquery):
        cols = slice(head * HD, (head + 1) * HD)
        own = slice(base, base + TILE)

        def rows_of(parts):
            return jnp.concatenate([parts[head, step] for step in range(blocks)], axis=0)

        dout_ref[:, cols] = ((dquery + rows_of(mem_q)) * SCALE).astype(BF)
        dout_ref[:, wide + head * HD:wide + (head + 1) * HD] = (
            (dk_acc[own, cols] + rows_of(mem_k)) * SCALE).astype(BF)
        dout_ref[:, 2 * wide + head * HD:2 * wide + (head + 1) * HD] = (
            dv_acc[own, cols] - rows_of(mem_v)).astype(BF)

    for head in range(heads):
        gates(head)
    per_turn = -(-heads // blocks)
    dqueries = {}
    for turn in range(blocks):
        for head in range(heads):
            memory(blocks - 1 - turn, head)
        for head in range(turn * per_turn, min(heads, (turn + 1) * per_turn)):
            dqueries[head] = attend(head)
    for head in range(heads):
        finish(head, dqueries[head])


def mix_backward_kernel(heads, n, tiles, q_ref, k_ref, v_ref, g_ref, dc_ref, pk_ref, pv_ref,
                        segc_ref, segr_ref, coef_ref, lse_ref, reads_ref, m0_ref, err_ref, *refs):
    own_refs, sib_refs = refs[:4], refs[4:8]
    dout_ref, dpk_ref, dpv_ref = refs[8:11]
    outs = refs[11:15]
    dmem, dmom, dk_acc, dv_acc = refs[15:19]
    scratch = refs[19:31]
    planes = (None, 0, 1, None)
    inbox = (None, refs[31], refs[32], None)
    sems = refs[33:]
    turn = pl.program_id(0)
    tile = tiles - 1 - turn
    items = [
        (own_refs[m], 0, outs[m].shape[1], sib_refs[m]) + tuple(scratch[3 * m:3 * m + 3]) + (outs[m], None, None, planes[m], inbox[m])
        for m in range(4)
    ]
    g = Scatter(n, items, sems)
    order = (1, 2, 3, 0)

    def hops(low, high):
        def one(s, carry):
            for m in order:
                g.advance(m, s)
            return carry

        lax.fori_loop(low, high, one, 0)

    @pl.when(turn == 0)
    def clear():
        greet(n, g.right, g.left, False, True)
        g.begin(order)
        dmem[...] = jnp.zeros_like(dmem)
        dmom[...] = jnp.zeros_like(dmom)
        dpk_ref[...] = jnp.zeros_like(dpk_ref)
        dpv_ref[...] = jnp.zeros_like(dpv_ref)
        for m in order:
            g.ready(m)
            g.start(m)

    @pl.when(turn > 0)
    def pass_on():
        hops(1 + hop_early(turn - 1, tiles - 2, n - 2), 1 + hop_early(turn, tiles - 2, n - 2))

    @pl.when(turn == tiles - 1)
    def settle():
        for m in order:
            g.settle(m)

    for part in range(TPS):
        @pl.when(lax.rem(tile, TPS) == part)
        def work():
            mix_backward_tile(heads, part, tile, q_ref, k_ref, v_ref, g_ref, dc_ref, pk_ref, pv_ref,
                              segc_ref, segr_ref, coef_ref, lse_ref, reads_ref, m0_ref, err_ref,
                              dout_ref, dmem, dmom, dk_acc, dv_acc, dpk_ref, dpv_ref)

    @pl.when(turn == tiles - 1)
    def end():
        for m in order:
            g.drain(m)


def mix_backward(n, qkvg, dcomb, pkey, pvalue, segc, segr, coef, lse, reads, m0, err, heads, owns, sibs):
    total = qkvg.shape[0]
    width = heads * HD
    tiles = total // TILE
    per = TILE // CH
    last = tiles - 1
    any_spec = pl.BlockSpec(memory_space=pl.ANY)
    arrays = [(a, a.shape[2], True) for a in owns]
    return pl.pallas_call(
        functools.partial(mix_backward_kernel, heads, n, tiles),
        grid=(tiles,),
        in_specs=[
            pl.BlockSpec((TILE, width), lambda t: (last - t, 0)),
            pl.BlockSpec((SEG, width), lambda t: ((last - t) // TPS, 1)),
            pl.BlockSpec((SEG, width), lambda t: ((last - t) // TPS, 2)),
            pl.BlockSpec((TILE, width), lambda t: (last - t, 3)),
            pl.BlockSpec((TILE, width), lambda t: (last - t, 0)),
            pl.BlockSpec((HD, width), lambda t: (0, 0)),
            pl.BlockSpec((HD, width), lambda t: (0, 0)),
            pl.BlockSpec((TILE, 1), lambda t: (last - t, 0)),
            pl.BlockSpec((1, SEG), lambda t: (0, (last - t) // TPS)),
            pl.BlockSpec(memory_space=pltpu.SMEM),
            pl.BlockSpec((TILE, HD), lambda t: (last - t, 0)),
            pl.BlockSpec((TILE, width), lambda t: (last - t, 0)),
            pl.BlockSpec((per, heads, HD, HD), lambda t: (last - t, 0, 0, 0)),
            pl.BlockSpec((TILE, width), lambda t: (last - t, 0)),
        ] + [any_spec] * 8,
        out_specs=[
            pl.BlockSpec((TILE, 4 * width), lambda t: (last - t, 0)),
            pl.BlockSpec((HD, width), lambda t: (0, 0)),
            pl.BlockSpec((HD, width), lambda t: (0, 0)),
        ] + [whole((a.shape[1], w)) for a, w, share in arrays],
        out_shape=[
            jax.ShapeDtypeStruct((total, 4 * width), BF),
            jax.ShapeDtypeStruct((HD, width), F32),
            jax.ShapeDtypeStruct((HD, width), F32),
        ] + [jax.ShapeDtypeStruct((a.shape[1], w), BF) for a, w, share in arrays],
        scratch_shapes=[
            pltpu.VMEM((heads, HD, HD), F32),
            pltpu.VMEM((heads, HD, HD), F32),
            pltpu.VMEM((SEG, width), F32),
            pltpu.VMEM((SEG, width), F32),
        ] + scatter_plan(arrays, False) + [pltpu.VMEM(a.shape, BF) for a in owns[1:3]] + scatter_sems(n, 4, True),
        compiler_params=pltpu.CompilerParams(
            collective_id=4, has_side_effects=True, vmem_limit_bytes=VMEM_MAX),
        name="mix_backward",
    )(qkvg, qkvg, qkvg, qkvg, dcomb, pkey, pvalue, segc, segr, coef, lse, reads, m0, err, *owns, *sibs)


def whole(shape):
    return pl.BlockSpec(shape, lambda t: (0,) * len(shape), pipeline_mode=pl.Buffered(1))


def ffn_kernel(tiles, comb_ref, x_ref, dy_ref, wo_ref, wg0, wg1, wu0, wu1, wd0, wd1, gain_ref,
               out_ref, dmid_ref, dgain_ref, sums_ref, dcomb_out, go_own, go_sib, gg_own, gg_sib,
               gu_own, gu_sib, gd_own, gd_sib, n2, n2t, mid, acc_out, acc_dn, hid_all, pair_all,
               dcomb_v, go_v, gbuf, ubuf, dbuf, keep_sem, send_sem, recv_sem, end_sem):
    turn = pl.program_id(0)
    core = lax.axis_index("col")
    other = 1 - core
    rows_all, dim = x_ref.shape
    half = dim // 2
    steps = rows_all // TILE
    ft = 2 * HD
    gain = gain_ref[...]
    slot = lax.rem(turn, 2)
    hidden_half = gg_own.shape[1]

    def push(src, dst, sem, rsem):
        return pltpu.make_async_remote_copy(
            src_ref=src, dst_ref=dst, send_sem=sem, recv_sem=rsem,
            device_id={"col": other}, device_id_type=MESH)

    def moves(t, s):
        stay, leave = [], []
        for i, (buf, own, sib) in enumerate(((gbuf, gg_own, gg_sib), (ubuf, gu_own, gu_sib))):
            cols = pl.ds(pl.multiple_of(t * HD, HD), HD)
            stay.append(pltpu.make_async_copy(
                buf.at[s, core], own.at[:, cols], keep_sem.at[i, s]))
            leave.append(push(buf.at[s, other], sib.at[:, cols], send_sem.at[i, s], recv_sem.at[i]))
        for i in range(2):
            rows = pl.ds(pl.multiple_of(i * hidden_half + t * HD, HD), HD)
            stay.append(pltpu.make_async_copy(
                dbuf.at[s, core, pl.ds(i * HD, HD)], gd_own.at[rows, :], keep_sem.at[2 + i, s]))
            leave.append(push(dbuf.at[s, other, pl.ds(i * HD, HD)], gd_sib.at[rows, :],
                              send_sem.at[2 + i, s], recv_sem.at[2 + i]))
        return stay, leave

    def settle(t, s):
        stay, leave = moves(t, s)
        for copy in stay:
            copy.wait()
        for copy in leave:
            copy.wait_send()

    @pl.when(turn == 0)
    def first():
        barrier = pltpu.get_barrier_semaphore()
        pl.semaphore_signal(barrier, inc=1, device_id={"col": other}, device_id_type=MESH)
        pl.semaphore_wait(barrier, 1)
        sums_ref[...] = jnp.zeros_like(sums_ref)
        dgain_ref[...] = jnp.zeros_like(dgain_ref)
        for i in range(steps):
            rows = slice(i * TILE, (i + 1) * TILE)
            xf = x_ref[rows, :].astype(F32)
            branch = nn(comb_ref[rows, :], wo_ref[...])
            middle = xf + branch
            mid[rows, :] = middle
            acc_out[rows, :] = middle
            inv = lax.rsqrt(jnp.mean(middle * middle, axis=1, keepdims=True) + EPS)
            normed = (middle * inv * gain).astype(BF)
            n2[rows, :] = normed
            n2t[:, rows] = normed.T
            acc_dn[rows, :] = jnp.zeros((TILE, dim), F32)
            sums_ref[0:1, :] += jnp.sum(xf * xf, axis=0, keepdims=True)
            sums_ref[1:2, :] += jnp.sum(branch * branch, axis=0, keepdims=True)

    wd = jnp.concatenate([wd0[...], wd1[...]], axis=0)
    both = jnp.concatenate([wg0[...], wg1[...], wu0[...], wu1[...]], axis=1)
    for i in range(steps):
        rows = slice(i * TILE, (i + 1) * TILE)
        gateup = nn(n2[rows, :], both)
        gate, up = gateup[:, :ft], gateup[:, ft:]
        dh = nt(dy_ref[rows, :], wd)
        sig = jax.nn.sigmoid(gate)
        silu = gate * sig
        hid = (silu * up).astype(BF)
        dg = (dh * up * (sig * (1.0 + gate * (1.0 - sig)))).astype(BF)
        du = (dh * silu).astype(BF)
        hid_all[rows, :] = hid
        pair = jnp.concatenate([dg, du], axis=1)
        pair_all[rows, :] = pair
        acc_out[rows, :] += nn(hid, wd)
        acc_dn[rows, :] += nt(pair, both)

    @pl.when(turn >= 2)
    def reuse():
        settle(turn - 2, slot)

    down = tn(hid_all[...], dy_ref[...]).astype(BF)
    grads = nn(n2t[...], pair_all[...]).astype(BF)
    for i in range(2):
        gbuf[slot, i] = grads[:, i * HD:(i + 1) * HD]
        ubuf[slot, i] = grads[:, ft + i * HD:ft + (i + 1) * HD]
        dbuf[slot, i] = down[:, i * half:(i + 1) * half]
    stay, leave = moves(turn, slot)
    for copy in stay + leave:
        copy.start()

    @pl.when(turn == tiles - 1)
    def last():
        for i in range(steps):
            rows = slice(i * TILE, (i + 1) * TILE)
            final = acc_out[rows, :]
            out_ref[rows, :] = final.astype(BF)
            sums_ref[2:3, :] += jnp.sum(final * final, axis=0, keepdims=True)
            middle = mid[rows, :]
            inv = lax.rsqrt(jnp.mean(middle * middle, axis=1, keepdims=True) + EPS)
            dnorm = acc_dn[rows, :]
            weighted = dnorm * gain
            inner = jnp.mean(weighted * middle, axis=1, keepdims=True)
            dgain_ref[...] += jnp.sum(dnorm * middle * inv, axis=0, keepdims=True)
            dmid = dy_ref[rows, :].astype(F32) + weighted * inv - middle * (inv * inv * inv) * inner
            low = dmid.astype(BF)
            dmid_ref[rows, :] = low
            dcomb = nt(low, wo_ref[...]).astype(BF)
            dcomb_v[0, rows, :] = dcomb[:, :half]
            dcomb_v[1, rows, :] = dcomb[:, half:]
        home = pl.ds(pl.multiple_of(core * rows_all, TILE), rows_all)
        stay_c = pltpu.make_async_copy(dcomb_v.at[core], dcomb_out.at[home, :], end_sem.at[0])
        leave_c = push(dcomb_v.at[other], dcomb_out.at[home, :], end_sem.at[1], end_sem.at[2])
        stay_c.start()
        leave_c.start()
        for i in range(dim // TILE):
            part = slice(i * TILE, (i + 1) * TILE)
            go = tn(comb_ref[:, part], dmid_ref[...]).astype(BF)
            go_v[0, part, :] = go[:, :half]
            go_v[1, part, :] = go[:, half:]
        stay_o = pltpu.make_async_copy(go_v.at[core], go_own, end_sem.at[3])
        leave_o = push(go_v.at[other], go_sib, end_sem.at[4], end_sem.at[5])
        stay_o.start()
        leave_o.start()
        settle(turn - 1, 1 - slot)
        settle(turn, slot)
        for i, sib in enumerate((gg_sib, gu_sib)):
            push(sib, sib, send_sem.at[i, 0], recv_sem.at[i]).wait_recv()
        for i in range(2):
            part = gd_sib.at[pl.ds(i * hidden_half, hidden_half), :]
            push(part, part, send_sem.at[2 + i, 0], recv_sem.at[2 + i]).wait_recv()
        stay_c.wait()
        stay_o.wait()
        leave_c.wait()
        leave_o.wait()


def ffn_block(comb, x, dy, w_out, w_gate, w_up, w_down, gain):
    rows, dim = x.shape
    hidden = w_gate.shape[1]
    tiles = hidden // (2 * HD)
    full = (rows, dim)
    half = dim // 2
    any_spec = pl.BlockSpec(memory_space=pl.ANY)
    front = pl.BlockSpec((dim, HD), lambda t: (0, t))
    rear = pl.BlockSpec((dim, HD), lambda t: (0, t + tiles))
    dma = pltpu.SemaphoreType.DMA
    return pl.pallas_call(
        functools.partial(ffn_kernel, tiles),
        grid=(tiles,),
        in_specs=[
            whole(full),
            whole(full),
            whole(full),
            whole((dim, dim)),
            front,
            rear,
            front,
            rear,
            pl.BlockSpec((HD, dim), lambda t: (t, 0)),
            pl.BlockSpec((HD, dim), lambda t: (t + tiles, 0)),
            whole((1, dim)),
        ],
        out_specs=[whole(full), whole(full), whole((1, dim)), whole((8, dim))] + [any_spec] * 9,
        out_shape=[
            jax.ShapeDtypeStruct(full, BF),
            jax.ShapeDtypeStruct(full, BF),
            jax.ShapeDtypeStruct((1, dim), F32),
            jax.ShapeDtypeStruct((8, dim), F32),
            jax.ShapeDtypeStruct((2 * rows, half), BF),
        ]
        + [jax.ShapeDtypeStruct((dim, half), BF)] * 2
        + [jax.ShapeDtypeStruct((dim, hidden // 2), BF)] * 4
        + [jax.ShapeDtypeStruct((hidden, half), BF)] * 2,
        scratch_shapes=[
            pltpu.VMEM(full, BF),
            pltpu.VMEM((dim, rows), BF),
            pltpu.VMEM(full, F32),
            pltpu.VMEM(full, F32),
            pltpu.VMEM(full, F32),
            pltpu.VMEM((rows, 2 * HD), BF),
            pltpu.VMEM((rows, 4 * HD), BF),
            pltpu.VMEM((2, rows, half), BF),
            pltpu.VMEM((2, dim, half), BF),
            pltpu.VMEM((2, 2, dim, HD), BF),
            pltpu.VMEM((2, 2, dim, HD), BF),
            pltpu.VMEM((2, 2, 2 * HD, half), BF),
            dma((4, 2)),
            dma((4, 2)),
            dma((4,)),
            dma((6,)),
        ],
        compiler_params=pltpu.CompilerParams(
            collective_id=5, has_side_effects=True, vmem_limit_bytes=VMEM_MAX),
        name="ffn_block",
    )(comb, x, dy, w_out, w_gate, w_gate, w_up, w_up, w_down, w_down, gain)


def ring_place(row, n):
    return jnp.where(lax.rem(row, 2) == 0, row // 2, n - 1 - row // 2)


def ring_row(place, n):
    return jnp.where(place < n // 2, 2 * place, 2 * (n - place) - 1)


def split_cols(width, flip):
    tiles = width // HD
    if tiles == 1:
        return ((0, width),)
    first = (tiles + (0 if flip else 1)) // 2 * HD
    return ((0, first), (first, width - first))


def mod(value, n):
    return lax.rem(value + n, n)


def neighbours(n):
    me = ring_place(lax.axis_index("row"), n)
    return me, ring_row(mod(me + 1, n), n), ring_row(mod(me - 1, n), n)


def greet(n, right, left, use_col, use_dp):
    barrier = pltpu.get_barrier_semaphore()
    count = 2
    for target in (right, left):
        pl.semaphore_signal(barrier, inc=1, device_id={"row": target}, device_id_type=MESH)
    if use_col:
        other = 1 - lax.axis_index("col")
        pl.semaphore_signal(barrier, inc=1, device_id={"col": other}, device_id_type=MESH)
        count += 1
    if use_dp:
        twin = 1 - lax.axis_index("dp")
        pl.semaphore_signal(barrier, inc=1, device_id={"dp": twin}, device_id_type=MESH)
        count += 1
    pl.semaphore_wait(barrier, count)


class Gather:
    def __init__(self, n, items, sems):
        self.n = n
        self.items = items
        self.send, self.recv, self.local, self.csend, self.crecv, self.xsend = sems
        self.me, self.right, self.left = neighbours(n)
        self.row = lax.axis_index("row")
        self.other = 1 - lax.axis_index("col")
        self.plane = lax.axis_index("dp")

    def ways(self, m):
        return range(len(split_cols(self.items[m][0].shape[1], m % 2)))

    def hop(self, m, d, s):
        block, whole_ref, base = self.items[m][:3]
        place = mod(self.me - s, self.n) if d == 0 else mod(self.me + s, self.n)
        owner = ring_row(place, self.n)
        start, size = split_cols(block.shape[1], m % 2)[d]
        return start, size, whole_ref.at[owner, :, pl.ds(base + start, size)]

    def ring(self, m, d, s, first=False):
        start, size, spot = self.hop(m, d, s)
        source = self.items[m][0].at[:, pl.ds(start, size)] if first else spot
        return pltpu.make_async_remote_copy(
            src_ref=source, dst_ref=spot, send_sem=self.send.at[m, d, s], recv_sem=self.recv.at[m, d, s],
            device_id={"row": self.right if d == 0 else self.left}, device_id_type=MESH)

    def over(self, m, d, s):
        spot = self.hop(m, d, s + 1)[2]
        return pltpu.make_async_remote_copy(
            src_ref=spot, dst_ref=spot, send_sem=self.xsend.at[m, d, s], recv_sem=self.recv.at[m, d, s],
            device_id={"dp": 1 - self.plane}, device_id_type=MESH)

    def across(self, m, source, spot):
        return pltpu.make_async_remote_copy(
            src_ref=source, dst_ref=spot, send_sem=self.csend.at[m], recv_sem=self.crecv.at[m],
            device_id={"col": self.other}, device_id_type=MESH)

    def keep(self, m):
        block, whole_ref, base = self.items[m][:3]
        return pltpu.make_async_copy(
            block, whole_ref.at[self.row, :, pl.ds(base, block.shape[1])], self.local.at[m])

    def when(self, m, inside, action):
        plane = self.items[m][4]
        if plane is None:
            if inside:
                action()
        else:
            pl.when((self.plane == plane) if inside else (self.plane != plane))(action)

    def begin(self, ms):
        for m in ms:
            def launch(m=m):
                for d in self.ways(m):
                    self.ring(m, d, 0, first=True).start()

            self.when(m, True, launch)
        for m in ms:
            block, whole_ref, base, share = self.items[m][:4]
            self.keep(m).start()
            if share:
                self.across(m, block, whole_ref.at[self.row, :, pl.ds(base, block.shape[1])]).start()

    def hand(self, m, d, s):
        if self.items[m][3]:
            spot = self.hop(m, d, s + 1)[2]
            self.across(m, spot, spot).start()

    def arrive(self, m, s):
        for d in self.ways(m):
            self.over(m, d, s).wait_recv()
            self.hand(m, d, s)

    def advance(self, m, s):
        def inside():
            for d in self.ways(m):
                self.ring(m, d, s).wait_recv()

                @pl.when(s < self.n - 2)
                def on():
                    self.ring(m, d, s + 1).start()

                if self.items[m][4] is not None:
                    self.over(m, d, s).start()
                self.hand(m, d, s)

        def outside():
            @pl.when(s > 0)
            def late():
                self.arrive(m, s - 1)

        self.when(m, True, inside)
        self.when(m, False, outside)

    def finish(self, ms):
        for m in ms:
            self.when(m, False, functools.partial(self.arrive, m, self.n - 2))
        for m in ms:
            block, whole_ref, base, share, plane = self.items[m]
            self.keep(m).wait()
            if share:
                spot = whole_ref.at[:, :, pl.ds(base, block.shape[1])]
                theirs = whole_ref.at[:, :, pl.ds(self.other * block.shape[1], block.shape[1])]
                self.across(m, spot, theirs).wait_recv()
                self.across(m, spot, theirs).wait_send()

            def drain(m=m, plane=plane):
                def sent(s, carry):
                    for d in self.ways(m):
                        self.ring(m, d, s).wait_send()
                        if plane is not None:
                            self.over(m, d, s).wait_send()
                    return carry

                lax.fori_loop(0, self.n - 1, sent, 0)

            self.when(m, True, drain)


def gather_sems(n, count):
    dma = pltpu.SemaphoreType.DMA
    return [dma((count, 2, n - 1))] * 2 + [dma((count,))] * 3 + [dma((count, 2, n - 1))]


def gather_kernel(n, *refs):
    blocks = refs[:5]
    x_ref = refs[5]
    wide, small, pair = refs[6:9]
    sems = refs[9:15]
    xsems = refs[15]
    core = lax.axis_index("col")
    items = [(blocks[m], wide, m * blocks[m].shape[1], False, None) for m in range(4)]
    items.append((blocks[4], small, core * blocks[4].shape[1], True, None))
    g = Gather(n, items, sems)
    greet(n, g.right, g.left, True, False)
    g.begin(range(5))
    mine = pltpu.make_async_copy(x_ref, pair.at[core], xsems.at[0])
    mine.start()
    theirs = pltpu.make_async_remote_copy(
        src_ref=x_ref, dst_ref=pair.at[core], send_sem=xsems.at[1], recv_sem=xsems.at[2],
        device_id={"col": 1 - core}, device_id_type=MESH)
    theirs.start()

    def step(s, carry):
        for m in range(5):
            g.advance(m, s)
        return carry

    lax.fori_loop(0, n - 1, step, 0)
    g.finish(range(5))
    mine.wait()
    theirs.wait()


def gather_first(n, blocks, small, x):
    rows, width = blocks[0].shape
    any_spec = pl.BlockSpec(memory_space=pl.ANY)
    vmem_spec = pl.BlockSpec(memory_space=pltpu.VMEM)
    shapes = [(n, rows, 4 * width), (n, small.shape[0], 2 * small.shape[1]), (2,) + x.shape]
    return pl.pallas_call(
        functools.partial(gather_kernel, n),
        in_specs=[vmem_spec] * 6,
        out_specs=[any_spec] * 3,
        out_shape=[jax.ShapeDtypeStruct(shape, BF) for shape in shapes],
        scratch_shapes=gather_sems(n, 5) + [pltpu.SemaphoreType.DMA((3,))],
        compiler_params=pltpu.CompilerParams(
            collective_id=1, has_side_effects=True, vmem_limit_bytes=VMEM_MAX),
        name="gather_first",
    )(*blocks, small, x)


class Scatter:
    def __init__(self, n, items, sems):
        self.n = n
        self.items = items
        self.send, self.recv, self.local, self.sib, self.dsend, self.drecv, self.xsend, self.xrecv = sems
        self.me, self.right, self.left = neighbours(n)
        self.plane = lax.axis_index("dp")
        self.twin = 1 - self.plane

    def ways(self, m):
        return range(len(split_cols(self.items[m][2], m % 2)))

    def loads(self, m):
        ref, base, width, other, own, sib = self.items[m][:6]
        copies = [pltpu.make_async_copy(ref.at[:, :, pl.ds(base, width)], own, self.local.at[m])]
        if other is not None:
            copies.append(pltpu.make_async_copy(other, sib, self.sib.at[m]))
        return copies

    def begin(self, ms):
        for m in ms:
            for copy in self.loads(m):
                copy.start()

    def ready(self, m):
        for copy in self.loads(m):
            copy.wait()

    def part(self, m, d, s):
        place = mod(self.me - 1 - s, self.n) if d == 0 else mod(self.me + 1 + s, self.n)
        start, size = split_cols(self.items[m][2], m % 2)[d]
        return ring_row(mod(place, self.n), self.n), slice(start, start + size)

    def ring(self, m, d, s):
        own, ring = self.items[m][4], self.items[m][6]
        owner, cols = self.part(m, d, s)
        return pltpu.make_async_remote_copy(
            src_ref=own.at[owner, :, cols], dst_ref=ring.at[s, :, cols],
            send_sem=self.send.at[m, d, s], recv_sem=self.recv.at[m, d, s],
            device_id={"row": self.right if d == 0 else self.left}, device_id_type=MESH)

    def plane_of(self, m):
        return self.items[m][10] if len(self.items[m]) > 10 else None

    def inside(self, m, action):
        plane = self.plane_of(m)
        if plane is None:
            action()
        else:
            pl.when(self.plane == plane)(action)

    def over(self, m, d, s):
        own, inbox = self.items[m][4], self.items[m][11]
        owner, cols = self.part(m, d, s)
        return pltpu.make_async_remote_copy(
            src_ref=own.at[owner, :, cols], dst_ref=inbox.at[owner, :, cols],
            send_sem=self.xsend.at[m, d, s], recv_sem=self.xrecv.at[m, d, s],
            device_id={"dp": self.twin}, device_id_type=MESH)

    def send_over(self, m):
        def one(s, carry):
            for d in self.ways(m):
                owner, cols, value = self.total(m, d, s, False, False)
                self.items[m][4][owner, :, cols] = value
                self.over(m, d, s).start()
            return carry

        lax.fori_loop(0, self.n, one, 0)

    def total(self, m, d, s, arrived, dp=True):
        other, own, sib, ring = self.items[m][3:7]
        owner, cols = self.part(m, d, s)
        value = own[owner, :, cols].astype(F32)
        if other is not None:
            value = value + sib[owner, :, cols].astype(F32)
        if dp and self.plane_of(m) is not None:
            self.over(m, d, s).wait_recv()
            value = value + self.items[m][11][owner, :, cols].astype(F32)
        if arrived:
            value = value + ring[s - 1, :, cols].astype(F32)
        return owner, cols, value.astype(own.dtype)

    def start(self, m):
        def go():
            for d in self.ways(m):
                if self.items[m][3] is not None:
                    owner, cols, value = self.total(m, d, 0, False)
                    self.items[m][4][owner, :, cols] = value
                self.ring(m, d, 0).start()

        self.inside(m, go)
        if self.plane_of(m) is not None:
            pl.when(self.plane != self.plane_of(m))(lambda: self.send_over(m))

    def advance(self, m, s):
        def go():
            for d in self.ways(m):
                self.ring(m, d, s - 1).wait_recv()
                owner, cols, value = self.total(m, d, s, True)
                self.items[m][4][owner, :, cols] = value
                self.ring(m, d, s).start()

        self.inside(m, go)

    def swap(self, m):
        low, twin = self.items[m][7:9]
        return pltpu.make_async_remote_copy(
            src_ref=low, dst_ref=twin, send_sem=self.dsend.at[m], recv_sem=self.drecv.at[m],
            device_id={"dp": self.twin}, device_id_type=MESH)

    def settle(self, m):
        def go():
            for d in self.ways(m):
                self.ring(m, d, self.n - 2).wait_recv()
                owner, cols, value = self.total(m, d, self.n - 1, True)
                self.items[m][7][:, cols] = value
            if self.items[m][8] is not None:
                self.swap(m).start()

        self.inside(m, go)

    def finish(self, m):
        low, twin, out = self.items[m][7:10]
        self.swap(m).wait_recv()
        out[...] = low[...].astype(F32) + twin[...].astype(F32)
        self.swap(m).wait_send()
        self.drain(m)

    def drain(self, m):
        def sent(s, carry):
            for d in self.ways(m):
                self.ring(m, d, s).wait_send()
            return carry

        def ring_done():
            lax.fori_loop(0, self.n - 1, sent, 0)

        self.inside(m, ring_done)
        if self.plane_of(m) is not None:
            def given(s, carry):
                for d in self.ways(m):
                    self.over(m, d, s).wait_send()
                return carry

            @pl.when(self.plane != self.plane_of(m))
            def given_done():
                lax.fori_loop(0, self.n, given, 0)


def scatter_sems(n, count, planes=False):
    dma = pltpu.SemaphoreType.DMA
    return [dma((count, 2, n - 1))] * 2 + [dma((count,))] * 4 + [dma((count, 2, n) if planes else (1,))] * 2


def scatter_plan(arrays, swap=True):
    scratch = []
    for array, width, share in arrays:
        n, rows, full = array.shape
        kind = array.dtype
        scratch.append(pltpu.VMEM((n, rows, width), kind))
        scratch.append(pltpu.VMEM((n, rows, width) if share else (1, 16, HD), kind))
        scratch.append(pltpu.VMEM((n - 1, rows, width), kind))
        if swap:
            scratch.append(pltpu.VMEM((rows, width), kind))
            scratch.append(pltpu.VMEM((rows, width), kind))
    return scratch


def post_kernel(n, normed_ref, d_ref, w_ref, x_ref, dmid_ref, gain_ref, small, *refs):
    late = refs[:4]
    own_w = refs[4:8]
    gin_ref = refs[8]
    outs = refs[9:14]
    late_outs = refs[14:18]
    dgain_ref = refs[18]
    turned, back, leave, came, dg_own, dg_sib, small_sib = refs[19:26]
    late_in = refs[26:30]
    scratch = refs[30:55]
    side, late_send, late_recv = refs[55:58]
    sems = refs[58:]
    turn = pl.program_id(0)
    core = lax.axis_index("col")
    other = 1 - core
    rows_all, dim = x_ref.shape
    width = outs[0].shape[1]
    block = outs[0].shape[0]
    items = []
    for m in range(5):
        first, sib = (0, None) if m < 4 else (core * HD, small_sib)
        items.append((None if m < 4 else small, first, outs[m].shape[1], sib)
                     + tuple(scratch[5 * m:5 * m + 5]) + (outs[m],))
    g = Scatter(n, items, sems)
    steps = 2 * rows_all // TILE

    def push(src, dst, at):
        return pltpu.make_async_remote_copy(
            src_ref=src, dst_ref=dst, send_sem=side.at[2 * at], recv_sem=side.at[2 * at + 1],
            device_id={"col": other}, device_id_type=MESH)

    def late_swap(i):
        return pltpu.make_async_remote_copy(
            src_ref=late[i], dst_ref=late_in[i], send_sem=late_send.at[i], recv_sem=late_recv.at[i],
            device_id={"dp": g.twin}, device_id_type=MESH)

    planes = (None, 0, 1, None)

    def late_start(i):
        if planes[i] is None:
            late_swap(i).start()
        else:
            pl.when(g.plane == planes[i])(lambda: late_swap(i).start())

    def late_end(i):
        if planes[i] is None:
            late_swap(i).wait()
            late_outs[i][...] = late[i][...].astype(F32) + late_in[i][...].astype(F32)
        else:
            @pl.when(g.plane == planes[i])
            def given():
                late_swap(i).wait_send()
                late_outs[i][...] = late[i][...].astype(F32)

            @pl.when(g.plane != planes[i])
            def taken():
                late_swap(i).wait_recv()
                late_outs[i][...] = late_in[i][...].astype(F32)

    cross = push(small.at[:, :, pl.ds(other * HD, HD)], small_sib, 0)
    swap_back = push(leave, came, 1)
    swap_gain = push(dg_own, dg_sib, 2)

    @pl.when(turn == 0)
    def first_turn():
        greet(n, g.right, g.left, True, True)
        cross.start()
        for i in range(4):
            late_start(i)
        for i in range(steps):
            rows = slice(i * TILE, (i + 1) * TILE)
            turned[:, rows] = normed_ref[rows, :].T
            back[rows, :] = jnp.zeros((TILE, dim), F32)

    rate = (n + 5) // 7

    def slot(u):
        for m in range(5):
            v = u - 2 * (m % 4)
            if v < 1:
                continue
            low, high = max(1, rate * (v - 1) + 1), min(n - 1, rate * v + 1)
            if low < high:
                def one(s, carry, m=m):
                    g.advance(m, s)
                    return carry

                lax.fori_loop(low, high, one, 0)
            elif rate * (v - 1) + 1 < n - 1 + rate:
                g.settle(m)

    for m in range(4):
        @pl.when(turn == m)
        def this():
            for part in range(2):
                cols = slice(part * (width // 2), (part + 1) * (width // 2))
                grad = nn(turned[...], d_ref[:, cols]).astype(BF)
                for q in range(n):
                    items[m][4][q, :, cols] = grad[q * block:(q + 1) * block]
            g.start(m)
            slot(2 * m)
            if m == 0:
                cross.wait()
                g.begin((4,))
                g.ready(4)
                g.start(4)
            for i in range(steps):
                rows = slice(i * TILE, (i + 1) * TILE)
                back[rows, :] += nt(d_ref[rows, :], w_ref[...])
            slot(2 * m + 1)

    @pl.when(turn == 3)
    def rest():
        theirs = pl.multiple_of(other * rows_all, TILE)
        for i in range(rows_all // TILE):
            rows = slice(i * TILE, (i + 1) * TILE)
            leave[rows, :] = back[pl.ds(theirs + i * TILE, TILE), :].astype(BF)
        swap_back.start()
        slot(8)
        slot(9)
        swap_back.wait()
        mine = pl.multiple_of(core * rows_all, TILE)
        gain = gain_ref[...]
        for i in range(rows_all // TILE):
            rows = slice(i * TILE, (i + 1) * TILE)
            xf = x_ref[rows, :].astype(F32)
            inv = lax.rsqrt(jnp.mean(xf * xf, axis=1, keepdims=True) + EPS)
            weighted = (back[pl.ds(mine + i * TILE, TILE), :] + came[rows, :].astype(F32)) * gain
            inner = jnp.mean(weighted * xf, axis=1, keepdims=True)
            value = dmid_ref[rows, :].astype(F32) + weighted * inv - xf * (inv * inv * inv) * inner
            gin_ref[rows, :] = value.astype(BF)
            if i < 2:
                slot(10 + i)
        for u in range(12, 15):
            slot(u)
        for i in range(4):
            late_end(i)
        total = jnp.zeros((block, 1), F32)
        for m in range(4):
            g.finish(m)
            total = total + jnp.sum(outs[m][...] * own_w[m][...].astype(F32), axis=1, keepdims=True)
        dg_own[...] = jnp.broadcast_to(total, (block, HD))
        swap_gain.start()
        g.finish(4)
        swap_gain.wait()
        dgain_ref[...] = dg_own[...] + dg_sib[...]


def post(n, normed, dqkvg, wide, x, dmid, gain, small, late, own_w):
    total, dim = normed.shape
    width = wide.shape[1] // 4
    rows = x.shape[0]
    block = dim // n
    arrays = [(jax.ShapeDtypeStruct((n, block, width), BF), width, False)] * 4 + [(small, HD, True)]
    any_spec = pl.BlockSpec(memory_space=pl.ANY)
    dma = pltpu.SemaphoreType.DMA
    outs = [((a.shape[1], w), F32) for a, w, share in arrays]
    late_outs = [(a.shape, F32) for a in late]
    shapes = [((rows, dim), BF)] + outs + late_outs + [((block, HD), F32)]
    return pl.pallas_call(
        functools.partial(post_kernel, n),
        grid=(4,),
        in_specs=[
            whole((total, dim)),
            pl.BlockSpec((total, width), lambda t: (0, t)),
            pl.BlockSpec((dim, width), lambda t: (0, t)),
            whole((rows, dim)),
            whole((rows, dim)),
            whole((1, dim)),
            any_spec,
        ] + [whole(a.shape) for a in late] + [whole(a.shape) for a in own_w],
        out_specs=[whole(shape) for shape, kind in shapes],
        out_shape=[jax.ShapeDtypeStruct(shape, kind) for shape, kind in shapes],
        scratch_shapes=[
            pltpu.VMEM((dim, total), BF),
            pltpu.VMEM((total, dim), F32),
            pltpu.VMEM((rows, dim), BF),
            pltpu.VMEM((rows, dim), BF),
            pltpu.VMEM((block, HD), F32),
            pltpu.VMEM((block, HD), F32),
            pltpu.VMEM((n, small.shape[1], HD), F32),
        ]
        + [pltpu.VMEM(a.shape, BF) for a in late]
        + scatter_plan(arrays)
        + [dma((6,)), dma((4,)), dma((4,))]
        + scatter_sems(n, 5),
        compiler_params=pltpu.CompilerParams(
            collective_id=2, has_side_effects=True, vmem_limit_bytes=VMEM_MAX),
        name="post",
    )(normed, dqkvg, wide, x, dmid, gain, small, *late, *own_w)


def local(
    tokens_in,
    grad_out,
    gain_attn,
    gain_ffn,
    w_query,
    w_key,
    w_value,
    w_gate,
    w_out,
    w_ffn_gate,
    w_ffn_up,
    w_ffn_down,
    persist_key,
    persist_value,
    mem_rate,
    mem_momentum,
    mem_forget,
    segment_ids,
    decay_index,
):
    n = lax.axis_size("row")
    core = lax.axis_index("col")
    local_tok, dim = tokens_in.shape
    heads = mem_rate.shape[1]
    width = heads * HD
    piece = gain_attn.shape[0]
    small = jnp.concatenate(
        [persist_key, persist_value, gain_attn[None, :], gain_ffn[None, :]], axis=0)
    small = jnp.pad(small, ((0, 48 - small.shape[0]), (0, HD - piece)))
    wide, small_all, pair = gather_first(n, (w_query, w_key, w_value, w_gate), small, tokens_in)
    wide = wide.reshape(dim, 4 * width)
    small_all = small_all.reshape(n, 48, 2, HD)[:, :, :, :piece].transpose(1, 0, 2, 3).reshape(48, dim)
    gain_a = small_all[2 * P_SIZE][None, :].astype(F32)
    gain_f = small_all[2 * P_SIZE + 1][None, :].astype(F32)
    own_small = lax.dynamic_slice_in_dim(small_all, core * width, width, 1)
    pad = ((0, HD - P_SIZE), (0, 0))
    pkey = jnp.pad(own_small[:P_SIZE], pad)
    pvalue = jnp.pad(own_small[P_SIZE:2 * P_SIZE], pad)

    inputs = pair.reshape(2 * local_tok, dim).astype(F32)
    inverse_a = lax.rsqrt(jnp.mean(inputs * inputs, axis=-1, keepdims=True) + EPS)
    normed = (inputs * inverse_a * gain_a).astype(BF)
    qkvg = nn(normed, wide).astype(BF)

    total = qkvg.shape[0]
    spans = total // CH
    span_ids = segment_ids.reshape(total // SEQ, SEQ // CH, CH)
    same = (span_ids[:, 1:, 0] == span_ids[:, :-1, CH - 1]).astype(F32)
    keep = jnp.concatenate([jnp.zeros((total // SEQ, 1), F32), same], axis=1).reshape(spans, 1)
    choose = (decay_index[:, None] == jnp.arange(mem_rate.shape[0])[None, :]).astype(F32)
    tables = jnp.concatenate([mem_rate, mem_momentum, 1.0 - mem_forget], axis=1)
    picked = jnp.dot(choose, tables, precision=HIGH)
    coef = jnp.stack(
        [jnp.broadcast_to(keep, (spans, heads))] + [picked[:, i * heads:(i + 1) * heads] for i in range(3)]
    ).reshape(4, spans * heads)
    segc, segr = segment_ids[:, None], segment_ids[None, :]

    later = (w_out, w_ffn_gate, w_ffn_up, w_ffn_down)
    lse, reads, m0, err, comb_tok, full_out, full_gate, full_up, full_down = mix_forward(
        n, qkvg, pkey, pvalue, segc, segr, coef, heads, later)
    full_out, full_gate, full_up = [a.reshape(dim, -1) for a in (full_out, full_gate, full_up)]
    full_down = full_down.reshape(-1, dim)
    result, dmid, dgain_f, sums, dcomb, *parts = ffn_block(
        comb_tok, tokens_in, grad_out, full_out, full_gate, full_up, full_down, gain_f)
    parts = [a.reshape(n, a.shape[0] // n, a.shape[1]) for a in parts]
    dqkvg, dpk, dpv, *grads_late = mix_backward(
        n, qkvg, dcomb, pkey, pvalue, segc, segr, coef, lse, reads, m0, err, heads,
        parts[0::2], parts[1::2])

    place = jnp.zeros((2 * P_SIZE, dim), F32)
    place = lax.dynamic_update_slice_in_dim(
        place, jnp.concatenate([dpk[:P_SIZE], dpv[:P_SIZE]], axis=0), core * width, 1)
    packed = jnp.concatenate([place, jnp.zeros((1, dim), F32), dgain_f], axis=0)
    packed = packed.reshape(2 * P_SIZE + 2, n, 2, piece).transpose(1, 0, 2, 3)
    packed = jnp.pad(packed, ((0, 0), (0, 0), (0, 0), (0, HD - piece)))
    stats = jnp.sum(sums.reshape(8, dim // HD, HD), axis=1)[:6]
    stats = jnp.broadcast_to(stats[None, :, None, :], (n, 6, 2, HD))
    packed = jnp.concatenate([packed, stats], axis=1).reshape(n, 2 * P_SIZE + 8, 2 * HD)
    grad_in, *rest = post(
        n, normed, dqkvg, wide, tokens_in, dmid, gain_a, packed, grads_late,
        (w_query, w_key, w_value, w_gate))
    grads, part, dgain_a = rest[:4] + rest[5:9], rest[4], rest[9]
    dgain_a = lax.dynamic_slice_in_dim(dgain_a[:, 0], core * piece, piece, 0) / gain_attn.astype(F32)
    entry_count = local_tok * dim * lax.axis_size("dp") * n * lax.axis_size("col")
    rms_stats = jnp.sqrt(jnp.sum(part[2 * P_SIZE + 2:2 * P_SIZE + 5], axis=1) / entry_count)
    part = part[:, :piece]
    return (
        result,
        grad_in,
        grads[0],
        grads[1],
        grads[2],
        grads[3],
        grads[4],
        grads[5],
        grads[6],
        grads[7],
        dgain_a,
        part[2 * P_SIZE + 1],
        part[:P_SIZE],
        part[P_SIZE:2 * P_SIZE],
        rms_stats,
    )


def solution(mesh):
    tokens = P(("dp", "row", "col"), None)
    vector = P(("row", "col"))
    weight = P("row", "col")
    persist = P(None, ("row", "col"))
    table = P(None, "col")
    ids = P(("dp", "row"))
    return jax.shard_map(
        local,
        mesh=mesh,
        in_specs=(tokens, tokens, vector, vector) + (weight,) * 8 + (persist,) * 2 + (table,) * 3 + (ids,) * 2,
        out_specs=(tokens, tokens) + (weight,) * 8 + (vector,) * 2 + (persist,) * 2 + (P(),),
        check_vma=False,
    )
```

```python
import functools
import jax
import jax.numpy as jnp
from jax import lax
from jax.experimental import pallas as pl
from jax.experimental.pallas import tpu as pltpu
from jax.sharding import PartitionSpec as P

HD = 128
P_SIZE = 16
SEG = 1024
CH = 64
SEQ = 2048
TILE = 256
TPS = SEG // TILE
EPS = 1e-06
NEG = -1e30
SCALE = HD ** (-0.5)
LOG2E = 1.4426950408889634
VMEM_MAX = 60 * 1024 * 1024
F32 = jnp.float32
BF = jnp.bfloat16
HIGH = lax.Precision.HIGHEST
MESH = pl.DeviceIdType.MESH


def nn(a, b):
    return lax.dot_general(a, b, (((1,), (0,)), ((), ())), preferred_element_type=F32)


def nt(a, b):
    return lax.dot_general(a, b, (((1,), (1,)), ((), ())), preferred_element_type=F32)


def tn(a, b):
    return lax.dot_general(a, b, (((0,), (0,)), ((), ())), preferred_element_type=F32)


def token_bias(segc, segr, part):
    width = (part + 1) * TILE
    same = segc == segr[:, :width]
    qpos = lax.broadcasted_iota(jnp.int32, (TILE, width), 0) + part * TILE
    kpos = lax.broadcasted_iota(jnp.int32, (TILE, width), 1)
    return jnp.where(same & (kpos <= qpos), 0.0, NEG).astype(F32)


def mix_forward_tile(heads, part, tile, q_ref, k_ref, v_ref, g_ref, pk_ref, pv_ref, segc_ref,
                     segr_ref, coef_ref, comb_ref, lse_ref, reads_ref, m0_ref, err_ref, mem, mom):
    width = (part + 1) * TILE
    base = part * TILE
    bias = token_bias(segc_ref[...], segr_ref[...], part)
    lane = lax.broadcasted_iota(jnp.int32, (TILE, HD), 1)
    lse_all = jnp.zeros((TILE, HD), F32)
    blocks = TILE // CH
    reads = [[None] * blocks for head in range(heads)]
    per_turn = -(-heads // blocks)
    attention = {}

    def memory(step, head):
        cols = slice(head * HD, (head + 1) * HD)
        rows = slice(step * CH, (step + 1) * CH)
        at = (tile * blocks + step) * heads + head
        keep = coef_ref[0, at]
        rate = coef_ref[1, at]
        moment = coef_ref[2, at]
        stay = coef_ref[3, at]
        start = mem[head] * keep
        low_start = start.astype(BF)
        m0_ref[step, head] = low_start
        key = k_ref[base + step * CH:base + (step + 1) * CH, cols]
        value = v_ref[base + step * CH:base + (step + 1) * CH, cols]
        both = jnp.concatenate([q_ref[rows, cols], key], axis=0)
        got = nn(both, low_start)
        reads[head][step] = got[:CH] * SCALE
        err = (got[CH:] * SCALE - value.astype(F32)).astype(BF)
        err_ref[rows, cols] = err
        speed = (moment * keep) * mom[head] - (rate * SCALE) * tn(key, err)
        mom[head] = speed
        mem[head] = stay * start + speed

    def attend(head):
        cols = slice(head * HD, (head + 1) * HD)
        query = q_ref[:, cols]
        tok = nt(query, k_ref[:width, cols]) * (SCALE * LOG2E) + bias
        per = nt(query, pk_ref[:, cols]) * (SCALE * LOG2E)
        per = jnp.where(lane < P_SIZE, per, NEG)
        top = jnp.maximum(jnp.max(tok, axis=1, keepdims=True), jnp.max(per, axis=1, keepdims=True))
        tok_e = jnp.exp2(tok - top)
        per_e = jnp.exp2(per - top)
        total = jnp.sum(tok_e, axis=1, keepdims=True) + jnp.sum(per_e, axis=1, keepdims=True)
        att = nn(tok_e.astype(BF), v_ref[:width, cols]) + nn(per_e.astype(BF), pv_ref[:, cols])
        attention[head] = att / total
        return top + jnp.log2(total)

    for step in range(blocks):
        for head in range(heads):
            memory(step, head)
        for head in range(step * per_turn, min(heads, (step + 1) * per_turn)):
            lse_all = jnp.where(lane == head, attend(head), lse_all)
    for head in range(heads):
        cols = slice(head * HD, (head + 1) * HD)
        read = jnp.concatenate(reads[head], axis=0)
        reads_ref[:, cols] = read.astype(BF)
        gate = jax.nn.sigmoid(g_ref[:, cols].astype(F32))
        comb_ref[:, cols] = (attention[head] + gate * read).astype(BF)
    lse_ref[...] = lse_all


def hop_bound(turn, tiles, hops):
    return (turn * hops) // tiles


def hop_early(turn, tiles, hops):
    return jnp.minimum(hops, (turn * hops + tiles - 1) // tiles)


def mix_forward_kernel(heads, n, tiles, q_ref, k_ref, v_ref, g_ref, pk_ref, pv_ref, segc_ref,
                       segr_ref, coef_ref, b0, b1, b2, lse_ref, reads_ref, m0_ref, err_ref,
                       comb_out, w0, w1, w2, mem, mom, comb_all, csems, *sems):
    tile = pl.program_id(0)
    core = lax.axis_index("col")
    blocks, wholes = (b0, b1, b2), (w0, w1, w2)
    planes = (0, 1, None)
    items = [(blk, ref, core * blk.shape[1], True, plane)
             for blk, ref, plane in zip(blocks, wholes, planes)]
    g = Gather(n, items, sems)
    each = range(len(items))
    width = heads * HD
    per_core = tiles // 2

    def hops(low, high):
        def one(s, carry):
            for m in each:
                g.advance(m, s)
            return carry

        lax.fori_loop(low, high, one, 0)

    def place(device, index):
        return comb_out.at[pl.ds(index * TILE, TILE), pl.ds(device * width, width)]

    @pl.when(tile == 0)
    def clear():
        greet(n, g.right, g.left, True, True)
        g.begin(each)
        mem[...] = jnp.zeros_like(mem)
        mom[...] = jnp.zeros_like(mom)

    @pl.when(tile > 0)
    def pass_on():
        hops(hop_bound(tile - 1, tiles, n - 1), hop_bound(tile, tiles, n - 1))

    for part in range(TPS):
        @pl.when(lax.rem(tile, TPS) == part)
        def work():
            mix_forward_tile(heads, part, tile, q_ref, k_ref, v_ref, g_ref, pk_ref, pv_ref,
                             segc_ref, segr_ref, coef_ref, comb_all.at[tile], lse_ref, reads_ref,
                             m0_ref, err_ref, mem, mom)

    def stay(index):
        return pltpu.make_async_copy(
            comb_all.at[core * per_core + index], place(core, index), csems.at[0, index])

    def leave(index):
        return pltpu.make_async_remote_copy(
            src_ref=comb_all.at[(1 - core) * per_core + index], dst_ref=place(core, index),
            send_sem=csems.at[1, index], recv_sem=csems.at[2, index],
            device_id={"col": 1 - core}, device_id_type=MESH)

    index = lax.rem(tile, per_core)

    @pl.when(tile // per_core == core)
    def mine():
        stay(index).start()

    @pl.when(tile // per_core != core)
    def theirs():
        leave(index).start()

    @pl.when(tile == tiles - 1)
    def end():
        hops(hop_bound(tiles - 1, tiles, n - 1), n - 1)
        g.finish(each)
        for i in range(per_core):
            stay(i).wait()
            leave(i).wait()


def mix_forward(n, qkvg, pkey, pvalue, segc, segr, coef, heads, blocks):
    total = qkvg.shape[0]
    width = heads * HD
    tiles = total // TILE
    per = TILE // CH
    any_spec = pl.BlockSpec(memory_space=pl.ANY)
    return pl.pallas_call(
        functools.partial(mix_forward_kernel, heads, n, tiles),
        grid=(tiles,),
        in_specs=[
            pl.BlockSpec((TILE, width), lambda t: (t, 0)),
            pl.BlockSpec((SEG, width), lambda t: (t // TPS, 1)),
            pl.BlockSpec((SEG, width), lambda t: (t // TPS, 2)),
            pl.BlockSpec((TILE, width), lambda t: (t, 3)),
            pl.BlockSpec((HD, width), lambda t: (0, 0)),
            pl.BlockSpec((HD, width), lambda t: (0, 0)),
            pl.BlockSpec((TILE, 1), lambda t: (t, 0)),
            pl.BlockSpec((1, SEG), lambda t: (0, t // TPS)),
            pl.BlockSpec(memory_space=pltpu.SMEM),
        ] + [whole(b.shape) for b in blocks],
        out_specs=[
            pl.BlockSpec((TILE, HD), lambda t: (t, 0)),
            pl.BlockSpec((TILE, width), lambda t: (t, 0)),
            pl.BlockSpec((per, heads, HD, HD), lambda t: (t, 0, 0, 0)),
            pl.BlockSpec((TILE, width), lambda t: (t, 0)),
        ] + [any_spec] * 4,
        out_shape=[
            jax.ShapeDtypeStruct((total, HD), F32),
            jax.ShapeDtypeStruct((total, width), BF),
            jax.ShapeDtypeStruct((total // CH, heads, HD, HD), BF),
            jax.ShapeDtypeStruct((total, width), BF),
            jax.ShapeDtypeStruct((total // 2, 2 * width), BF),
        ] + [jax.ShapeDtypeStruct((n, b.shape[0], 2 * b.shape[1]), BF) for b in blocks],
        scratch_shapes=[
            pltpu.VMEM((heads, HD, HD), F32),
            pltpu.VMEM((heads, HD, HD), F32),
            pltpu.VMEM((tiles, TILE, width), BF),
            pltpu.SemaphoreType.DMA((3, tiles // 2)),
        ] + gather_sems(n, 3),
        compiler_params=pltpu.CompilerParams(
            collective_id=3, has_side_effects=True, vmem_limit_bytes=VMEM_MAX),
        name="mix_forward",
    )(qkvg, qkvg, qkvg, qkvg, pkey, pvalue, segc, segr, coef, *blocks)


def mix_backward_tile(heads, part, tile, q_ref, k_ref, v_ref, g_ref, dc_ref, pk_ref, pv_ref,
                      segc_ref, segr_ref, coef_ref, lse_ref, reads_ref, m0_ref, err_ref, dout_ref,
                      dmem, dmom, dk_acc, dv_acc, dpk_acc, dpv_acc):
    width = (part + 1) * TILE
    base = part * TILE
    wide = heads * HD
    bias = token_bias(segc_ref[...], segr_ref[...], part)
    pcol = lax.broadcasted_iota(jnp.int32, (TILE, HD), 1)
    blocks = TILE // CH
    lse_all = lse_ref[...]
    dreads = {}
    mem_q, mem_k, mem_v = {}, {}, {}

    def gates(head):
        cols = slice(head * HD, (head + 1) * HD)
        upf = dc_ref[:, cols].astype(F32)
        gate = jax.nn.sigmoid(g_ref[:, cols].astype(F32))
        dreads[head] = (upf * gate).astype(BF)
        dgate = upf * reads_ref[:, cols].astype(F32) * gate * (1.0 - gate)
        dout_ref[:, 3 * wide + head * HD:3 * wide + (head + 1) * HD] = dgate.astype(BF)

    def memory(step, head):
        cols = slice(head * HD, (head + 1) * HD)
        rows = slice(step * CH, (step + 1) * CH)
        at = (tile * blocks + step) * heads + head
        keep = coef_ref[0, at]
        rate = coef_ref[1, at]
        moment = coef_ref[2, at]
        stay = coef_ref[3, at]
        key = k_ref[base + step * CH:base + (step + 1) * CH, cols]
        start = m0_ref[step, head]
        err = err_ref[rows, cols]
        dstate = dmem[head]
        dspeed = dmom[head] + dstate
        dslope = (dspeed * (-rate)).astype(BF)
        derr = nn(key, dslope) * SCALE
        top = jnp.concatenate([dreads[head][rows], derr.astype(BF)], axis=0)
        both = jnp.concatenate([q_ref[rows, cols], key], axis=0)
        dmem[head] = keep * (stay * dstate + SCALE * tn(both, top))
        dmom[head] = (moment * keep) * dspeed
        back = nt(top, start)
        mem_q[head, step] = back[:CH]
        mem_k[head, step] = back[CH:] + nt(err, dslope)
        mem_v[head, step] = derr

    def attend(head):
        cols = slice(head * HD, (head + 1) * HD)
        query = q_ref[:, cols]
        up = dc_ref[:, cols]
        tok = nt(query, k_ref[:width, cols]) * (SCALE * LOG2E) + bias
        per = nt(query, pk_ref[:, cols]) * (SCALE * LOG2E)
        per = jnp.where(pcol < P_SIZE, per, NEG)
        lse = lse_all[:, head:head + 1]
        tok_p = jnp.exp2(tok - lse)
        per_p = jnp.exp2(per - lse)
        tok_dp = nt(up, v_ref[:width, cols])
        per_dp = nt(up, pv_ref[:, cols])
        inner = jnp.sum(tok_p * tok_dp, axis=1, keepdims=True) + jnp.sum(
            per_p * per_dp, axis=1, keepdims=True)
        tok_ds = (tok_p * (tok_dp - inner)).astype(BF)
        per_ds = (per_p * (per_dp - inner)).astype(BF)
        dquery = nn(tok_ds, k_ref[:width, cols]) + nn(per_ds, pk_ref[:, cols])
        dpk_acc[:, cols] += tn(per_ds, query) * SCALE
        dpv_acc[:, cols] += tn(per_p.astype(BF), up)
        dkey = tn(tok_ds, query)
        dval = tn(tok_p.astype(BF), up)
        own = slice(base, base + TILE)
        if part == TPS - 1:
            dk_acc[:, cols] = dkey
            dv_acc[:, cols] = dval
        else:
            dk_acc[:base + TILE, cols] += dkey
            dv_acc[:base + TILE, cols] += dval
        return dquery

    def finish(head, dquery):
        cols = slice(head * HD, (head + 1) * HD)
        own = slice(base, base + TILE)

        def rows_of(parts):
            return jnp.concatenate([parts[head, step] for step in range(blocks)], axis=0)

        dout_ref[:, cols] = ((dquery + rows_of(mem_q)) * SCALE).astype(BF)
        dout_ref[:, wide + head * HD:wide + (head + 1) * HD] = (
            (dk_acc[own, cols] + rows_of(mem_k)) * SCALE).astype(BF)
        dout_ref[:, 2 * wide + head * HD:2 * wide + (head + 1) * HD] = (
            dv_acc[own, cols] - rows_of(mem_v)).astype(BF)

    for head in range(heads):
        gates(head)
    per_turn = -(-heads // blocks)
    dqueries = {}
    for turn in range(blocks):
        for head in range(heads):
            memory(blocks - 1 - turn, head)
        for head in range(turn * per_turn, min(heads, (turn + 1) * per_turn)):
            dqueries[head] = attend(head)
    for head in range(heads):
        finish(head, dqueries[head])


def mix_backward_kernel(heads, n, tiles, q_ref, k_ref, v_ref, g_ref, dc_ref, pk_ref, pv_ref,
                        segc_ref, segr_ref, coef_ref, lse_ref, reads_ref, m0_ref, err_ref, *refs):
    own_refs, sib_refs = refs[:4], refs[4:8]
    dout_ref, dpk_ref, dpv_ref = refs[8:11]
    outs = refs[11:15]
    dmem, dmom, dk_acc, dv_acc = refs[15:19]
    scratch = refs[19:31]
    planes = (None, 0, 1, None)
    inbox = (None, refs[31], refs[32], None)
    sems = refs[33:]
    turn = pl.program_id(0)
    tile = tiles - 1 - turn
    items = [
        (own_refs[m], 0, outs[m].shape[1], sib_refs[m]) + tuple(scratch[3 * m:3 * m + 3]) + (outs[m], None, None, planes[m], inbox[m])
        for m in range(4)
    ]
    g = Scatter(n, items, sems)
    order = (3, 0, 1, 2)

    def hops(low, high):
        def one(s, carry):
            for m in order:
                g.advance(m, s)
            return carry

        lax.fori_loop(low, high, one, 0)

    @pl.when(turn == 0)
    def clear():
        greet(n, g.right, g.left, False, True)
        g.begin(order)
        dmem[...] = jnp.zeros_like(dmem)
        dmom[...] = jnp.zeros_like(dmom)
        dpk_ref[...] = jnp.zeros_like(dpk_ref)
        dpv_ref[...] = jnp.zeros_like(dpv_ref)
        for m in order:
            g.ready(m)
            g.start(m)
        for m in (1, 2):
            g.give(m)
        for m in (1, 2):
            g.inside(m, functools.partial(g.launch, m))

    @pl.when(turn > 0)
    def pass_on():
        hops(1 + hop_early(turn - 1, tiles - 2, n - 2), 1 + hop_early(turn, tiles - 2, n - 2))

    @pl.when(turn == tiles - 1)
    def settle():
        for m in order:
            g.settle(m)

    for part in range(TPS):
        @pl.when(lax.rem(tile, TPS) == part)
        def work():
            mix_backward_tile(heads, part, tile, q_ref, k_ref, v_ref, g_ref, dc_ref, pk_ref, pv_ref,
                              segc_ref, segr_ref, coef_ref, lse_ref, reads_ref, m0_ref, err_ref,
                              dout_ref, dmem, dmom, dk_acc, dv_acc, dpk_ref, dpv_ref)

    @pl.when(turn == tiles - 1)
    def end():
        for m in order:
            g.drain(m)


def mix_backward(n, qkvg, dcomb, pkey, pvalue, segc, segr, coef, lse, reads, m0, err, heads, owns, sibs):
    total = qkvg.shape[0]
    width = heads * HD
    tiles = total // TILE
    per = TILE // CH
    last = tiles - 1
    any_spec = pl.BlockSpec(memory_space=pl.ANY)
    arrays = [(a, a.shape[2], True) for a in owns]
    return pl.pallas_call(
        functools.partial(mix_backward_kernel, heads, n, tiles),
        grid=(tiles,),
        in_specs=[
            pl.BlockSpec((TILE, width), lambda t: (last - t, 0)),
            pl.BlockSpec((SEG, width), lambda t: ((last - t) // TPS, 1)),
            pl.BlockSpec((SEG, width), lambda t: ((last - t) // TPS, 2)),
            pl.BlockSpec((TILE, width), lambda t: (last - t, 3)),
            pl.BlockSpec((TILE, width), lambda t: (last - t, 0)),
            pl.BlockSpec((HD, width), lambda t: (0, 0)),
            pl.BlockSpec((HD, width), lambda t: (0, 0)),
            pl.BlockSpec((TILE, 1), lambda t: (last - t, 0)),
            pl.BlockSpec((1, SEG), lambda t: (0, (last - t) // TPS)),
            pl.BlockSpec(memory_space=pltpu.SMEM),
            pl.BlockSpec((TILE, HD), lambda t: (last - t, 0)),
            pl.BlockSpec((TILE, width), lambda t: (last - t, 0)),
            pl.BlockSpec((per, heads, HD, HD), lambda t: (last - t, 0, 0, 0)),
            pl.BlockSpec((TILE, width), lambda t: (last - t, 0)),
        ] + [any_spec] * 8,
        out_specs=[
            pl.BlockSpec((TILE, 4 * width), lambda t: (last - t, 0)),
            pl.BlockSpec((HD, width), lambda t: (0, 0)),
            pl.BlockSpec((HD, width), lambda t: (0, 0)),
        ] + [whole((a.shape[1], w)) for a, w, share in arrays],
        out_shape=[
            jax.ShapeDtypeStruct((total, 4 * width), BF),
            jax.ShapeDtypeStruct((HD, width), F32),
            jax.ShapeDtypeStruct((HD, width), F32),
        ] + [jax.ShapeDtypeStruct((a.shape[1], w), BF) for a, w, share in arrays],
        scratch_shapes=[
            pltpu.VMEM((heads, HD, HD), F32),
            pltpu.VMEM((heads, HD, HD), F32),
            pltpu.VMEM((SEG, width), F32),
            pltpu.VMEM((SEG, width), F32),
        ] + scatter_plan(arrays, False) + [pltpu.VMEM(a.shape, BF) for a in owns[1:3]] + scatter_sems(n, 4, True),
        compiler_params=pltpu.CompilerParams(
            collective_id=4, has_side_effects=True, vmem_limit_bytes=VMEM_MAX),
        name="mix_backward",
    )(qkvg, qkvg, qkvg, qkvg, dcomb, pkey, pvalue, segc, segr, coef, lse, reads, m0, err, *owns, *sibs)


def whole(shape):
    return pl.BlockSpec(shape, lambda t: (0,) * len(shape), pipeline_mode=pl.Buffered(1))


def ffn_kernel(tiles, comb_ref, x_ref, dy_ref, wo_ref, wg0, wg1, wu0, wu1, wd0, wd1, gain_ref,
               out_ref, dmid_ref, dgain_ref, sums_ref, dcomb_out, go_own, go_sib, gg_own, gg_sib,
               gu_own, gu_sib, gd_own, gd_sib, n2, n2t, mid, acc_out, acc_dn, hid_all, pair_all,
               dcomb_v, go_v, gbuf, ubuf, dbuf, keep_sem, send_sem, recv_sem, end_sem):
    turn = pl.program_id(0)
    core = lax.axis_index("col")
    other = 1 - core
    rows_all, dim = x_ref.shape
    half = dim // 2
    steps = rows_all // TILE
    ft = 2 * HD
    gain = gain_ref[...]
    slot = lax.rem(turn, 2)
    hidden_half = gg_own.shape[1]

    def push(src, dst, sem, rsem):
        return pltpu.make_async_remote_copy(
            src_ref=src, dst_ref=dst, send_sem=sem, recv_sem=rsem,
            device_id={"col": other}, device_id_type=MESH)

    def moves(t, s):
        stay, leave = [], []
        for i, (buf, own, sib) in enumerate(((gbuf, gg_own, gg_sib), (ubuf, gu_own, gu_sib))):
            cols = pl.ds(pl.multiple_of(t * HD, HD), HD)
            stay.append(pltpu.make_async_copy(
                buf.at[s, core], own.at[:, cols], keep_sem.at[i, s]))
            leave.append(push(buf.at[s, other], sib.at[:, cols], send_sem.at[i, s], recv_sem.at[i]))
        for i in range(2):
            rows = pl.ds(pl.multiple_of(i * hidden_half + t * HD, HD), HD)
            stay.append(pltpu.make_async_copy(
                dbuf.at[s, core, pl.ds(i * HD, HD)], gd_own.at[rows, :], keep_sem.at[2 + i, s]))
            leave.append(push(dbuf.at[s, other, pl.ds(i * HD, HD)], gd_sib.at[rows, :],
                              send_sem.at[2 + i, s], recv_sem.at[2 + i]))
        return stay, leave

    def settle(t, s):
        stay, leave = moves(t, s)
        for copy in stay:
            copy.wait()
        for copy in leave:
            copy.wait_send()

    @pl.when(turn == 0)
    def first():
        barrier = pltpu.get_barrier_semaphore()
        pl.semaphore_signal(barrier, inc=1, device_id={"col": other}, device_id_type=MESH)
        pl.semaphore_wait(barrier, 1)
        sums_ref[...] = jnp.zeros_like(sums_ref)
        dgain_ref[...] = jnp.zeros_like(dgain_ref)
        for i in range(steps):
            rows = slice(i * TILE, (i + 1) * TILE)
            xf = x_ref[rows, :].astype(F32)
            branch = nn(comb_ref[rows, :], wo_ref[...])
            middle = xf + branch
            mid[rows, :] = middle
            acc_out[rows, :] = middle
            inv = lax.rsqrt(jnp.mean(middle * middle, axis=1, keepdims=True) + EPS)
            normed = (middle * inv * gain).astype(BF)
            n2[rows, :] = normed
            n2t[:, rows] = normed.T
            acc_dn[rows, :] = jnp.zeros((TILE, dim), F32)
            sums_ref[0:1, :] += jnp.sum(xf * xf, axis=0, keepdims=True)
            sums_ref[1:2, :] += jnp.sum(branch * branch, axis=0, keepdims=True)

    wd = jnp.concatenate([wd0[...], wd1[...]], axis=0)
    both = jnp.concatenate([wg0[...], wg1[...], wu0[...], wu1[...]], axis=1)
    for i in range(steps):
        rows = slice(i * TILE, (i + 1) * TILE)
        gateup = nn(n2[rows, :], both)
        gate, up = gateup[:, :ft], gateup[:, ft:]
        dh = nt(dy_ref[rows, :], wd)
        sig = jax.nn.sigmoid(gate)
        silu = gate * sig
        hid = (silu * up).astype(BF)
        dg = (dh * up * (sig * (1.0 + gate * (1.0 - sig)))).astype(BF)
        du = (dh * silu).astype(BF)
        hid_all[rows, :] = hid
        pair = jnp.concatenate([dg, du], axis=1)
        pair_all[rows, :] = pair
        acc_out[rows, :] += nn(hid, wd)
        acc_dn[rows, :] += nt(pair, both)

    @pl.when(turn >= 2)
    def reuse():
        settle(turn - 2, slot)

    down = tn(hid_all[...], dy_ref[...]).astype(BF)
    grads = nn(n2t[...], pair_all[...]).astype(BF)
    for i in range(2):
        gbuf[slot, i] = grads[:, i * HD:(i + 1) * HD]
        ubuf[slot, i] = grads[:, ft + i * HD:ft + (i + 1) * HD]
        dbuf[slot, i] = down[:, i * half:(i + 1) * half]
    stay, leave = moves(turn, slot)
    for copy in stay + leave:
        copy.start()

    @pl.when(turn == tiles - 1)
    def last():
        for i in range(steps):
            rows = slice(i * TILE, (i + 1) * TILE)
            final = acc_out[rows, :]
            out_ref[rows, :] = final.astype(BF)
            sums_ref[2:3, :] += jnp.sum(final * final, axis=0, keepdims=True)
            middle = mid[rows, :]
            inv = lax.rsqrt(jnp.mean(middle * middle, axis=1, keepdims=True) + EPS)
            dnorm = acc_dn[rows, :]
            weighted = dnorm * gain
            inner = jnp.mean(weighted * middle, axis=1, keepdims=True)
            dgain_ref[...] += jnp.sum(dnorm * middle * inv, axis=0, keepdims=True)
            dmid = dy_ref[rows, :].astype(F32) + weighted * inv - middle * (inv * inv * inv) * inner
            low = dmid.astype(BF)
            dmid_ref[rows, :] = low
            dcomb = nt(low, wo_ref[...]).astype(BF)
            dcomb_v[0, rows, :] = dcomb[:, :half]
            dcomb_v[1, rows, :] = dcomb[:, half:]
        home = pl.ds(pl.multiple_of(core * rows_all, TILE), rows_all)
        stay_c = pltpu.make_async_copy(dcomb_v.at[core], dcomb_out.at[home, :], end_sem.at[0])
        leave_c = push(dcomb_v.at[other], dcomb_out.at[home, :], end_sem.at[1], end_sem.at[2])
        stay_c.start()
        leave_c.start()
        for i in range(dim // TILE):
            part = slice(i * TILE, (i + 1) * TILE)
            go = tn(comb_ref[:, part], dmid_ref[...]).astype(BF)
            go_v[0, part, :] = go[:, :half]
            go_v[1, part, :] = go[:, half:]
        stay_o = pltpu.make_async_copy(go_v.at[core], go_own, end_sem.at[3])
        leave_o = push(go_v.at[other], go_sib, end_sem.at[4], end_sem.at[5])
        stay_o.start()
        leave_o.start()
        settle(turn - 1, 1 - slot)
        settle(turn, slot)
        for i, sib in enumerate((gg_sib, gu_sib)):
            push(sib, sib, send_sem.at[i, 0], recv_sem.at[i]).wait_recv()
        for i in range(2):
            part = gd_sib.at[pl.ds(i * hidden_half, hidden_half), :]
            push(part, part, send_sem.at[2 + i, 0], recv_sem.at[2 + i]).wait_recv()
        stay_c.wait()
        stay_o.wait()
        leave_c.wait()
        leave_o.wait()


def ffn_block(comb, x, dy, w_out, w_gate, w_up, w_down, gain):
    rows, dim = x.shape
    hidden = w_gate.shape[1]
    tiles = hidden // (2 * HD)
    full = (rows, dim)
    half = dim // 2
    any_spec = pl.BlockSpec(memory_space=pl.ANY)
    front = pl.BlockSpec((dim, HD), lambda t: (0, t))
    rear = pl.BlockSpec((dim, HD), lambda t: (0, t + tiles))
    dma = pltpu.SemaphoreType.DMA
    return pl.pallas_call(
        functools.partial(ffn_kernel, tiles),
        grid=(tiles,),
        in_specs=[
            whole(full),
            whole(full),
            whole(full),
            whole((dim, dim)),
            front,
            rear,
            front,
            rear,
            pl.BlockSpec((HD, dim), lambda t: (t, 0)),
            pl.BlockSpec((HD, dim), lambda t: (t + tiles, 0)),
            whole((1, dim)),
        ],
        out_specs=[whole(full), whole(full), whole((1, dim)), whole((8, dim))] + [any_spec] * 9,
        out_shape=[
            jax.ShapeDtypeStruct(full, BF),
            jax.ShapeDtypeStruct(full, BF),
            jax.ShapeDtypeStruct((1, dim), F32),
            jax.ShapeDtypeStruct((8, dim), F32),
            jax.ShapeDtypeStruct((2 * rows, half), BF),
        ]
        + [jax.ShapeDtypeStruct((dim, half), BF)] * 2
        + [jax.ShapeDtypeStruct((dim, hidden // 2), BF)] * 4
        + [jax.ShapeDtypeStruct((hidden, half), BF)] * 2,
        scratch_shapes=[
            pltpu.VMEM(full, BF),
            pltpu.VMEM((dim, rows), BF),
            pltpu.VMEM(full, F32),
            pltpu.VMEM(full, F32),
            pltpu.VMEM(full, F32),
            pltpu.VMEM((rows, 2 * HD), BF),
            pltpu.VMEM((rows, 4 * HD), BF),
            pltpu.VMEM((2, rows, half), BF),
            pltpu.VMEM((2, dim, half), BF),
            pltpu.VMEM((2, 2, dim, HD), BF),
            pltpu.VMEM((2, 2, dim, HD), BF),
            pltpu.VMEM((2, 2, 2 * HD, half), BF),
            dma((4, 2)),
            dma((4, 2)),
            dma((4,)),
            dma((6,)),
        ],
        compiler_params=pltpu.CompilerParams(
            collective_id=5, has_side_effects=True, vmem_limit_bytes=VMEM_MAX),
        name="ffn_block",
    )(comb, x, dy, w_out, w_gate, w_gate, w_up, w_up, w_down, w_down, gain)


def ring_place(row, n):
    return jnp.where(lax.rem(row, 2) == 0, row // 2, n - 1 - row // 2)


def ring_row(place, n):
    return jnp.where(place < n // 2, 2 * place, 2 * (n - place) - 1)


def split_cols(width, flip):
    tiles = width // HD
    if tiles == 1:
        return ((0, width),)
    first = (tiles + (0 if flip else 1)) // 2 * HD
    return ((0, first), (first, width - first))


def mod(value, n):
    return lax.rem(value + n, n)


def neighbours(n):
    me = ring_place(lax.axis_index("row"), n)
    return me, ring_row(mod(me + 1, n), n), ring_row(mod(me - 1, n), n)


def greet(n, right, left, use_col, use_dp):
    barrier = pltpu.get_barrier_semaphore()
    count = 2
    for target in (right, left):
        pl.semaphore_signal(barrier, inc=1, device_id={"row": target}, device_id_type=MESH)
    if use_col:
        other = 1 - lax.axis_index("col")
        pl.semaphore_signal(barrier, inc=1, device_id={"col": other}, device_id_type=MESH)
        count += 1
    if use_dp:
        twin = 1 - lax.axis_index("dp")
        pl.semaphore_signal(barrier, inc=1, device_id={"dp": twin}, device_id_type=MESH)
        count += 1
    pl.semaphore_wait(barrier, count)


class Gather:
    def __init__(self, n, items, sems):
        self.n = n
        self.items = items
        self.send, self.recv, self.local, self.csend, self.crecv, self.xsend = sems
        self.me, self.right, self.left = neighbours(n)
        self.row = lax.axis_index("row")
        self.other = 1 - lax.axis_index("col")
        self.plane = lax.axis_index("dp")

    def ways(self, m):
        return range(len(split_cols(self.items[m][0].shape[1], m % 2)))

    def hop(self, m, d, s):
        block, whole_ref, base = self.items[m][:3]
        place = mod(self.me - s, self.n) if d == 0 else mod(self.me + s, self.n)
        owner = ring_row(place, self.n)
        start, size = split_cols(block.shape[1], m % 2)[d]
        return start, size, whole_ref.at[owner, :, pl.ds(base + start, size)]

    def ring(self, m, d, s, first=False):
        start, size, spot = self.hop(m, d, s)
        source = self.items[m][0].at[:, pl.ds(start, size)] if first else spot
        return pltpu.make_async_remote_copy(
            src_ref=source, dst_ref=spot, send_sem=self.send.at[m, d, s], recv_sem=self.recv.at[m, d, s],
            device_id={"row": self.right if d == 0 else self.left}, device_id_type=MESH)

    def over(self, m, d, s):
        spot = self.hop(m, d, s + 1)[2]
        return pltpu.make_async_remote_copy(
            src_ref=spot, dst_ref=spot, send_sem=self.xsend.at[m, d, s], recv_sem=self.recv.at[m, d, s],
            device_id={"dp": 1 - self.plane}, device_id_type=MESH)

    def across(self, m, source, spot):
        return pltpu.make_async_remote_copy(
            src_ref=source, dst_ref=spot, send_sem=self.csend.at[m], recv_sem=self.crecv.at[m],
            device_id={"col": self.other}, device_id_type=MESH)

    def keep(self, m):
        block, whole_ref, base = self.items[m][:3]
        return pltpu.make_async_copy(
            block, whole_ref.at[self.row, :, pl.ds(base, block.shape[1])], self.local.at[m])

    def when(self, m, inside, action):
        plane = self.items[m][4]
        if plane is None:
            if inside:
                action()
        else:
            pl.when((self.plane == plane) if inside else (self.plane != plane))(action)

    def begin(self, ms):
        for m in ms:
            def launch(m=m):
                for d in self.ways(m):
                    self.ring(m, d, 0, first=True).start()

            self.when(m, True, launch)
        for m in ms:
            block, whole_ref, base, share = self.items[m][:4]
            self.keep(m).start()
            if share:
                self.across(m, block, whole_ref.at[self.row, :, pl.ds(base, block.shape[1])]).start()

    def hand(self, m, d, s):
        if self.items[m][3]:
            spot = self.hop(m, d, s + 1)[2]
            self.across(m, spot, spot).start()

    def arrive(self, m, s):
        for d in self.ways(m):
            self.over(m, d, s).wait_recv()
            self.hand(m, d, s)

    def advance(self, m, s):
        def inside():
            for d in self.ways(m):
                self.ring(m, d, s).wait_recv()

                @pl.when(s < self.n - 2)
                def on():
                    self.ring(m, d, s + 1).start()

                if self.items[m][4] is not None:
                    self.over(m, d, s).start()
                self.hand(m, d, s)

        def outside():
            @pl.when(s > 0)
            def late():
                self.arrive(m, s - 1)

        self.when(m, True, inside)
        self.when(m, False, outside)

    def finish(self, ms):
        for m in ms:
            self.when(m, False, functools.partial(self.arrive, m, self.n - 2))
        for m in ms:
            block, whole_ref, base, share, plane = self.items[m]
            self.keep(m).wait()
            if share:
                spot = whole_ref.at[:, :, pl.ds(base, block.shape[1])]
                theirs = whole_ref.at[:, :, pl.ds(self.other * block.shape[1], block.shape[1])]
                self.across(m, spot, theirs).wait_recv()
                self.across(m, spot, theirs).wait_send()

            def drain(m=m, plane=plane):
                def sent(s, carry):
                    for d in self.ways(m):
                        self.ring(m, d, s).wait_send()
                        if plane is not None:
                            self.over(m, d, s).wait_send()
                    return carry

                lax.fori_loop(0, self.n - 1, sent, 0)

            self.when(m, True, drain)


def gather_sems(n, count):
    dma = pltpu.SemaphoreType.DMA
    return [dma((count, 2, n - 1))] * 2 + [dma((count,))] * 3 + [dma((count, 2, n - 1))]


def pre_kernel(n, *refs):
    blocks, x_ref = refs[:6], refs[6]
    wide_out, small_out, full_out, normed_out, qkvg_out, gain_a_ref, gain_f_ref = refs[7:14]
    wide, small, pair, normed_v, qkvg_v, xsems, osems = refs[14:21]
    sems = refs[21:]
    core = lax.axis_index("col")
    dim = x_ref.shape[1]
    planes = (0, 1, None, None)
    items = [(blocks[m], wide, m * blocks[m].shape[1], False, planes[m]) for m in range(4)]
    items.append((blocks[4], small, core * HD, True, None))
    items.append((blocks[5], full_out, core * blocks[5].shape[1], True, None))
    g = Gather(n, items, sems)
    greet(n, g.right, g.left, True, True)
    g.begin(range(5))
    mine = pltpu.make_async_copy(x_ref, pair.at[core], xsems.at[0])
    mine.start()
    theirs = pltpu.make_async_remote_copy(
        src_ref=x_ref, dst_ref=pair.at[core], send_sem=xsems.at[1], recv_sem=xsems.at[2],
        device_id={"col": 1 - core}, device_id_type=MESH)
    theirs.start()

    def hops(ms, low, high):
        def step(s, carry):
            for m in ms:
                g.advance(m, s)
            return carry

        lax.fori_loop(low, high, step, 0)

    lag = n // 2 - 1
    hops(range(5), 0, lag)
    g.begin((5,))

    def both(s, carry):
        for m in range(5):
            g.advance(m, s)
        g.advance(5, s - lag)
        return carry

    lax.fori_loop(lag, n - 1, both, 0)
    done = n - 1 - lag
    g.finish(range(5))
    mine.wait()
    theirs.wait()
    copies = [pltpu.make_async_copy(wide, wide_out, osems.at[0]),
              pltpu.make_async_copy(small, small_out, osems.at[1])]
    for copy in copies:
        copy.start()
    gains = jnp.zeros((16, HD), F32)
    for q in range(n):
        for i in range(2):
            gains = gains + small[q, 2 * P_SIZE:, i * HD:(i + 1) * HD].astype(F32)
    tiles = dim // HD
    gain = jnp.concatenate([gains[i:i + 1] for i in range(tiles)], axis=1)
    gain_a_ref[...] = gain
    gain_f_ref[...] = jnp.concatenate([gains[tiles + i:tiles + i + 1] for i in range(tiles)], axis=1)
    chunk = normed_v.shape[1]
    count = normed_v.shape[0]
    per_core = count // 2
    width = qkvg_v.shape[2] // 2
    slots = 2 * count - 1
    for i in range(count):
        rows = slice((i % per_core) * chunk, (i % per_core + 1) * chunk)
        xf = pair[i // per_core, rows, :].astype(F32)
        inv = lax.rsqrt(jnp.mean(xf * xf, axis=1, keepdims=True) + EPS)
        normed_v[i] = (xf * inv * gain).astype(BF)
        copies.append(pltpu.make_async_copy(
            normed_v.at[i], normed_out.at[pl.ds(i * chunk, chunk)], osems.at[2 + i]))
        copies[-1].start()
        for j in range(2):
            cols = slice(j * width, (j + 1) * width)
            weight = wide[:, :, cols].reshape(dim, width)
            qkvg_v[i, :, cols] = nn(normed_v[i], weight).astype(BF)
            u = 2 * i + j
            if u < slots:
                hops((5,), done + u * lag // slots, done + (u + 1) * lag // slots)
        copies.append(pltpu.make_async_copy(
            qkvg_v.at[i], qkvg_out.at[pl.ds(i * chunk, chunk)], osems.at[2 + count + i]))
        copies[-1].start()
    g.finish((5,))
    for copy in copies:
        copy.wait()


def pre(n, blocks, small, w_out, x):
    rows, width = blocks[0].shape
    tokens, dim = x.shape
    count = 2 * tokens // 512
    any_spec = pl.BlockSpec(memory_space=pl.ANY)
    vmem_spec = pl.BlockSpec(memory_space=pltpu.VMEM)
    dma = pltpu.SemaphoreType.DMA
    wide = (n, rows, 4 * width)
    smalls = (n, small.shape[0], 2 * small.shape[1])
    shapes = [wide, smalls, (n, rows, 2 * w_out.shape[1]), (2 * tokens, dim), (2 * tokens, 4 * width)]
    return pl.pallas_call(
        functools.partial(pre_kernel, n),
        in_specs=[vmem_spec] * 7,
        out_specs=[any_spec] * 5 + [vmem_spec] * 2,
        out_shape=[jax.ShapeDtypeStruct(shape, BF) for shape in shapes]
        + [jax.ShapeDtypeStruct((1, dim), F32)] * 2,
        scratch_shapes=[
            pltpu.VMEM(wide, BF),
            pltpu.VMEM(smalls, BF),
            pltpu.VMEM((2,) + x.shape, BF),
            pltpu.VMEM((count, 512, dim), BF),
            pltpu.VMEM((count, 512, 4 * width), BF),
            dma((3,)),
            dma((2 + 2 * count,)),
        ] + gather_sems(n, 6),
        compiler_params=pltpu.CompilerParams(
            collective_id=1, has_side_effects=True, vmem_limit_bytes=VMEM_MAX),
        name="pre",
    )(*blocks, small, w_out, x)


class Scatter:
    def __init__(self, n, items, sems):
        self.n = n
        self.items = items
        self.send, self.recv, self.local, self.sib, self.dsend, self.drecv, self.xsend, self.xrecv = sems
        self.me, self.right, self.left = neighbours(n)
        self.plane = lax.axis_index("dp")
        self.twin = 1 - self.plane

    def ways(self, m):
        return range(len(split_cols(self.items[m][2], m % 2)))

    def loads(self, m):
        ref, base, width, other, own, sib = self.items[m][:6]
        copies = [pltpu.make_async_copy(ref.at[:, :, pl.ds(base, width)], own, self.local.at[m])]
        if other is not None:
            copies.append(pltpu.make_async_copy(other, sib, self.sib.at[m]))
        return copies

    def begin(self, ms):
        for m in ms:
            for copy in self.loads(m):
                copy.start()

    def ready(self, m):
        for copy in self.loads(m):
            copy.wait()

    def part(self, m, d, s):
        place = mod(self.me - 1 - s, self.n) if d == 0 else mod(self.me + 1 + s, self.n)
        start, size = split_cols(self.items[m][2], m % 2)[d]
        return ring_row(mod(place, self.n), self.n), slice(start, start + size)

    def ring(self, m, d, s):
        own, ring = self.items[m][4], self.items[m][6]
        owner, cols = self.part(m, d, s)
        return pltpu.make_async_remote_copy(
            src_ref=own.at[owner, :, cols], dst_ref=ring.at[s, :, cols],
            send_sem=self.send.at[m, d, s], recv_sem=self.recv.at[m, d, s],
            device_id={"row": self.right if d == 0 else self.left}, device_id_type=MESH)

    def plane_of(self, m):
        return self.items[m][10] if len(self.items[m]) > 10 else None

    def inside(self, m, action):
        plane = self.plane_of(m)
        if plane is None:
            action()
        else:
            pl.when(self.plane == plane)(action)

    def over(self, m, d, s):
        own, inbox = self.items[m][4], self.items[m][11]
        owner, cols = self.part(m, d, s)
        return pltpu.make_async_remote_copy(
            src_ref=own.at[owner, :, cols], dst_ref=inbox.at[owner, :, cols],
            send_sem=self.xsend.at[m, d, s], recv_sem=self.xrecv.at[m, d, s],
            device_id={"dp": self.twin}, device_id_type=MESH)

    def send_over(self, m):
        def one(s, carry):
            for d in self.ways(m):
                owner, cols, value = self.total(m, d, s, False, False)
                self.items[m][4][owner, :, cols] = value
                self.over(m, d, s).start()
            return carry

        lax.fori_loop(0, self.n, one, 0)

    def total(self, m, d, s, arrived, dp=True):
        other, own, sib, ring = self.items[m][3:7]
        owner, cols = self.part(m, d, s)
        value = own[owner, :, cols].astype(F32)
        if other is not None:
            value = value + sib[owner, :, cols].astype(F32)
        if dp and self.plane_of(m) is not None:
            self.over(m, d, s).wait_recv()
            value = value + self.items[m][11][owner, :, cols].astype(F32)
        if arrived:
            value = value + ring[s - 1, :, cols].astype(F32)
        return owner, cols, value.astype(own.dtype)

    def launch(self, m):
        for d in self.ways(m):
            if self.items[m][3] is not None:
                owner, cols, value = self.total(m, d, 0, False)
                self.items[m][4][owner, :, cols] = value
            self.ring(m, d, 0).start()

    def give(self, m):
        pl.when(self.plane != self.plane_of(m))(lambda: self.send_over(m))

    def start(self, m):
        if self.plane_of(m) is None:
            self.launch(m)

    def advance(self, m, s):
        def go():
            for d in self.ways(m):
                self.ring(m, d, s - 1).wait_recv()
                owner, cols, value = self.total(m, d, s, True)
                self.items[m][4][owner, :, cols] = value
                self.ring(m, d, s).start()

        self.inside(m, go)

    def swap(self, m):
        low, twin = self.items[m][7:9]
        return pltpu.make_async_remote_copy(
            src_ref=low, dst_ref=twin, send_sem=self.dsend.at[m], recv_sem=self.drecv.at[m],
            device_id={"dp": self.twin}, device_id_type=MESH)

    def settle(self, m):
        def go():
            for d in self.ways(m):
                self.ring(m, d, self.n - 2).wait_recv()
                owner, cols, value = self.total(m, d, self.n - 1, True)
                self.items[m][7][:, cols] = value
            if self.items[m][8] is not None:
                self.swap(m).start()

        self.inside(m, go)

    def finish(self, m):
        low, twin, out = self.items[m][7:10]
        self.swap(m).wait_recv()
        out[...] = low[...].astype(F32) + twin[...].astype(F32)
        self.swap(m).wait_send()
        self.drain(m)

    def drain(self, m):
        def sent(s, carry):
            for d in self.ways(m):
                self.ring(m, d, s).wait_send()
            return carry

        def ring_done():
            lax.fori_loop(0, self.n - 1, sent, 0)

        self.inside(m, ring_done)
        if self.plane_of(m) is not None:
            def given(s, carry):
                for d in self.ways(m):
                    self.over(m, d, s).wait_send()
                return carry

            @pl.when(self.plane != self.plane_of(m))
            def given_done():
                lax.fori_loop(0, self.n, given, 0)


def scatter_sems(n, count, planes=False):
    dma = pltpu.SemaphoreType.DMA
    return [dma((count, 2, n - 1))] * 2 + [dma((count,))] * 4 + [dma((count, 2, n) if planes else (1,))] * 2


def scatter_plan(arrays, swap=True):
    scratch = []
    for array, width, share in arrays:
        n, rows, full = array.shape
        kind = array.dtype
        scratch.append(pltpu.VMEM((n, rows, width), kind))
        scratch.append(pltpu.VMEM((n, rows, width) if share else (1, 16, HD), kind))
        scratch.append(pltpu.VMEM((n - 1, rows, width), kind))
        if swap:
            scratch.append(pltpu.VMEM((rows, width), kind))
            scratch.append(pltpu.VMEM((rows, width), kind))
    return scratch


def post_kernel(n, normed_ref, d_ref, w_ref, x_ref, dmid_ref, gain_ref, small, *refs):
    late = refs[:4]
    own_w = refs[4:8]
    gin_ref = refs[8]
    outs = refs[9:14]
    late_outs = refs[14:18]
    dgain_ref = refs[18]
    turned, back, leave, came, dg_own, dg_sib, small_sib = refs[19:26]
    late_in = refs[26:30]
    scratch = refs[30:55]
    side, late_send, late_recv = refs[55:58]
    sems = refs[58:]
    turn = pl.program_id(0)
    core = lax.axis_index("col")
    other = 1 - core
    rows_all, dim = x_ref.shape
    width = outs[0].shape[1]
    block = outs[0].shape[0]
    items = []
    for m in range(5):
        first, sib = (0, None) if m < 4 else (core * HD, small_sib)
        items.append((None if m < 4 else small, first, outs[m].shape[1], sib)
                     + tuple(scratch[5 * m:5 * m + 5]) + (outs[m],))
    g = Scatter(n, items, sems)
    steps = 2 * rows_all // TILE

    def push(src, dst, at):
        return pltpu.make_async_remote_copy(
            src_ref=src, dst_ref=dst, send_sem=side.at[2 * at], recv_sem=side.at[2 * at + 1],
            device_id={"col": other}, device_id_type=MESH)

    def late_swap(i):
        return pltpu.make_async_remote_copy(
            src_ref=late[i], dst_ref=late_in[i], send_sem=late_send.at[i], recv_sem=late_recv.at[i],
            device_id={"dp": g.twin}, device_id_type=MESH)

    planes = (None, 0, 1, None)

    def late_start(i):
        if planes[i] is None:
            late_swap(i).start()
        else:
            pl.when(g.plane == planes[i])(lambda: late_swap(i).start())

    def late_end(i):
        if planes[i] is None:
            late_swap(i).wait()
            late_outs[i][...] = late[i][...].astype(F32) + late_in[i][...].astype(F32)
        else:
            @pl.when(g.plane == planes[i])
            def given():
                late_swap(i).wait_send()
                late_outs[i][...] = late[i][...].astype(F32)

            @pl.when(g.plane != planes[i])
            def taken():
                late_swap(i).wait_recv()
                late_outs[i][...] = late_in[i][...].astype(F32)

    cross = push(small.at[:, :, pl.ds(other * HD, HD)], small_sib, 0)
    swap_back = push(leave, came, 1)
    swap_gain = push(dg_own, dg_sib, 2)

    @pl.when(turn == 0)
    def first_turn():
        greet(n, g.right, g.left, True, True)
        cross.start()
        for i in range(4):
            late_start(i)
        for i in range(steps):
            rows = slice(i * TILE, (i + 1) * TILE)
            turned[:, rows] = normed_ref[rows, :].T
            back[rows, :] = jnp.zeros((TILE, dim), F32)

    rate = (n + 5) // 7

    def slot(u):
        for m in range(5):
            v = u - 2 * (m % 4)
            if v < 1:
                continue
            low, high = max(1, rate * (v - 1) + 1), min(n - 1, rate * v + 1)
            if low < high:
                def one(s, carry, m=m):
                    g.advance(m, s)
                    return carry

                lax.fori_loop(low, high, one, 0)
            elif rate * (v - 1) + 1 < n - 1 + rate:
                g.settle(m)

    for m in range(4):
        @pl.when(turn == m)
        def this():
            for part in range(2):
                cols = slice(part * (width // 2), (part + 1) * (width // 2))
                grad = nn(turned[...], d_ref[:, cols]).astype(BF)
                for q in range(n):
                    items[m][4][q, :, cols] = grad[q * block:(q + 1) * block]
            g.start(m)
            slot(2 * m)
            if m == 0:
                cross.wait()
                g.begin((4,))
                g.ready(4)
                g.start(4)
            for i in range(steps):
                rows = slice(i * TILE, (i + 1) * TILE)
                back[rows, :] += nt(d_ref[rows, :], w_ref[...])
            slot(2 * m + 1)

    @pl.when(turn == 3)
    def rest():
        theirs = pl.multiple_of(other * rows_all, TILE)
        for i in range(rows_all // TILE):
            rows = slice(i * TILE, (i + 1) * TILE)
            leave[rows, :] = back[pl.ds(theirs + i * TILE, TILE), :].astype(BF)
        swap_back.start()
        slot(8)
        slot(9)
        swap_back.wait()
        mine = pl.multiple_of(core * rows_all, TILE)
        gain = gain_ref[...]
        for i in range(rows_all // TILE):
            rows = slice(i * TILE, (i + 1) * TILE)
            xf = x_ref[rows, :].astype(F32)
            inv = lax.rsqrt(jnp.mean(xf * xf, axis=1, keepdims=True) + EPS)
            weighted = (back[pl.ds(mine + i * TILE, TILE), :] + came[rows, :].astype(F32)) * gain
            inner = jnp.mean(weighted * xf, axis=1, keepdims=True)
            value = dmid_ref[rows, :].astype(F32) + weighted * inv - xf * (inv * inv * inv) * inner
            gin_ref[rows, :] = value.astype(BF)
            if i < 2:
                slot(10 + i)
        for u in range(12, 15):
            slot(u)
        for i in range(4):
            late_end(i)
        total = jnp.zeros((block, 1), F32)
        for m in range(4):
            g.finish(m)
            total = total + jnp.sum(outs[m][...] * own_w[m][...].astype(F32), axis=1, keepdims=True)
        dg_own[...] = jnp.broadcast_to(total, (block, HD))
        swap_gain.start()
        g.finish(4)
        swap_gain.wait()
        dgain_ref[...] = dg_own[...] + dg_sib[...]


def post(n, normed, dqkvg, wide, x, dmid, gain, small, late, own_w):
    total, dim = normed.shape
    width = wide.shape[1] // 4
    rows = x.shape[0]
    block = dim // n
    arrays = [(jax.ShapeDtypeStruct((n, block, width), BF), width, False)] * 4 + [(small, HD, True)]
    any_spec = pl.BlockSpec(memory_space=pl.ANY)
    dma = pltpu.SemaphoreType.DMA
    outs = [((a.shape[1], w), F32) for a, w, share in arrays]
    late_outs = [(a.shape, F32) for a in late]
    shapes = [((rows, dim), BF)] + outs + late_outs + [((block, HD), F32)]
    return pl.pallas_call(
        functools.partial(post_kernel, n),
        grid=(4,),
        in_specs=[
            whole((total, dim)),
            pl.BlockSpec((total, width), lambda t: (0, t)),
            pl.BlockSpec((dim, width), lambda t: (0, t)),
            whole((rows, dim)),
            whole((rows, dim)),
            whole((1, dim)),
            any_spec,
        ] + [whole(a.shape) for a in late] + [whole(a.shape) for a in own_w],
        out_specs=[whole(shape) for shape, kind in shapes],
        out_shape=[jax.ShapeDtypeStruct(shape, kind) for shape, kind in shapes],
        scratch_shapes=[
            pltpu.VMEM((dim, total), BF),
            pltpu.VMEM((total, dim), F32),
            pltpu.VMEM((rows, dim), BF),
            pltpu.VMEM((rows, dim), BF),
            pltpu.VMEM((block, HD), F32),
            pltpu.VMEM((block, HD), F32),
            pltpu.VMEM((n, small.shape[1], HD), F32),
        ]
        + [pltpu.VMEM(a.shape, BF) for a in late]
        + scatter_plan(arrays)
        + [dma((6,)), dma((4,)), dma((4,))]
        + scatter_sems(n, 5),
        compiler_params=pltpu.CompilerParams(
            collective_id=2, has_side_effects=True, vmem_limit_bytes=VMEM_MAX),
        name="post",
    )(normed, dqkvg, wide, x, dmid, gain, small, *late, *own_w)


def local(
    tokens_in,
    grad_out,
    gain_attn,
    gain_ffn,
    w_query,
    w_key,
    w_value,
    w_gate,
    w_out,
    w_ffn_gate,
    w_ffn_up,
    w_ffn_down,
    persist_key,
    persist_value,
    mem_rate,
    mem_momentum,
    mem_forget,
    segment_ids,
    decay_index,
):
    n = lax.axis_size("row")
    core = lax.axis_index("col")
    local_tok, dim = tokens_in.shape
    heads = mem_rate.shape[1]
    width = heads * HD
    piece = gain_attn.shape[0]
    slot = lax.axis_index("row") * 2 + core

    def spread(part):
        return lax.dynamic_update_slice(jnp.zeros((dim,), BF), part, (slot * piece,)).reshape(dim // HD, HD)

    persist = jnp.pad(jnp.concatenate([persist_key, persist_value], axis=0), ((0, 0), (0, HD - piece)))
    small = jnp.concatenate([persist, spread(gain_attn), spread(gain_ffn)], axis=0)
    wide, small_all, full_out, normed, qkvg, gain_a, gain_f = pre(
        n, (w_query, w_key, w_value, w_gate), small, w_out, tokens_in)
    wide = wide.reshape(dim, 4 * width)
    small_all = small_all[:, :2 * P_SIZE].reshape(n, 2 * P_SIZE, 2, HD)[:, :, :, :piece]
    small_all = small_all.transpose(1, 0, 2, 3).reshape(2 * P_SIZE, dim)
    own_small = lax.dynamic_slice_in_dim(small_all, core * width, width, 1)
    pad = ((0, HD - P_SIZE), (0, 0))
    pkey = jnp.pad(own_small[:P_SIZE], pad)
    pvalue = jnp.pad(own_small[P_SIZE:2 * P_SIZE], pad)

    total = qkvg.shape[0]
    spans = total // CH
    span_ids = segment_ids.reshape(total // SEQ, SEQ // CH, CH)
    same = (span_ids[:, 1:, 0] == span_ids[:, :-1, CH - 1]).astype(F32)
    keep = jnp.concatenate([jnp.zeros((total // SEQ, 1), F32), same], axis=1).reshape(spans, 1)
    choose = (decay_index[:, None] == jnp.arange(mem_rate.shape[0])[None, :]).astype(F32)
    tables = jnp.concatenate([mem_rate, mem_momentum, 1.0 - mem_forget], axis=1)
    picked = jnp.dot(choose, tables, precision=HIGH)
    coef = jnp.stack(
        [jnp.broadcast_to(keep, (spans, heads))] + [picked[:, i * heads:(i + 1) * heads] for i in range(3)]
    ).reshape(4, spans * heads)
    segc, segr = segment_ids[:, None], segment_ids[None, :]

    later = (w_ffn_gate, w_ffn_up, w_ffn_down)
    lse, reads, m0, err, comb_tok, full_gate, full_up, full_down = mix_forward(
        n, qkvg, pkey, pvalue, segc, segr, coef, heads, later)
    full_out, full_gate, full_up = [a.reshape(dim, -1) for a in (full_out, full_gate, full_up)]
    full_down = full_down.reshape(-1, dim)
    result, dmid, dgain_f, sums, dcomb, *parts = ffn_block(
        comb_tok, tokens_in, grad_out, full_out, full_gate, full_up, full_down, gain_f)
    parts = [a.reshape(n, a.shape[0] // n, a.shape[1]) for a in parts]
    dqkvg, dpk, dpv, *grads_late = mix_backward(
        n, qkvg, dcomb, pkey, pvalue, segc, segr, coef, lse, reads, m0, err, heads,
        parts[0::2], parts[1::2])

    place = jnp.zeros((2 * P_SIZE, dim), F32)
    place = lax.dynamic_update_slice_in_dim(
        place, jnp.concatenate([dpk[:P_SIZE], dpv[:P_SIZE]], axis=0), core * width, 1)
    packed = jnp.concatenate([place, jnp.zeros((1, dim), F32), dgain_f], axis=0)
    packed = packed.reshape(2 * P_SIZE + 2, n, 2, piece).transpose(1, 0, 2, 3)
    packed = jnp.pad(packed, ((0, 0), (0, 0), (0, 0), (0, HD - piece)))
    stats = jnp.sum(sums.reshape(8, dim // HD, HD), axis=1)[:6]
    stats = jnp.broadcast_to(stats[None, :, None, :], (n, 6, 2, HD))
    packed = jnp.concatenate([packed, stats], axis=1).reshape(n, 2 * P_SIZE + 8, 2 * HD)
    grad_in, *rest = post(
        n, normed, dqkvg, wide, tokens_in, dmid, gain_a, packed, grads_late,
        (w_query, w_key, w_value, w_gate))
    grads, part, dgain_a = rest[:4] + rest[5:9], rest[4], rest[9]
    dgain_a = lax.dynamic_slice_in_dim(dgain_a[:, 0], core * piece, piece, 0) / gain_attn.astype(F32)
    entry_count = local_tok * dim * lax.axis_size("dp") * n * lax.axis_size("col")
    rms_stats = jnp.sqrt(jnp.sum(part[2 * P_SIZE + 2:2 * P_SIZE + 5], axis=1) / entry_count)
    part = part[:, :piece]
    return (
        result,
        grad_in,
        grads[0],
        grads[1],
        grads[2],
        grads[3],
        grads[4],
        grads[5],
        grads[6],
        grads[7],
        dgain_a,
        part[2 * P_SIZE + 1],
        part[:P_SIZE],
        part[P_SIZE:2 * P_SIZE],
        rms_stats,
    )


def solution(mesh):
    tokens = P(("dp", "row", "col"), None)
    vector = P(("row", "col"))
    weight = P("row", "col")
    persist = P(None, ("row", "col"))
    table = P(None, "col")
    ids = P(("dp", "row"))
    return jax.shard_map(
        local,
        mesh=mesh,
        in_specs=(tokens, tokens, vector, vector) + (weight,) * 8 + (persist,) * 2 + (table,) * 3 + (ids,) * 2,
        out_specs=(tokens, tokens) + (weight,) * 8 + (vector,) * 2 + (persist,) * 2 + (P(),),
        check_vma=False,
    )
```

```python
import functools
import jax
import jax.numpy as jnp
from jax import lax
from jax.experimental import pallas as pl
from jax.experimental.pallas import tpu as pltpu
from jax.sharding import PartitionSpec as P

HD = 128
P_SIZE = 16
SEG = 1024
CH = 64
SEQ = 2048
TILE = 256
TPS = SEG // TILE
EPS = 1e-06
NEG = -1e30
SCALE = HD ** (-0.5)
LOG2E = 1.4426950408889634
VMEM_MAX = 60 * 1024 * 1024
F32 = jnp.float32
BF = jnp.bfloat16
HIGH = lax.Precision.HIGHEST
MESH = pl.DeviceIdType.MESH


def nn(a, b):
    return lax.dot_general(a, b, (((1,), (0,)), ((), ())), preferred_element_type=F32)


def nt(a, b):
    return lax.dot_general(a, b, (((1,), (1,)), ((), ())), preferred_element_type=F32)


def tn(a, b):
    return lax.dot_general(a, b, (((0,), (0,)), ((), ())), preferred_element_type=F32)


def token_bias(segc, segr, part):
    width = (part + 1) * TILE
    same = segc == segr[:, :width]
    qpos = lax.broadcasted_iota(jnp.int32, (TILE, width), 0) + part * TILE
    kpos = lax.broadcasted_iota(jnp.int32, (TILE, width), 1)
    return jnp.where(same & (kpos <= qpos), 0.0, NEG).astype(F32)


def mix_forward_tile(heads, part, tile, q_ref, k_ref, v_ref, g_ref, pk_ref, pv_ref, segc_ref,
                     segr_ref, coef_ref, comb_ref, lse_ref, reads_ref, m0_ref, err_ref, mem, mom):
    width = (part + 1) * TILE
    base = part * TILE
    bias = token_bias(segc_ref[...], segr_ref[...], part)
    lane = lax.broadcasted_iota(jnp.int32, (TILE, HD), 1)
    lse_all = jnp.zeros((TILE, HD), F32)
    blocks = TILE // CH
    reads = [[None] * blocks for head in range(heads)]
    per_turn = -(-heads // blocks)
    attention = {}

    def memory(step, head):
        cols = slice(head * HD, (head + 1) * HD)
        rows = slice(step * CH, (step + 1) * CH)
        at = (tile * blocks + step) * heads + head
        keep = coef_ref[0, at]
        rate = coef_ref[1, at]
        moment = coef_ref[2, at]
        stay = coef_ref[3, at]
        start = mem[head] * keep
        low_start = start.astype(BF)
        m0_ref[step, head] = low_start
        key = k_ref[base + step * CH:base + (step + 1) * CH, cols]
        value = v_ref[base + step * CH:base + (step + 1) * CH, cols]
        both = jnp.concatenate([q_ref[rows, cols], key], axis=0)
        got = nn(both, low_start)
        reads[head][step] = got[:CH] * SCALE
        err = (got[CH:] * SCALE - value.astype(F32)).astype(BF)
        err_ref[rows, cols] = err
        speed = (moment * keep) * mom[head] - (rate * SCALE) * tn(key, err)
        mom[head] = speed
        mem[head] = stay * start + speed

    def attend(head):
        cols = slice(head * HD, (head + 1) * HD)
        query = q_ref[:, cols]
        tok = nt(query, k_ref[:width, cols]) * (SCALE * LOG2E) + bias
        per = nt(query, pk_ref[:, cols]) * (SCALE * LOG2E)
        per = jnp.where(lane < P_SIZE, per, NEG)
        top = jnp.maximum(jnp.max(tok, axis=1, keepdims=True), jnp.max(per, axis=1, keepdims=True))
        tok_e = jnp.exp2(tok - top)
        per_e = jnp.exp2(per - top)
        total = jnp.sum(tok_e, axis=1, keepdims=True) + jnp.sum(per_e, axis=1, keepdims=True)
        att = nn(tok_e.astype(BF), v_ref[:width, cols]) + nn(per_e.astype(BF), pv_ref[:, cols])
        attention[head] = att / total
        return top + jnp.log2(total)

    for step in range(blocks):
        for head in range(heads):
            memory(step, head)
        for head in range(step * per_turn, min(heads, (step + 1) * per_turn)):
            lse_all = jnp.where(lane == head, attend(head), lse_all)
    for head in range(heads):
        cols = slice(head * HD, (head + 1) * HD)
        read = jnp.concatenate(reads[head], axis=0)
        reads_ref[:, cols] = read.astype(BF)
        gate = jax.nn.sigmoid(g_ref[:, cols].astype(F32))
        comb_ref[:, cols] = (attention[head] + gate * read).astype(BF)
    lse_ref[...] = lse_all


def hop_bound(turn, tiles, hops):
    return (turn * hops) // tiles


def hop_early(turn, tiles, hops):
    return jnp.minimum(hops, (turn * hops + tiles - 1) // tiles)


def mix_forward_kernel(heads, n, tiles, q_ref, k_ref, v_ref, g_ref, pk_ref, pv_ref, segc_ref,
                       segr_ref, coef_ref, b0, b1, b2, lse_ref, reads_ref, m0_ref, err_ref,
                       comb_out, w0, w1, w2, mem, mom, comb_all, csems, *sems):
    tile = pl.program_id(0)
    core = lax.axis_index("col")
    blocks, wholes = (b0, b1, b2), (w0, w1, w2)
    planes = (0, 1, None)
    items = [(blk, ref, core * blk.shape[1], True, plane)
             for blk, ref, plane in zip(blocks, wholes, planes)]
    g = Gather(n, items, sems)
    each = range(len(items))
    width = heads * HD
    per_core = tiles // 2

    def hops(low, high):
        def one(s, carry):
            for m in each:
                g.advance(m, s)
            return carry

        lax.fori_loop(low, high, one, 0)

    def place(device, index):
        return comb_out.at[pl.ds(index * TILE, TILE), pl.ds(device * width, width)]

    @pl.when(tile == 0)
    def clear():
        greet(n, g.right, g.left, True, True)
        g.begin(each)
        mem[...] = jnp.zeros_like(mem)
        mom[...] = jnp.zeros_like(mom)

    @pl.when(tile > 0)
    def pass_on():
        hops(hop_bound(tile - 1, tiles, n - 1), hop_bound(tile, tiles, n - 1))

    for part in range(TPS):
        @pl.when(lax.rem(tile, TPS) == part)
        def work():
            mix_forward_tile(heads, part, tile, q_ref, k_ref, v_ref, g_ref, pk_ref, pv_ref,
                             segc_ref, segr_ref, coef_ref, comb_all.at[tile], lse_ref, reads_ref,
                             m0_ref, err_ref, mem, mom)

    def stay(index):
        return pltpu.make_async_copy(
            comb_all.at[core * per_core + index], place(core, index), csems.at[0, index])

    def leave(index):
        return pltpu.make_async_remote_copy(
            src_ref=comb_all.at[(1 - core) * per_core + index], dst_ref=place(core, index),
            send_sem=csems.at[1, index], recv_sem=csems.at[2, index],
            device_id={"col": 1 - core}, device_id_type=MESH)

    index = lax.rem(tile, per_core)

    @pl.when(tile // per_core == core)
    def mine():
        stay(index).start()

    @pl.when(tile // per_core != core)
    def theirs():
        leave(index).start()

    @pl.when(tile == tiles - 1)
    def end():
        hops(hop_bound(tiles - 1, tiles, n - 1), n - 1)
        g.finish(each)
        for i in range(per_core):
            stay(i).wait()
            leave(i).wait()


def mix_forward(n, qkvg, pkey, pvalue, segc, segr, coef, heads, blocks):
    total = qkvg.shape[0]
    width = heads * HD
    tiles = total // TILE
    per = TILE // CH
    any_spec = pl.BlockSpec(memory_space=pl.ANY)
    return pl.pallas_call(
        functools.partial(mix_forward_kernel, heads, n, tiles),
        grid=(tiles,),
        in_specs=[
            pl.BlockSpec((TILE, width), lambda t: (t, 0)),
            pl.BlockSpec((SEG, width), lambda t: (t // TPS, 1)),
            pl.BlockSpec((SEG, width), lambda t: (t // TPS, 2)),
            pl.BlockSpec((TILE, width), lambda t: (t, 3)),
            pl.BlockSpec((HD, width), lambda t: (0, 0)),
            pl.BlockSpec((HD, width), lambda t: (0, 0)),
            pl.BlockSpec((TILE, 1), lambda t: (t, 0)),
            pl.BlockSpec((1, SEG), lambda t: (0, t // TPS)),
            pl.BlockSpec(memory_space=pltpu.SMEM),
        ] + [whole(b.shape) for b in blocks],
        out_specs=[
            pl.BlockSpec((TILE, HD), lambda t: (t, 0)),
            pl.BlockSpec((TILE, width), lambda t: (t, 0)),
            pl.BlockSpec((per, heads, HD, HD), lambda t: (t, 0, 0, 0)),
            pl.BlockSpec((TILE, width), lambda t: (t, 0)),
        ] + [any_spec] * 4,
        out_shape=[
            jax.ShapeDtypeStruct((total, HD), F32),
            jax.ShapeDtypeStruct((total, width), BF),
            jax.ShapeDtypeStruct((total // CH, heads, HD, HD), BF),
            jax.ShapeDtypeStruct((total, width), BF),
            jax.ShapeDtypeStruct((total // 2, 2 * width), BF),
        ] + [jax.ShapeDtypeStruct((n, b.shape[0], 2 * b.shape[1]), BF) for b in blocks],
        scratch_shapes=[
            pltpu.VMEM((heads, HD, HD), F32),
            pltpu.VMEM((heads, HD, HD), F32),
            pltpu.VMEM((tiles, TILE, width), BF),
            pltpu.SemaphoreType.DMA((3, tiles // 2)),
        ] + gather_sems(n, 3),
        compiler_params=pltpu.CompilerParams(
            collective_id=3, has_side_effects=True, vmem_limit_bytes=VMEM_MAX),
        name="mix_forward",
    )(qkvg, qkvg, qkvg, qkvg, pkey, pvalue, segc, segr, coef, *blocks)


def mix_backward_tile(heads, part, tile, q_ref, k_ref, v_ref, g_ref, dc_ref, pk_ref, pv_ref,
                      segc_ref, segr_ref, coef_ref, lse_ref, reads_ref, m0_ref, err_ref, dout_ref,
                      dmem, dmom, dk_acc, dv_acc, dpk_acc, dpv_acc):
    width = (part + 1) * TILE
    base = part * TILE
    wide = heads * HD
    bias = token_bias(segc_ref[...], segr_ref[...], part)
    pcol = lax.broadcasted_iota(jnp.int32, (TILE, HD), 1)
    blocks = TILE // CH
    lse_all = lse_ref[...]
    dreads = {}
    mem_q, mem_k, mem_v = {}, {}, {}

    def gates(head):
        cols = slice(head * HD, (head + 1) * HD)
        upf = dc_ref[:, cols].astype(F32)
        gate = jax.nn.sigmoid(g_ref[:, cols].astype(F32))
        dreads[head] = (upf * gate).astype(BF)
        dgate = upf * reads_ref[:, cols].astype(F32) * gate * (1.0 - gate)
        dout_ref[:, 3 * wide + head * HD:3 * wide + (head + 1) * HD] = dgate.astype(BF)

    def memory(step, head):
        cols = slice(head * HD, (head + 1) * HD)
        rows = slice(step * CH, (step + 1) * CH)
        at = (tile * blocks + step) * heads + head
        keep = coef_ref[0, at]
        rate = coef_ref[1, at]
        moment = coef_ref[2, at]
        stay = coef_ref[3, at]
        key = k_ref[base + step * CH:base + (step + 1) * CH, cols]
        start = m0_ref[step, head]
        err = err_ref[rows, cols]
        dstate = dmem[head]
        dspeed = dmom[head] + dstate
        dslope = (dspeed * (-rate)).astype(BF)
        derr = nn(key, dslope) * SCALE
        top = jnp.concatenate([dreads[head][rows], derr.astype(BF)], axis=0)
        both = jnp.concatenate([q_ref[rows, cols], key], axis=0)
        dmem[head] = keep * (stay * dstate + SCALE * tn(both, top))
        dmom[head] = (moment * keep) * dspeed
        back = nt(top, start)
        mem_q[head, step] = back[:CH]
        mem_k[head, step] = back[CH:] + nt(err, dslope)
        mem_v[head, step] = derr

    def attend(head):
        cols = slice(head * HD, (head + 1) * HD)
        query = q_ref[:, cols]
        up = dc_ref[:, cols]
        tok = nt(query, k_ref[:width, cols]) * (SCALE * LOG2E) + bias
        per = nt(query, pk_ref[:, cols]) * (SCALE * LOG2E)
        per = jnp.where(pcol < P_SIZE, per, NEG)
        lse = lse_all[:, head:head + 1]
        tok_p = jnp.exp2(tok - lse)
        per_p = jnp.exp2(per - lse)
        tok_dp = nt(up, v_ref[:width, cols])
        per_dp = nt(up, pv_ref[:, cols])
        inner = jnp.sum(tok_p * tok_dp, axis=1, keepdims=True) + jnp.sum(
            per_p * per_dp, axis=1, keepdims=True)
        tok_ds = (tok_p * (tok_dp - inner)).astype(BF)
        per_ds = (per_p * (per_dp - inner)).astype(BF)
        dquery = nn(tok_ds, k_ref[:width, cols]) + nn(per_ds, pk_ref[:, cols])
        dpk_acc[:, cols] += tn(per_ds, query) * SCALE
        dpv_acc[:, cols] += tn(per_p.astype(BF), up)
        dkey = tn(tok_ds, query)
        dval = tn(tok_p.astype(BF), up)
        own = slice(base, base + TILE)
        if part == TPS - 1:
            dk_acc[:, cols] = dkey
            dv_acc[:, cols] = dval
        else:
            dk_acc[:base + TILE, cols] += dkey
            dv_acc[:base + TILE, cols] += dval
        return dquery

    def finish(head, dquery):
        cols = slice(head * HD, (head + 1) * HD)
        own = slice(base, base + TILE)

        def rows_of(parts):
            return jnp.concatenate([parts[head, step] for step in range(blocks)], axis=0)

        dout_ref[:, cols] = ((dquery + rows_of(mem_q)) * SCALE).astype(BF)
        dout_ref[:, wide + head * HD:wide + (head + 1) * HD] = (
            (dk_acc[own, cols] + rows_of(mem_k)) * SCALE).astype(BF)
        dout_ref[:, 2 * wide + head * HD:2 * wide + (head + 1) * HD] = (
            dv_acc[own, cols] - rows_of(mem_v)).astype(BF)

    for head in range(heads):
        gates(head)
    per_turn = -(-heads // blocks)
    dqueries = {}
    for turn in range(blocks):
        for head in range(heads):
            memory(blocks - 1 - turn, head)
        for head in range(turn * per_turn, min(heads, (turn + 1) * per_turn)):
            dqueries[head] = attend(head)
    for head in range(heads):
        finish(head, dqueries[head])


def mix_backward_kernel(heads, n, tiles, q_ref, k_ref, v_ref, g_ref, dc_ref, pk_ref, pv_ref,
                        segc_ref, segr_ref, coef_ref, lse_ref, reads_ref, m0_ref, err_ref, *refs):
    own_refs, sib_refs = refs[:4], refs[4:8]
    dout_ref, dpk_ref, dpv_ref = refs[8:11]
    outs = refs[11:15]
    dmem, dmom, dk_acc, dv_acc = refs[15:19]
    scratch = refs[19:31]
    planes = (None, 0, 1, None)
    inbox = (None, refs[31], refs[32], None)
    sems = refs[33:]
    turn = pl.program_id(0)
    tile = tiles - 1 - turn
    items = [
        (own_refs[m], 0, outs[m].shape[1], sib_refs[m]) + tuple(scratch[3 * m:3 * m + 3]) + (outs[m], None, None, planes[m], inbox[m])
        for m in range(4)
    ]
    g = Scatter(n, items, sems)
    order = (3, 0, 1, 2)

    def hops(low, high):
        def one(s, carry):
            for m in order:
                g.advance(m, s)
            return carry

        lax.fori_loop(low, high, one, 0)

    @pl.when(turn == 0)
    def clear():
        greet(n, g.right, g.left, False, True)
        g.begin(order)
        dmem[...] = jnp.zeros_like(dmem)
        dmom[...] = jnp.zeros_like(dmom)
        dpk_ref[...] = jnp.zeros_like(dpk_ref)
        dpv_ref[...] = jnp.zeros_like(dpv_ref)
        for m in order:
            g.ready(m)
            g.start(m)
        for m in (1, 2):
            g.give(m)
        for m in (1, 2):
            g.inside(m, functools.partial(g.launch, m))

    @pl.when(turn > 0)
    def pass_on():
        hops(1 + hop_early(turn - 1, tiles - 2, n - 2), 1 + hop_early(turn, tiles - 2, n - 2))

    @pl.when(turn == tiles - 1)
    def settle():
        for m in order:
            g.settle(m)

    for part in range(TPS):
        @pl.when(lax.rem(tile, TPS) == part)
        def work():
            mix_backward_tile(heads, part, tile, q_ref, k_ref, v_ref, g_ref, dc_ref, pk_ref, pv_ref,
                              segc_ref, segr_ref, coef_ref, lse_ref, reads_ref, m0_ref, err_ref,
                              dout_ref, dmem, dmom, dk_acc, dv_acc, dpk_ref, dpv_ref)

    @pl.when(turn == tiles - 1)
    def end():
        for m in order:
            g.drain(m)


def mix_backward(n, qkvg, dcomb, pkey, pvalue, segc, segr, coef, lse, reads, m0, err, heads, owns, sibs):
    total = qkvg.shape[0]
    width = heads * HD
    tiles = total // TILE
    per = TILE // CH
    last = tiles - 1
    any_spec = pl.BlockSpec(memory_space=pl.ANY)
    arrays = [(a, a.shape[2], True) for a in owns]
    return pl.pallas_call(
        functools.partial(mix_backward_kernel, heads, n, tiles),
        grid=(tiles,),
        in_specs=[
            pl.BlockSpec((TILE, width), lambda t: (last - t, 0)),
            pl.BlockSpec((SEG, width), lambda t: ((last - t) // TPS, 1)),
            pl.BlockSpec((SEG, width), lambda t: ((last - t) // TPS, 2)),
            pl.BlockSpec((TILE, width), lambda t: (last - t, 3)),
            pl.BlockSpec((TILE, width), lambda t: (last - t, 0)),
            pl.BlockSpec((HD, width), lambda t: (0, 0)),
            pl.BlockSpec((HD, width), lambda t: (0, 0)),
            pl.BlockSpec((TILE, 1), lambda t: (last - t, 0)),
            pl.BlockSpec((1, SEG), lambda t: (0, (last - t) // TPS)),
            pl.BlockSpec(memory_space=pltpu.SMEM),
            pl.BlockSpec((TILE, HD), lambda t: (last - t, 0)),
            pl.BlockSpec((TILE, width), lambda t: (last - t, 0)),
            pl.BlockSpec((per, heads, HD, HD), lambda t: (last - t, 0, 0, 0)),
            pl.BlockSpec((TILE, width), lambda t: (last - t, 0)),
        ] + [any_spec] * 8,
        out_specs=[
            pl.BlockSpec((TILE, 4 * width), lambda t: (last - t, 0)),
            pl.BlockSpec((HD, width), lambda t: (0, 0)),
            pl.BlockSpec((HD, width), lambda t: (0, 0)),
        ] + [whole((a.shape[1], w)) for a, w, share in arrays],
        out_shape=[
            jax.ShapeDtypeStruct((total, 4 * width), BF),
            jax.ShapeDtypeStruct((HD, width), F32),
            jax.ShapeDtypeStruct((HD, width), F32),
        ] + [jax.ShapeDtypeStruct((a.shape[1], w), BF) for a, w, share in arrays],
        scratch_shapes=[
            pltpu.VMEM((heads, HD, HD), F32),
            pltpu.VMEM((heads, HD, HD), F32),
            pltpu.VMEM((SEG, width), F32),
            pltpu.VMEM((SEG, width), F32),
        ] + scatter_plan(arrays, False) + [pltpu.VMEM(a.shape, BF) for a in owns[1:3]] + scatter_sems(n, 4, True),
        compiler_params=pltpu.CompilerParams(
            collective_id=4, has_side_effects=True, vmem_limit_bytes=VMEM_MAX),
        name="mix_backward",
    )(qkvg, qkvg, qkvg, qkvg, dcomb, pkey, pvalue, segc, segr, coef, lse, reads, m0, err, *owns, *sibs)


def whole(shape):
    return pl.BlockSpec(shape, lambda t: (0,) * len(shape), pipeline_mode=pl.Buffered(1))


def ffn_kernel(tiles, comb_ref, x_ref, dy_ref, wo_ref, wg0, wg1, wu0, wu1, wd0, wd1, gain_ref,
               out_ref, dmid_ref, dgain_ref, sums_ref, dcomb_out, go_own, go_sib, gg_own, gg_sib,
               gu_own, gu_sib, gd_own, gd_sib, n2, n2t, mid, acc_out, acc_dn, hid_all, pair_all,
               dcomb_v, go_v, gbuf, ubuf, dbuf, keep_sem, send_sem, recv_sem, end_sem):
    turn = pl.program_id(0)
    core = lax.axis_index("col")
    other = 1 - core
    rows_all, dim = x_ref.shape
    half = dim // 2
    steps = rows_all // TILE
    ft = 2 * HD
    gain = gain_ref[...]
    slot = lax.rem(turn, 2)
    hidden_half = gg_own.shape[1]

    def push(src, dst, sem, rsem):
        return pltpu.make_async_remote_copy(
            src_ref=src, dst_ref=dst, send_sem=sem, recv_sem=rsem,
            device_id={"col": other}, device_id_type=MESH)

    def moves(t, s):
        stay, leave = [], []
        for i, (buf, own, sib) in enumerate(((gbuf, gg_own, gg_sib), (ubuf, gu_own, gu_sib))):
            cols = pl.ds(pl.multiple_of(t * HD, HD), HD)
            stay.append(pltpu.make_async_copy(
                buf.at[s, core], own.at[:, cols], keep_sem.at[i, s]))
            leave.append(push(buf.at[s, other], sib.at[:, cols], send_sem.at[i, s], recv_sem.at[i]))
        for i in range(2):
            rows = pl.ds(pl.multiple_of(i * hidden_half + t * HD, HD), HD)
            stay.append(pltpu.make_async_copy(
                dbuf.at[s, core, pl.ds(i * HD, HD)], gd_own.at[rows, :], keep_sem.at[2 + i, s]))
            leave.append(push(dbuf.at[s, other, pl.ds(i * HD, HD)], gd_sib.at[rows, :],
                              send_sem.at[2 + i, s], recv_sem.at[2 + i]))
        return stay, leave

    def settle(t, s):
        stay, leave = moves(t, s)
        for copy in stay:
            copy.wait()
        for copy in leave:
            copy.wait_send()

    @pl.when(turn == 0)
    def first():
        barrier = pltpu.get_barrier_semaphore()
        pl.semaphore_signal(barrier, inc=1, device_id={"col": other}, device_id_type=MESH)
        pl.semaphore_wait(barrier, 1)
        sums_ref[...] = jnp.zeros_like(sums_ref)
        dgain_ref[...] = jnp.zeros_like(dgain_ref)
        for i in range(steps):
            rows = slice(i * TILE, (i + 1) * TILE)
            xf = x_ref[rows, :].astype(F32)
            branch = nn(comb_ref[rows, :], wo_ref[...])
            middle = xf + branch
            mid[rows, :] = middle
            acc_out[rows, :] = middle
            inv = lax.rsqrt(jnp.mean(middle * middle, axis=1, keepdims=True) + EPS)
            normed = (middle * inv * gain).astype(BF)
            n2[rows, :] = normed
            n2t[:, rows] = normed.T
            acc_dn[rows, :] = jnp.zeros((TILE, dim), F32)
            sums_ref[0:1, :] += jnp.sum(xf * xf, axis=0, keepdims=True)
            sums_ref[1:2, :] += jnp.sum(branch * branch, axis=0, keepdims=True)

    wd = jnp.concatenate([wd0[...], wd1[...]], axis=0)
    both = jnp.concatenate([wg0[...], wg1[...], wu0[...], wu1[...]], axis=1)
    chunk = 2 * TILE
    for i in range(rows_all // chunk):
        rows = slice(i * chunk, (i + 1) * chunk)
        gateup = nn(n2[rows, :], both)
        gate, up = gateup[:, :ft], gateup[:, ft:]
        dh = nt(dy_ref[rows, :], wd)
        sig = jax.nn.sigmoid(gate)
        silu = gate * sig
        hid = (silu * up).astype(BF)
        dg = (dh * up * (sig * (1.0 + gate * (1.0 - sig)))).astype(BF)
        du = (dh * silu).astype(BF)
        hid_all[rows, :] = hid
        pair = jnp.concatenate([dg, du], axis=1)
        pair_all[rows, :] = pair
        acc_out[rows, :] += nn(hid, wd)
        acc_dn[rows, :] += nt(pair, both)

    @pl.when(turn >= 2)
    def reuse():
        settle(turn - 2, slot)

    down = tn(hid_all[...], dy_ref[...]).astype(BF)
    grads = nn(n2t[...], pair_all[...]).astype(BF)
    for i in range(2):
        gbuf[slot, i] = grads[:, i * HD:(i + 1) * HD]
        ubuf[slot, i] = grads[:, ft + i * HD:ft + (i + 1) * HD]
        dbuf[slot, i] = down[:, i * half:(i + 1) * half]
    stay, leave = moves(turn, slot)
    for copy in stay + leave:
        copy.start()

    @pl.when(turn == tiles - 1)
    def last():
        for i in range(steps):
            rows = slice(i * TILE, (i + 1) * TILE)
            final = acc_out[rows, :]
            out_ref[rows, :] = final.astype(BF)
            sums_ref[2:3, :] += jnp.sum(final * final, axis=0, keepdims=True)
            middle = mid[rows, :]
            inv = lax.rsqrt(jnp.mean(middle * middle, axis=1, keepdims=True) + EPS)
            dnorm = acc_dn[rows, :]
            weighted = dnorm * gain
            inner = jnp.mean(weighted * middle, axis=1, keepdims=True)
            dgain_ref[...] += jnp.sum(dnorm * middle * inv, axis=0, keepdims=True)
            dmid = dy_ref[rows, :].astype(F32) + weighted * inv - middle * (inv * inv * inv) * inner
            low = dmid.astype(BF)
            dmid_ref[rows, :] = low
            dcomb = nt(low, wo_ref[...]).astype(BF)
            dcomb_v[0, rows, :] = dcomb[:, :half]
            dcomb_v[1, rows, :] = dcomb[:, half:]
        home = pl.ds(pl.multiple_of(core * rows_all, TILE), rows_all)
        stay_c = pltpu.make_async_copy(dcomb_v.at[core], dcomb_out.at[home, :], end_sem.at[0])
        leave_c = push(dcomb_v.at[other], dcomb_out.at[home, :], end_sem.at[1], end_sem.at[2])
        stay_c.start()
        leave_c.start()
        for i in range(dim // TILE):
            part = slice(i * TILE, (i + 1) * TILE)
            go = tn(comb_ref[:, part], dmid_ref[...]).astype(BF)
            go_v[0, part, :] = go[:, :half]
            go_v[1, part, :] = go[:, half:]
        stay_o = pltpu.make_async_copy(go_v.at[core], go_own, end_sem.at[3])
        leave_o = push(go_v.at[other], go_sib, end_sem.at[4], end_sem.at[5])
        stay_o.start()
        leave_o.start()
        settle(turn - 1, 1 - slot)
        settle(turn, slot)
        for i, sib in enumerate((gg_sib, gu_sib)):
            push(sib, sib, send_sem.at[i, 0], recv_sem.at[i]).wait_recv()
        for i in range(2):
            part = gd_sib.at[pl.ds(i * hidden_half, hidden_half), :]
            push(part, part, send_sem.at[2 + i, 0], recv_sem.at[2 + i]).wait_recv()
        stay_c.wait()
        stay_o.wait()
        leave_c.wait()
        leave_o.wait()


def ffn_block(comb, x, dy, w_out, w_gate, w_up, w_down, gain):
    rows, dim = x.shape
    hidden = w_gate.shape[1]
    tiles = hidden // (2 * HD)
    full = (rows, dim)
    half = dim // 2
    any_spec = pl.BlockSpec(memory_space=pl.ANY)
    front = pl.BlockSpec((dim, HD), lambda t: (0, t))
    rear = pl.BlockSpec((dim, HD), lambda t: (0, t + tiles))
    dma = pltpu.SemaphoreType.DMA
    return pl.pallas_call(
        functools.partial(ffn_kernel, tiles),
        grid=(tiles,),
        in_specs=[
            whole(full),
            whole(full),
            whole(full),
            whole((dim, dim)),
            front,
            rear,
            front,
            rear,
            pl.BlockSpec((HD, dim), lambda t: (t, 0)),
            pl.BlockSpec((HD, dim), lambda t: (t + tiles, 0)),
            whole((1, dim)),
        ],
        out_specs=[whole(full), whole(full), whole((1, dim)), whole((8, dim))] + [any_spec] * 9,
        out_shape=[
            jax.ShapeDtypeStruct(full, BF),
            jax.ShapeDtypeStruct(full, BF),
            jax.ShapeDtypeStruct((1, dim), F32),
            jax.ShapeDtypeStruct((8, dim), F32),
            jax.ShapeDtypeStruct((2 * rows, half), BF),
        ]
        + [jax.ShapeDtypeStruct((dim, half), BF)] * 2
        + [jax.ShapeDtypeStruct((dim, hidden // 2), BF)] * 4
        + [jax.ShapeDtypeStruct((hidden, half), BF)] * 2,
        scratch_shapes=[
            pltpu.VMEM(full, BF),
            pltpu.VMEM((dim, rows), BF),
            pltpu.VMEM(full, F32),
            pltpu.VMEM(full, F32),
            pltpu.VMEM(full, F32),
            pltpu.VMEM((rows, 2 * HD), BF),
            pltpu.VMEM((rows, 4 * HD), BF),
            pltpu.VMEM((2, rows, half), BF),
            pltpu.VMEM((2, dim, half), BF),
            pltpu.VMEM((2, 2, dim, HD), BF),
            pltpu.VMEM((2, 2, dim, HD), BF),
            pltpu.VMEM((2, 2, 2 * HD, half), BF),
            dma((4, 2)),
            dma((4, 2)),
            dma((4,)),
            dma((6,)),
        ],
        compiler_params=pltpu.CompilerParams(
            collective_id=5, has_side_effects=True, vmem_limit_bytes=VMEM_MAX),
        name="ffn_block",
    )(comb, x, dy, w_out, w_gate, w_gate, w_up, w_up, w_down, w_down, gain)


def ring_place(row, n):
    return jnp.where(lax.rem(row, 2) == 0, row // 2, n - 1 - row // 2)


def ring_row(place, n):
    return jnp.where(place < n // 2, 2 * place, 2 * (n - place) - 1)


def split_cols(width, flip):
    tiles = width // HD
    if tiles == 1:
        return ((0, width),)
    first = (tiles + (0 if flip else 1)) // 2 * HD
    return ((0, first), (first, width - first))


def mod(value, n):
    return lax.rem(value + n, n)


def neighbours(n):
    me = ring_place(lax.axis_index("row"), n)
    return me, ring_row(mod(me + 1, n), n), ring_row(mod(me - 1, n), n)


def greet(n, right, left, use_col, use_dp):
    barrier = pltpu.get_barrier_semaphore()
    count = 2
    for target in (right, left):
        pl.semaphore_signal(barrier, inc=1, device_id={"row": target}, device_id_type=MESH)
    if use_col:
        other = 1 - lax.axis_index("col")
        pl.semaphore_signal(barrier, inc=1, device_id={"col": other}, device_id_type=MESH)
        count += 1
    if use_dp:
        twin = 1 - lax.axis_index("dp")
        pl.semaphore_signal(barrier, inc=1, device_id={"dp": twin}, device_id_type=MESH)
        count += 1
    pl.semaphore_wait(barrier, count)


class Gather:
    def __init__(self, n, items, sems):
        self.n = n
        self.items = items
        self.send, self.recv, self.local, self.csend, self.crecv, self.xsend = sems
        self.me, self.right, self.left = neighbours(n)
        self.row = lax.axis_index("row")
        self.other = 1 - lax.axis_index("col")
        self.plane = lax.axis_index("dp")

    def ways(self, m):
        return range(len(split_cols(self.items[m][0].shape[1], m % 2)))

    def hop(self, m, d, s):
        block, whole_ref, base = self.items[m][:3]
        place = mod(self.me - s, self.n) if d == 0 else mod(self.me + s, self.n)
        owner = ring_row(place, self.n)
        start, size = split_cols(block.shape[1], m % 2)[d]
        return start, size, whole_ref.at[owner, :, pl.ds(base + start, size)]

    def ring(self, m, d, s, first=False):
        start, size, spot = self.hop(m, d, s)
        source = self.items[m][0].at[:, pl.ds(start, size)] if first else spot
        return pltpu.make_async_remote_copy(
            src_ref=source, dst_ref=spot, send_sem=self.send.at[m, d, s], recv_sem=self.recv.at[m, d, s],
            device_id={"row": self.right if d == 0 else self.left}, device_id_type=MESH)

    def over(self, m, d, s):
        spot = self.hop(m, d, s + 1)[2]
        return pltpu.make_async_remote_copy(
            src_ref=spot, dst_ref=spot, send_sem=self.xsend.at[m, d, s], recv_sem=self.recv.at[m, d, s],
            device_id={"dp": 1 - self.plane}, device_id_type=MESH)

    def across(self, m, source, spot):
        return pltpu.make_async_remote_copy(
            src_ref=source, dst_ref=spot, send_sem=self.csend.at[m], recv_sem=self.crecv.at[m],
            device_id={"col": self.other}, device_id_type=MESH)

    def keep(self, m):
        block, whole_ref, base = self.items[m][:3]
        return pltpu.make_async_copy(
            block, whole_ref.at[self.row, :, pl.ds(base, block.shape[1])], self.local.at[m])

    def when(self, m, inside, action):
        plane = self.items[m][4]
        if plane is None:
            if inside:
                action()
        else:
            pl.when((self.plane == plane) if inside else (self.plane != plane))(action)

    def begin(self, ms):
        for m in ms:
            def launch(m=m):
                for d in self.ways(m):
                    self.ring(m, d, 0, first=True).start()

            self.when(m, True, launch)
        for m in ms:
            block, whole_ref, base, share = self.items[m][:4]
            self.keep(m).start()
            if share:
                self.across(m, block, whole_ref.at[self.row, :, pl.ds(base, block.shape[1])]).start()

    def hand(self, m, d, s):
        if self.items[m][3]:
            spot = self.hop(m, d, s + 1)[2]
            self.across(m, spot, spot).start()

    def arrive(self, m, s):
        for d in self.ways(m):
            self.over(m, d, s).wait_recv()
            self.hand(m, d, s)

    def advance(self, m, s):
        def inside():
            for d in self.ways(m):
                self.ring(m, d, s).wait_recv()

                @pl.when(s < self.n - 2)
                def on():
                    self.ring(m, d, s + 1).start()

                if self.items[m][4] is not None:
                    self.over(m, d, s).start()
                self.hand(m, d, s)

        def outside():
            @pl.when(s > 0)
            def late():
                self.arrive(m, s - 1)

        self.when(m, True, inside)
        self.when(m, False, outside)

    def finish(self, ms):
        for m in ms:
            self.when(m, False, functools.partial(self.arrive, m, self.n - 2))
        for m in ms:
            block, whole_ref, base, share, plane = self.items[m]
            self.keep(m).wait()
            if share:
                spot = whole_ref.at[:, :, pl.ds(base, block.shape[1])]
                theirs = whole_ref.at[:, :, pl.ds(self.other * block.shape[1], block.shape[1])]
                self.across(m, spot, theirs).wait_recv()
                self.across(m, spot, theirs).wait_send()

            def drain(m=m, plane=plane):
                def sent(s, carry):
                    for d in self.ways(m):
                        self.ring(m, d, s).wait_send()
                        if plane is not None:
                            self.over(m, d, s).wait_send()
                    return carry

                lax.fori_loop(0, self.n - 1, sent, 0)

            self.when(m, True, drain)


def gather_sems(n, count):
    dma = pltpu.SemaphoreType.DMA
    return [dma((count, 2, n - 1))] * 2 + [dma((count,))] * 3 + [dma((count, 2, n - 1))]


def pre_kernel(n, *refs):
    blocks, x_ref = refs[:6], refs[6]
    wide_out, small_out, full_out, normed_out, qkvg_out, gain_a_ref, gain_f_ref = refs[7:14]
    wide, small, pair, normed_v, turned_v, qkvg_v, xsems, osems = refs[14:22]
    sems = refs[22:]
    core = lax.axis_index("col")
    dim = x_ref.shape[1]
    planes = (0, 1, None, None)
    items = [(blocks[m], wide, m * blocks[m].shape[1], False, planes[m]) for m in range(4)]
    items.append((blocks[4], small, core * HD, True, None))
    items.append((blocks[5], full_out, core * blocks[5].shape[1], True, None))
    g = Gather(n, items, sems)
    greet(n, g.right, g.left, True, True)
    g.begin(range(5))
    mine = pltpu.make_async_copy(x_ref, pair.at[core], xsems.at[0])
    mine.start()
    theirs = pltpu.make_async_remote_copy(
        src_ref=x_ref, dst_ref=pair.at[core], send_sem=xsems.at[1], recv_sem=xsems.at[2],
        device_id={"col": 1 - core}, device_id_type=MESH)
    theirs.start()

    def hops(ms, low, high):
        def step(s, carry):
            for m in ms:
                g.advance(m, s)
            return carry

        lax.fori_loop(low, high, step, 0)

    lag = n // 2 - 1
    hops(range(5), 0, lag)
    g.begin((5,))

    def both(s, carry):
        for m in range(5):
            g.advance(m, s)
        g.advance(5, s - lag)
        return carry

    lax.fori_loop(lag, n - 1, both, 0)
    done = n - 1 - lag
    g.finish(range(5))
    mine.wait()
    theirs.wait()
    copies = [pltpu.make_async_copy(wide, wide_out, osems.at[0]),
              pltpu.make_async_copy(small, small_out, osems.at[1])]
    for copy in copies:
        copy.start()
    gains = jnp.zeros((16, HD), F32)
    for q in range(n):
        for i in range(2):
            gains = gains + small[q, 2 * P_SIZE:, i * HD:(i + 1) * HD].astype(F32)
    tiles = dim // HD
    gain = jnp.concatenate([gains[i:i + 1] for i in range(tiles)], axis=1)
    gain_a_ref[...] = gain
    gain_f_ref[...] = jnp.concatenate([gains[tiles + i:tiles + i + 1] for i in range(tiles)], axis=1)
    chunk = normed_v.shape[1]
    count = normed_v.shape[0]
    per_core = count // 2
    width = qkvg_v.shape[2] // 2
    slots = 2 * count - 1
    for i in range(count):
        rows = slice((i % per_core) * chunk, (i % per_core + 1) * chunk)
        xf = pair[i // per_core, rows, :].astype(F32)
        inv = lax.rsqrt(jnp.mean(xf * xf, axis=1, keepdims=True) + EPS)
        normed_v[i] = (xf * inv * gain).astype(BF)
        for j in range(2):
            cols = slice(j * width, (j + 1) * width)
            weight = wide[:, :, cols].reshape(dim, width)
            qkvg_v[i, :, cols] = nn(normed_v[i], weight).astype(BF)
            u = 2 * i + j
            if u < slots:
                hops((5,), done + u * lag // slots, done + (u + 1) * lag // slots)
        turned_v[i] = normed_v[i].T
        copies.append(pltpu.make_async_copy(
            turned_v.at[i], normed_out.at[:, pl.ds(i * chunk, chunk)], osems.at[2 + i]))
        copies[-1].start()
        copies.append(pltpu.make_async_copy(
            qkvg_v.at[i], qkvg_out.at[pl.ds(i * chunk, chunk)], osems.at[2 + count + i]))
        copies[-1].start()
    g.finish((5,))
    for copy in copies:
        copy.wait()


def pre(n, blocks, small, w_out, x):
    rows, width = blocks[0].shape
    tokens, dim = x.shape
    count = 2 * tokens // 512
    any_spec = pl.BlockSpec(memory_space=pl.ANY)
    vmem_spec = pl.BlockSpec(memory_space=pltpu.VMEM)
    dma = pltpu.SemaphoreType.DMA
    wide = (n, rows, 4 * width)
    smalls = (n, small.shape[0], 2 * small.shape[1])
    shapes = [wide, smalls, (n, rows, 2 * w_out.shape[1]), (dim, 2 * tokens), (2 * tokens, 4 * width)]
    return pl.pallas_call(
        functools.partial(pre_kernel, n),
        in_specs=[vmem_spec] * 7,
        out_specs=[any_spec] * 5 + [vmem_spec] * 2,
        out_shape=[jax.ShapeDtypeStruct(shape, BF) for shape in shapes]
        + [jax.ShapeDtypeStruct((1, dim), F32)] * 2,
        scratch_shapes=[
            pltpu.VMEM(wide, BF),
            pltpu.VMEM(smalls, BF),
            pltpu.VMEM((2,) + x.shape, BF),
            pltpu.VMEM((count, 512, dim), BF),
            pltpu.VMEM((count, dim, 512), BF),
            pltpu.VMEM((count, 512, 4 * width), BF),
            dma((3,)),
            dma((2 + 2 * count,)),
        ] + gather_sems(n, 6),
        compiler_params=pltpu.CompilerParams(
            collective_id=1, has_side_effects=True, vmem_limit_bytes=VMEM_MAX),
        name="pre",
    )(*blocks, small, w_out, x)


class Scatter:
    def __init__(self, n, items, sems):
        self.n = n
        self.items = items
        self.send, self.recv, self.local, self.sib, self.dsend, self.drecv, self.xsend, self.xrecv = sems
        self.me, self.right, self.left = neighbours(n)
        self.plane = lax.axis_index("dp")
        self.twin = 1 - self.plane

    def ways(self, m):
        return range(len(split_cols(self.items[m][2], m % 2)))

    def loads(self, m):
        ref, base, width, other, own, sib = self.items[m][:6]
        copies = [pltpu.make_async_copy(ref.at[:, :, pl.ds(base, width)], own, self.local.at[m])]
        if other is not None:
            copies.append(pltpu.make_async_copy(other, sib, self.sib.at[m]))
        return copies

    def begin(self, ms):
        for m in ms:
            for copy in self.loads(m):
                copy.start()

    def ready(self, m):
        for copy in self.loads(m):
            copy.wait()

    def part(self, m, d, s):
        place = mod(self.me - 1 - s, self.n) if d == 0 else mod(self.me + 1 + s, self.n)
        start, size = split_cols(self.items[m][2], m % 2)[d]
        return ring_row(mod(place, self.n), self.n), slice(start, start + size)

    def ring(self, m, d, s):
        own, ring = self.items[m][4], self.items[m][6]
        owner, cols = self.part(m, d, s)
        return pltpu.make_async_remote_copy(
            src_ref=own.at[owner, :, cols], dst_ref=ring.at[s, :, cols],
            send_sem=self.send.at[m, d, s], recv_sem=self.recv.at[m, d, s],
            device_id={"row": self.right if d == 0 else self.left}, device_id_type=MESH)

    def plane_of(self, m):
        return self.items[m][10] if len(self.items[m]) > 10 else None

    def inside(self, m, action):
        plane = self.plane_of(m)
        if plane is None:
            action()
        else:
            pl.when(self.plane == plane)(action)

    def over(self, m, d, s):
        own, inbox = self.items[m][4], self.items[m][11]
        owner, cols = self.part(m, d, s)
        return pltpu.make_async_remote_copy(
            src_ref=own.at[owner, :, cols], dst_ref=inbox.at[owner, :, cols],
            send_sem=self.xsend.at[m, d, s], recv_sem=self.xrecv.at[m, d, s],
            device_id={"dp": self.twin}, device_id_type=MESH)

    def send_over(self, m):
        def one(s, carry):
            for d in self.ways(m):
                owner, cols, value = self.total(m, d, s, False, False)
                self.items[m][4][owner, :, cols] = value
                self.over(m, d, s).start()
            return carry

        lax.fori_loop(0, self.n, one, 0)

    def total(self, m, d, s, arrived, dp=True):
        other, own, sib, ring = self.items[m][3:7]
        owner, cols = self.part(m, d, s)
        value = own[owner, :, cols].astype(F32)
        if other is not None:
            value = value + sib[owner, :, cols].astype(F32)
        if dp and self.plane_of(m) is not None:
            self.over(m, d, s).wait_recv()
            value = value + self.items[m][11][owner, :, cols].astype(F32)
        if arrived:
            value = value + ring[s - 1, :, cols].astype(F32)
        return owner, cols, value.astype(own.dtype)

    def launch(self, m):
        for d in self.ways(m):
            if self.items[m][3] is not None:
                owner, cols, value = self.total(m, d, 0, False)
                self.items[m][4][owner, :, cols] = value
            self.ring(m, d, 0).start()

    def give(self, m):
        pl.when(self.plane != self.plane_of(m))(lambda: self.send_over(m))

    def start(self, m):
        if self.plane_of(m) is None:
            self.launch(m)

    def advance(self, m, s):
        def go():
            for d in self.ways(m):
                self.ring(m, d, s - 1).wait_recv()
                owner, cols, value = self.total(m, d, s, True)
                self.items[m][4][owner, :, cols] = value
                self.ring(m, d, s).start()

        self.inside(m, go)

    def swap(self, m):
        low, twin = self.items[m][7:9]
        return pltpu.make_async_remote_copy(
            src_ref=low, dst_ref=twin, send_sem=self.dsend.at[m], recv_sem=self.drecv.at[m],
            device_id={"dp": self.twin}, device_id_type=MESH)

    def settle(self, m):
        def go():
            for d in self.ways(m):
                self.ring(m, d, self.n - 2).wait_recv()
                owner, cols, value = self.total(m, d, self.n - 1, True)
                self.items[m][7][:, cols] = value
            if self.items[m][8] is not None:
                self.swap(m).start()

        self.inside(m, go)

    def finish(self, m):
        low, twin, out = self.items[m][7:10]
        self.swap(m).wait_recv()
        out[...] = low[...].astype(F32) + twin[...].astype(F32)
        self.swap(m).wait_send()
        self.drain(m)

    def drain(self, m):
        def sent(s, carry):
            for d in self.ways(m):
                self.ring(m, d, s).wait_send()
            return carry

        def ring_done():
            lax.fori_loop(0, self.n - 1, sent, 0)

        self.inside(m, ring_done)
        if self.plane_of(m) is not None:
            def given(s, carry):
                for d in self.ways(m):
                    self.over(m, d, s).wait_send()
                return carry

            @pl.when(self.plane != self.plane_of(m))
            def given_done():
                lax.fori_loop(0, self.n, given, 0)


def scatter_sems(n, count, planes=False):
    dma = pltpu.SemaphoreType.DMA
    return [dma((count, 2, n - 1))] * 2 + [dma((count,))] * 4 + [dma((count, 2, n) if planes else (1,))] * 2


def scatter_plan(arrays, swap=True):
    scratch = []
    for array, width, share in arrays:
        n, rows, full = array.shape
        kind = array.dtype
        scratch.append(pltpu.VMEM((n, rows, width), kind))
        scratch.append(pltpu.VMEM((n, rows, width) if share else (1, 16, HD), kind))
        scratch.append(pltpu.VMEM((n - 1, rows, width), kind))
        if swap:
            scratch.append(pltpu.VMEM((rows, width), kind))
            scratch.append(pltpu.VMEM((rows, width), kind))
    return scratch


def post_kernel(n, turned, d_ref, w_ref, x_ref, dmid_ref, gain_ref, small, *refs):
    late = refs[:4]
    own_w = refs[4:8]
    gin_ref = refs[8]
    outs = refs[9:14]
    late_outs = refs[14:18]
    dgain_ref = refs[18]
    back, leave, came, dg_own, dg_sib, small_sib = refs[19:25]
    late_in = refs[25:29]
    scratch = refs[29:54]
    side, late_send, late_recv = refs[54:57]
    sems = refs[57:]
    turn = pl.program_id(0)
    core = lax.axis_index("col")
    other = 1 - core
    rows_all, dim = x_ref.shape
    width = outs[0].shape[1]
    block = outs[0].shape[0]
    items = []
    for m in range(5):
        first, sib = (0, None) if m < 4 else (core * HD, small_sib)
        items.append((None if m < 4 else small, first, outs[m].shape[1], sib)
                     + tuple(scratch[5 * m:5 * m + 5]) + (outs[m],))
    g = Scatter(n, items, sems)
    steps = 2 * rows_all // TILE

    def push(src, dst, at):
        return pltpu.make_async_remote_copy(
            src_ref=src, dst_ref=dst, send_sem=side.at[2 * at], recv_sem=side.at[2 * at + 1],
            device_id={"col": other}, device_id_type=MESH)

    def late_swap(i):
        return pltpu.make_async_remote_copy(
            src_ref=late[i], dst_ref=late_in[i], send_sem=late_send.at[i], recv_sem=late_recv.at[i],
            device_id={"dp": g.twin}, device_id_type=MESH)

    planes = (None, 0, 1, None)

    def late_start(i):
        if planes[i] is None:
            late_swap(i).start()
        else:
            pl.when(g.plane == planes[i])(lambda: late_swap(i).start())

    def late_end(i):
        if planes[i] is None:
            late_swap(i).wait()
            late_outs[i][...] = late[i][...].astype(F32) + late_in[i][...].astype(F32)
        else:
            @pl.when(g.plane == planes[i])
            def given():
                late_swap(i).wait_send()
                late_outs[i][...] = late[i][...].astype(F32)

            @pl.when(g.plane != planes[i])
            def taken():
                late_swap(i).wait_recv()
                late_outs[i][...] = late_in[i][...].astype(F32)

    cross = push(small.at[:, :, pl.ds(other * HD, HD)], small_sib, 0)
    swap_back = push(leave, came, 1)
    swap_gain = push(dg_own, dg_sib, 2)

    @pl.when(turn == 0)
    def first_turn():
        greet(n, g.right, g.left, True, True)
        cross.start()
        for i in range(4):
            late_start(i)

    rate = (n + 5) // 7

    def slot(u):
        for m in range(5):
            v = u - 2 * (m % 4)
            if v < 1:
                continue
            low, high = max(1, rate * (v - 1) + 1), min(n - 1, rate * v + 1)
            if low < high:
                def one(s, carry, m=m):
                    g.advance(m, s)
                    return carry

                lax.fori_loop(low, high, one, 0)
            elif rate * (v - 1) + 1 < n - 1 + rate:
                g.settle(m)

    for m in range(4):
        @pl.when(turn == m)
        def this():
            for part in range(2):
                cols = slice(part * (width // 2), (part + 1) * (width // 2))
                grad = nn(turned[...], d_ref[:, cols]).astype(BF)
                for q in range(n):
                    items[m][4][q, :, cols] = grad[q * block:(q + 1) * block]
            g.start(m)
            slot(2 * m)
            if m == 0:
                cross.wait()
                g.begin((4,))
                g.ready(4)
                g.start(4)
            for i in range(steps // 2):
                rows = slice(2 * i * TILE, 2 * (i + 1) * TILE)
                if m == 0:
                    back[rows, :] = nt(d_ref[rows, :], w_ref[...])
                else:
                    back[rows, :] += nt(d_ref[rows, :], w_ref[...])
            slot(2 * m + 1)

    @pl.when(turn == 3)
    def rest():
        theirs = pl.multiple_of(other * rows_all, TILE)
        for i in range(rows_all // TILE):
            rows = slice(i * TILE, (i + 1) * TILE)
            leave[rows, :] = back[pl.ds(theirs + i * TILE, TILE), :].astype(BF)
        swap_back.start()
        slot(8)
        slot(9)
        swap_back.wait()
        mine = pl.multiple_of(core * rows_all, TILE)
        gain = gain_ref[...]
        for i in range(rows_all // TILE):
            rows = slice(i * TILE, (i + 1) * TILE)
            xf = x_ref[rows, :].astype(F32)
            inv = lax.rsqrt(jnp.mean(xf * xf, axis=1, keepdims=True) + EPS)
            weighted = (back[pl.ds(mine + i * TILE, TILE), :] + came[rows, :].astype(F32)) * gain
            inner = jnp.mean(weighted * xf, axis=1, keepdims=True)
            value = dmid_ref[rows, :].astype(F32) + weighted * inv - xf * (inv * inv * inv) * inner
            gin_ref[rows, :] = value.astype(BF)
            if i < 2:
                slot(10 + i)
        for u in range(12, 15):
            slot(u)
        for i in range(4):
            late_end(i)
        total = jnp.zeros((block, 1), F32)
        for m in range(4):
            g.finish(m)
            total = total + jnp.sum(outs[m][...] * own_w[m][...].astype(F32), axis=1, keepdims=True)
        dg_own[...] = jnp.broadcast_to(total, (block, HD))
        swap_gain.start()
        g.finish(4)
        swap_gain.wait()
        dgain_ref[...] = dg_own[...] + dg_sib[...]


def post(n, normed, dqkvg, wide, x, dmid, gain, small, late, own_w):
    dim, total = normed.shape
    width = wide.shape[1] // 4
    rows = x.shape[0]
    block = dim // n
    arrays = [(jax.ShapeDtypeStruct((n, block, width), BF), width, False)] * 4 + [(small, HD, True)]
    any_spec = pl.BlockSpec(memory_space=pl.ANY)
    dma = pltpu.SemaphoreType.DMA
    outs = [((a.shape[1], w), F32) for a, w, share in arrays]
    late_outs = [(a.shape, F32) for a in late]
    shapes = [((rows, dim), BF)] + outs + late_outs + [((block, HD), F32)]
    return pl.pallas_call(
        functools.partial(post_kernel, n),
        grid=(4,),
        in_specs=[
            whole((dim, total)),
            pl.BlockSpec((total, width), lambda t: (0, t)),
            pl.BlockSpec((dim, width), lambda t: (0, t)),
            whole((rows, dim)),
            whole((rows, dim)),
            whole((1, dim)),
            any_spec,
        ] + [whole(a.shape) for a in late] + [whole(a.shape) for a in own_w],
        out_specs=[whole(shape) for shape, kind in shapes],
        out_shape=[jax.ShapeDtypeStruct(shape, kind) for shape, kind in shapes],
        scratch_shapes=[
            pltpu.VMEM((total, dim), F32),
            pltpu.VMEM((rows, dim), BF),
            pltpu.VMEM((rows, dim), BF),
            pltpu.VMEM((block, HD), F32),
            pltpu.VMEM((block, HD), F32),
            pltpu.VMEM((n, small.shape[1], HD), F32),
        ]
        + [pltpu.VMEM(a.shape, BF) for a in late]
        + scatter_plan(arrays)
        + [dma((6,)), dma((4,)), dma((4,))]
        + scatter_sems(n, 5),
        compiler_params=pltpu.CompilerParams(
            collective_id=2, has_side_effects=True, vmem_limit_bytes=VMEM_MAX),
        name="post",
    )(normed, dqkvg, wide, x, dmid, gain, small, *late, *own_w)


def local(
    tokens_in,
    grad_out,
    gain_attn,
    gain_ffn,
    w_query,
    w_key,
    w_value,
    w_gate,
    w_out,
    w_ffn_gate,
    w_ffn_up,
    w_ffn_down,
    persist_key,
    persist_value,
    mem_rate,
    mem_momentum,
    mem_forget,
    segment_ids,
    decay_index,
):
    n = lax.axis_size("row")
    core = lax.axis_index("col")
    local_tok, dim = tokens_in.shape
    heads = mem_rate.shape[1]
    width = heads * HD
    piece = gain_attn.shape[0]
    slot = lax.axis_index("row") * 2 + core

    def spread(part):
        return lax.dynamic_update_slice(jnp.zeros((dim,), BF), part, (slot * piece,)).reshape(dim // HD, HD)

    persist = jnp.pad(jnp.concatenate([persist_key, persist_value], axis=0), ((0, 0), (0, HD - piece)))
    small = jnp.concatenate([persist, spread(gain_attn), spread(gain_ffn)], axis=0)
    wide, small_all, full_out, normed, qkvg, gain_a, gain_f = pre(
        n, (w_query, w_key, w_value, w_gate), small, w_out, tokens_in)
    wide = wide.reshape(dim, 4 * width)
    small_all = small_all[:, :2 * P_SIZE].reshape(n, 2 * P_SIZE, 2, HD)[:, :, :, :piece]
    small_all = small_all.transpose(1, 0, 2, 3).reshape(2 * P_SIZE, dim)
    own_small = lax.dynamic_slice_in_dim(small_all, core * width, width, 1)
    pad = ((0, HD - P_SIZE), (0, 0))
    pkey = jnp.pad(own_small[:P_SIZE], pad)
    pvalue = jnp.pad(own_small[P_SIZE:2 * P_SIZE], pad)

    total = qkvg.shape[0]
    spans = total // CH
    span_ids = segment_ids.reshape(total // SEQ, SEQ // CH, CH)
    same = (span_ids[:, 1:, 0] == span_ids[:, :-1, CH - 1]).astype(F32)
    keep = jnp.concatenate([jnp.zeros((total // SEQ, 1), F32), same], axis=1).reshape(spans, 1)
    choose = (decay_index[:, None] == jnp.arange(mem_rate.shape[0])[None, :]).astype(F32)
    tables = jnp.concatenate([mem_rate, mem_momentum, 1.0 - mem_forget], axis=1)
    picked = jnp.dot(choose, tables, precision=HIGH)
    coef = jnp.stack(
        [jnp.broadcast_to(keep, (spans, heads))] + [picked[:, i * heads:(i + 1) * heads] for i in range(3)]
    ).reshape(4, spans * heads)
    segc, segr = segment_ids[:, None], segment_ids[None, :]

    later = (w_ffn_gate, w_ffn_up, w_ffn_down)
    lse, reads, m0, err, comb_tok, full_gate, full_up, full_down = mix_forward(
        n, qkvg, pkey, pvalue, segc, segr, coef, heads, later)
    full_out, full_gate, full_up = [a.reshape(dim, -1) for a in (full_out, full_gate, full_up)]
    full_down = full_down.reshape(-1, dim)
    result, dmid, dgain_f, sums, dcomb, *parts = ffn_block(
        comb_tok, tokens_in, grad_out, full_out, full_gate, full_up, full_down, gain_f)
    parts = [a.reshape(n, a.shape[0] // n, a.shape[1]) for a in parts]
    dqkvg, dpk, dpv, *grads_late = mix_backward(
        n, qkvg, dcomb, pkey, pvalue, segc, segr, coef, lse, reads, m0, err, heads,
        parts[0::2], parts[1::2])

    place = jnp.zeros((2 * P_SIZE, dim), F32)
    place = lax.dynamic_update_slice_in_dim(
        place, jnp.concatenate([dpk[:P_SIZE], dpv[:P_SIZE]], axis=0), core * width, 1)
    packed = jnp.concatenate([place, jnp.zeros((1, dim), F32), dgain_f], axis=0)
    packed = packed.reshape(2 * P_SIZE + 2, n, 2, piece).transpose(1, 0, 2, 3)
    packed = jnp.pad(packed, ((0, 0), (0, 0), (0, 0), (0, HD - piece)))
    stats = jnp.sum(sums.reshape(8, dim // HD, HD), axis=1)[:6]
    stats = jnp.broadcast_to(stats[None, :, None, :], (n, 6, 2, HD))
    packed = jnp.concatenate([packed, stats], axis=1).reshape(n, 2 * P_SIZE + 8, 2 * HD)
    grad_in, *rest = post(
        n, normed, dqkvg, wide, tokens_in, dmid, gain_a, packed, grads_late,
        (w_query, w_key, w_value, w_gate))
    grads, part, dgain_a = rest[:4] + rest[5:9], rest[4], rest[9]
    dgain_a = lax.dynamic_slice_in_dim(dgain_a[:, 0], core * piece, piece, 0) / gain_attn.astype(F32)
    entry_count = local_tok * dim * lax.axis_size("dp") * n * lax.axis_size("col")
    rms_stats = jnp.sqrt(jnp.sum(part[2 * P_SIZE + 2:2 * P_SIZE + 5], axis=1) / entry_count)
    part = part[:, :piece]
    return (
        result,
        grad_in,
        grads[0],
        grads[1],
        grads[2],
        grads[3],
        grads[4],
        grads[5],
        grads[6],
        grads[7],
        dgain_a,
        part[2 * P_SIZE + 1],
        part[:P_SIZE],
        part[P_SIZE:2 * P_SIZE],
        rms_stats,
    )


def solution(mesh):
    tokens = P(("dp", "row", "col"), None)
    vector = P(("row", "col"))
    weight = P("row", "col")
    persist = P(None, ("row", "col"))
    table = P(None, "col")
    ids = P(("dp", "row"))
    return jax.shard_map(
        local,
        mesh=mesh,
        in_specs=(tokens, tokens, vector, vector) + (weight,) * 8 + (persist,) * 2 + (table,) * 3 + (ids,) * 2,
        out_specs=(tokens, tokens) + (weight,) * 8 + (vector,) * 2 + (persist,) * 2 + (P(),),
        check_vma=False,
    )
```

```python
import functools
import jax
import jax.numpy as jnp
from jax import lax
from jax.experimental import pallas as pl
from jax.experimental.pallas import tpu as pltpu
from jax.sharding import PartitionSpec as P

HD = 128
P_SIZE = 16
SEG = 1024
CH = 64
SEQ = 2048
TILE = 256
TPS = SEG // TILE
EPS = 1e-06
NEG = -1e30
SCALE = HD ** (-0.5)
LOG2E = 1.4426950408889634
VMEM_MAX = 60 * 1024 * 1024
F32 = jnp.float32
BF = jnp.bfloat16
HIGH = lax.Precision.HIGHEST
MESH = pl.DeviceIdType.MESH


def nn(a, b):
    return lax.dot_general(a, b, (((1,), (0,)), ((), ())), preferred_element_type=F32)


def nt(a, b):
    return lax.dot_general(a, b, (((1,), (1,)), ((), ())), preferred_element_type=F32)


def tn(a, b):
    return lax.dot_general(a, b, (((0,), (0,)), ((), ())), preferred_element_type=F32)


def token_bias(segc, segr, part):
    width = (part + 1) * TILE
    same = segc == segr[:, :width]
    qpos = lax.broadcasted_iota(jnp.int32, (TILE, width), 0) + part * TILE
    kpos = lax.broadcasted_iota(jnp.int32, (TILE, width), 1)
    return jnp.where(same & (kpos <= qpos), 0.0, NEG).astype(F32)


def mix_forward_tile(heads, part, tile, q_ref, k_ref, v_ref, g_ref, pk_ref, pv_ref, segc_ref,
                     segr_ref, coef_ref, comb_ref, lse_ref, reads_ref, m0_ref, err_ref, mem, mom):
    width = (part + 1) * TILE
    base = part * TILE
    bias = token_bias(segc_ref[...], segr_ref[...], part)
    lane = lax.broadcasted_iota(jnp.int32, (TILE, HD), 1)
    lse_all = jnp.zeros((TILE, HD), F32)
    blocks = TILE // CH
    reads = [[None] * blocks for head in range(heads)]
    per_turn = -(-heads // blocks)
    attention = {}

    def memory(step, head):
        cols = slice(head * HD, (head + 1) * HD)
        rows = slice(step * CH, (step + 1) * CH)
        at = (tile * blocks + step) * heads + head
        keep = coef_ref[0, at]
        rate = coef_ref[1, at]
        moment = coef_ref[2, at]
        stay = coef_ref[3, at]
        start = mem[head] * keep
        low_start = start.astype(BF)
        m0_ref[step, head] = low_start
        key = k_ref[base + step * CH:base + (step + 1) * CH, cols]
        value = v_ref[base + step * CH:base + (step + 1) * CH, cols]
        both = jnp.concatenate([q_ref[rows, cols], key], axis=0)
        got = nn(both, low_start)
        reads[head][step] = got[:CH] * SCALE
        err = (got[CH:] * SCALE - value.astype(F32)).astype(BF)
        err_ref[rows, cols] = err
        speed = (moment * keep) * mom[head] - (rate * SCALE) * tn(key, err)
        mom[head] = speed
        mem[head] = stay * start + speed

    def attend(head):
        cols = slice(head * HD, (head + 1) * HD)
        query = q_ref[:, cols]
        tok = nt(query, k_ref[:width, cols]) * (SCALE * LOG2E) + bias
        per = nt(query, pk_ref[:, cols]) * (SCALE * LOG2E)
        per = jnp.where(lane < P_SIZE, per, NEG)
        top = jnp.maximum(jnp.max(tok, axis=1, keepdims=True), jnp.max(per, axis=1, keepdims=True))
        tok_e = jnp.exp2(tok - top)
        per_e = jnp.exp2(per - top)
        total = jnp.sum(tok_e, axis=1, keepdims=True) + jnp.sum(per_e, axis=1, keepdims=True)
        att = nn(tok_e.astype(BF), v_ref[:width, cols]) + nn(per_e.astype(BF), pv_ref[:, cols])
        attention[head] = att / total
        return top + jnp.log2(total)

    for step in range(blocks):
        for head in range(heads):
            memory(step, head)
        for head in range(step * per_turn, min(heads, (step + 1) * per_turn)):
            lse_all = jnp.where(lane == head, attend(head), lse_all)
    for head in range(heads):
        cols = slice(head * HD, (head + 1) * HD)
        read = jnp.concatenate(reads[head], axis=0)
        reads_ref[:, cols] = read.astype(BF)
        gate = jax.nn.sigmoid(g_ref[:, cols].astype(F32))
        comb_ref[:, cols] = (attention[head] + gate * read).astype(BF)
    lse_ref[...] = lse_all


def hop_bound(turn, tiles, hops):
    return (turn * hops) // tiles


def hop_early(turn, tiles, hops):
    return jnp.minimum(hops, (turn * hops + tiles - 1) // tiles)


def mix_forward_kernel(heads, n, tiles, q_ref, k_ref, v_ref, g_ref, pk_ref, pv_ref, segc_ref,
                       segr_ref, coef_ref, b0, b1, b2, lse_ref, reads_ref, m0_ref, err_ref,
                       comb_out, w0, w1, w2, mem, mom, comb_all, csems, *sems):
    tile = pl.program_id(0)
    core = lax.axis_index("col")
    blocks, wholes = (b0, b1, b2), (w0, w1, w2)
    planes = (0, 1, None)
    items = [(blk, ref, core * blk.shape[1], True, plane)
             for blk, ref, plane in zip(blocks, wholes, planes)]
    g = Gather(n, items, sems)
    each = range(len(items))
    width = heads * HD
    per_core = tiles // 2

    def hops(low, high):
        def one(s, carry):
            for m in each:
                g.advance(m, s)
            return carry

        lax.fori_loop(low, high, one, 0)

    def place(device, index):
        return comb_out.at[pl.ds(index * TILE, TILE), pl.ds(device * width, width)]

    @pl.when(tile == 0)
    def clear():
        greet(n, g.right, g.left, True, True)
        g.begin(each)
        mem[...] = jnp.zeros_like(mem)
        mom[...] = jnp.zeros_like(mom)

    @pl.when(tile > 0)
    def pass_on():
        hops(hop_bound(tile - 1, tiles, n - 1), hop_bound(tile, tiles, n - 1))

    for part in range(TPS):
        @pl.when(lax.rem(tile, TPS) == part)
        def work():
            mix_forward_tile(heads, part, tile, q_ref, k_ref, v_ref, g_ref, pk_ref, pv_ref,
                             segc_ref, segr_ref, coef_ref, comb_all.at[tile], lse_ref, reads_ref,
                             m0_ref, err_ref, mem, mom)

    def stay(index):
        return pltpu.make_async_copy(
            comb_all.at[core * per_core + index], place(core, index), csems.at[0, index])

    def leave(index):
        return pltpu.make_async_remote_copy(
            src_ref=comb_all.at[(1 - core) * per_core + index], dst_ref=place(core, index),
            send_sem=csems.at[1, index], recv_sem=csems.at[2, index],
            device_id={"col": 1 - core}, device_id_type=MESH)

    index = lax.rem(tile, per_core)

    @pl.when(tile // per_core == core)
    def mine():
        stay(index).start()

    @pl.when(tile // per_core != core)
    def theirs():
        leave(index).start()

    @pl.when(tile == tiles - 1)
    def end():
        hops(hop_bound(tiles - 1, tiles, n - 1), n - 1)
        g.finish(each)
        for i in range(per_core):
            stay(i).wait()
            leave(i).wait()


def mix_forward(n, qkvg, pkey, pvalue, segc, segr, coef, heads, blocks):
    total = qkvg.shape[0]
    width = heads * HD
    tiles = total // TILE
    per = TILE // CH
    any_spec = pl.BlockSpec(memory_space=pl.ANY)
    return pl.pallas_call(
        functools.partial(mix_forward_kernel, heads, n, tiles),
        grid=(tiles,),
        in_specs=[
            pl.BlockSpec((TILE, width), lambda t: (t, 0)),
            pl.BlockSpec((SEG, width), lambda t: (t // TPS, 1)),
            pl.BlockSpec((SEG, width), lambda t: (t // TPS, 2)),
            pl.BlockSpec((TILE, width), lambda t: (t, 3)),
            pl.BlockSpec((HD, width), lambda t: (0, 0)),
            pl.BlockSpec((HD, width), lambda t: (0, 0)),
            pl.BlockSpec((TILE, 1), lambda t: (t, 0)),
            pl.BlockSpec((1, SEG), lambda t: (0, t // TPS)),
            pl.BlockSpec(memory_space=pltpu.SMEM),
        ] + [whole(b.shape) for b in blocks],
        out_specs=[
            pl.BlockSpec((TILE, HD), lambda t: (t, 0)),
            pl.BlockSpec((TILE, width), lambda t: (t, 0)),
            pl.BlockSpec((per, heads, HD, HD), lambda t: (t, 0, 0, 0)),
            pl.BlockSpec((TILE, width), lambda t: (t, 0)),
        ] + [any_spec] * 4,
        out_shape=[
            jax.ShapeDtypeStruct((total, HD), F32),
            jax.ShapeDtypeStruct((total, width), BF),
            jax.ShapeDtypeStruct((total // CH, heads, HD, HD), BF),
            jax.ShapeDtypeStruct((total, width), BF),
            jax.ShapeDtypeStruct((total // 2, 2 * width), BF),
        ] + [jax.ShapeDtypeStruct((n, b.shape[0], 2 * b.shape[1]), BF) for b in blocks],
        scratch_shapes=[
            pltpu.VMEM((heads, HD, HD), F32),
            pltpu.VMEM((heads, HD, HD), F32),
            pltpu.VMEM((tiles, TILE, width), BF),
            pltpu.SemaphoreType.DMA((3, tiles // 2)),
        ] + gather_sems(n, 3),
        compiler_params=pltpu.CompilerParams(
            collective_id=3, has_side_effects=True, vmem_limit_bytes=VMEM_MAX),
        name="mix_forward",
    )(qkvg, qkvg, qkvg, qkvg, pkey, pvalue, segc, segr, coef, *blocks)


def mix_backward_tile(heads, part, tile, q_ref, k_ref, v_ref, g_ref, dc_ref, pk_ref, pv_ref,
                      segc_ref, segr_ref, coef_ref, lse_ref, reads_ref, m0_ref, err_ref, dout_ref,
                      dmem, dmom, dk_acc, dv_acc, dpk_acc, dpv_acc):
    width = (part + 1) * TILE
    base = part * TILE
    wide = heads * HD
    bias = token_bias(segc_ref[...], segr_ref[...], part)
    pcol = lax.broadcasted_iota(jnp.int32, (TILE, HD), 1)
    blocks = TILE // CH
    lse_all = lse_ref[...]
    dreads = {}
    mem_q, mem_k, mem_v = {}, {}, {}

    def gates(head):
        cols = slice(head * HD, (head + 1) * HD)
        upf = dc_ref[:, cols].astype(F32)
        gate = jax.nn.sigmoid(g_ref[:, cols].astype(F32))
        dreads[head] = (upf * gate).astype(BF)
        dgate = upf * reads_ref[:, cols].astype(F32) * gate * (1.0 - gate)
        dout_ref[:, 3 * wide + head * HD:3 * wide + (head + 1) * HD] = dgate.astype(BF)

    def memory(step, head):
        cols = slice(head * HD, (head + 1) * HD)
        rows = slice(step * CH, (step + 1) * CH)
        at = (tile * blocks + step) * heads + head
        keep = coef_ref[0, at]
        rate = coef_ref[1, at]
        moment = coef_ref[2, at]
        stay = coef_ref[3, at]
        key = k_ref[base + step * CH:base + (step + 1) * CH, cols]
        start = m0_ref[step, head]
        err = err_ref[rows, cols]
        dstate = dmem[head]
        dspeed = dmom[head] + dstate
        dslope = (dspeed * (-rate)).astype(BF)
        derr = nn(key, dslope) * SCALE
        top = jnp.concatenate([dreads[head][rows], derr.astype(BF)], axis=0)
        both = jnp.concatenate([q_ref[rows, cols], key], axis=0)
        dmem[head] = keep * (stay * dstate + SCALE * tn(both, top))
        dmom[head] = (moment * keep) * dspeed
        back = nt(top, start)
        mem_q[head, step] = back[:CH]
        mem_k[head, step] = back[CH:] + nt(err, dslope)
        mem_v[head, step] = derr

    def attend(head):
        cols = slice(head * HD, (head + 1) * HD)
        query = q_ref[:, cols]
        up = dc_ref[:, cols]
        tok = nt(query, k_ref[:width, cols]) * (SCALE * LOG2E) + bias
        per = nt(query, pk_ref[:, cols]) * (SCALE * LOG2E)
        per = jnp.where(pcol < P_SIZE, per, NEG)
        lse = lse_all[:, head:head + 1]
        tok_p = jnp.exp2(tok - lse)
        per_p = jnp.exp2(per - lse)
        tok_dp = nt(up, v_ref[:width, cols])
        per_dp = nt(up, pv_ref[:, cols])
        inner = jnp.sum(tok_p * tok_dp, axis=1, keepdims=True) + jnp.sum(
            per_p * per_dp, axis=1, keepdims=True)
        tok_ds = (tok_p * (tok_dp - inner)).astype(BF)
        per_ds = (per_p * (per_dp - inner)).astype(BF)
        dquery = nn(tok_ds, k_ref[:width, cols]) + nn(per_ds, pk_ref[:, cols])
        dpk_acc[:, cols] += tn(per_ds, query) * SCALE
        dpv_acc[:, cols] += tn(per_p.astype(BF), up)
        dkey = tn(tok_ds, query)
        dval = tn(tok_p.astype(BF), up)
        own = slice(base, base + TILE)
        if part == TPS - 1:
            dk_acc[:, cols] = dkey
            dv_acc[:, cols] = dval
        else:
            dk_acc[:base + TILE, cols] += dkey
            dv_acc[:base + TILE, cols] += dval
        return dquery

    def finish(head, dquery):
        cols = slice(head * HD, (head + 1) * HD)
        own = slice(base, base + TILE)

        def rows_of(parts):
            return jnp.concatenate([parts[head, step] for step in range(blocks)], axis=0)

        dout_ref[:, cols] = ((dquery + rows_of(mem_q)) * SCALE).astype(BF)
        dout_ref[:, wide + head * HD:wide + (head + 1) * HD] = (
            (dk_acc[own, cols] + rows_of(mem_k)) * SCALE).astype(BF)
        dout_ref[:, 2 * wide + head * HD:2 * wide + (head + 1) * HD] = (
            dv_acc[own, cols] - rows_of(mem_v)).astype(BF)

    for head in range(heads):
        gates(head)
    per_turn = -(-heads // blocks)
    dqueries = {}
    for turn in range(blocks):
        for head in range(heads):
            memory(blocks - 1 - turn, head)
        for head in range(turn * per_turn, min(heads, (turn + 1) * per_turn)):
            dqueries[head] = attend(head)
    for head in range(heads):
        finish(head, dqueries[head])


def mix_backward_kernel(heads, n, tiles, q_ref, k_ref, v_ref, g_ref, dc_ref, pk_ref, pv_ref,
                        segc_ref, segr_ref, coef_ref, lse_ref, reads_ref, m0_ref, err_ref, *refs):
    own_refs, sib_refs = refs[:4], refs[4:8]
    dout_ref, dpk_ref, dpv_ref = refs[8:11]
    outs = refs[11:15]
    dmem, dmom, dk_acc, dv_acc = refs[15:19]
    scratch = refs[19:31]
    planes = (None, 0, 1, None)
    inbox = (None, refs[31], refs[32], None)
    sems = refs[33:]
    turn = pl.program_id(0)
    tile = tiles - 1 - turn
    items = [
        (own_refs[m], 0, outs[m].shape[1], sib_refs[m]) + tuple(scratch[3 * m:3 * m + 3]) + (outs[m], None, None, planes[m], inbox[m])
        for m in range(4)
    ]
    g = Scatter(n, items, sems)
    order = (3, 0, 1, 2)

    def hops(low, high):
        def one(s, carry):
            for m in order:
                g.advance(m, s)
            return carry

        lax.fori_loop(low, high, one, 0)

    @pl.when(turn == 0)
    def clear():
        greet(n, g.right, g.left, False, True)
        g.begin(order)
        dmem[...] = jnp.zeros_like(dmem)
        dmom[...] = jnp.zeros_like(dmom)
        dpk_ref[...] = jnp.zeros_like(dpk_ref)
        dpv_ref[...] = jnp.zeros_like(dpv_ref)
        for m in order:
            g.ready(m)
            g.start(m)
        for m in (1, 2):
            g.give(m)
        for m in (1, 2):
            g.inside(m, functools.partial(g.launch, m))

    @pl.when(turn > 0)
    def pass_on():
        hops(1 + hop_early(turn - 1, tiles - 2, n - 2), 1 + hop_early(turn, tiles - 2, n - 2))

    for part in range(TPS):
        @pl.when(lax.rem(tile, TPS) == part)
        def work():
            mix_backward_tile(heads, part, tile, q_ref, k_ref, v_ref, g_ref, dc_ref, pk_ref, pv_ref,
                              segc_ref, segr_ref, coef_ref, lse_ref, reads_ref, m0_ref, err_ref,
                              dout_ref, dmem, dmom, dk_acc, dv_acc, dpk_ref, dpv_ref)

    @pl.when(turn == tiles - 1)
    def end():
        for m in order:
            g.settle(m)
        for m in order:
            g.drain(m)


def mix_backward(n, qkvg, dcomb, pkey, pvalue, segc, segr, coef, lse, reads, m0, err, heads, owns, sibs):
    total = qkvg.shape[0]
    width = heads * HD
    tiles = total // TILE
    per = TILE // CH
    last = tiles - 1
    any_spec = pl.BlockSpec(memory_space=pl.ANY)
    arrays = [(a, a.shape[2], True) for a in owns]
    return pl.pallas_call(
        functools.partial(mix_backward_kernel, heads, n, tiles),
        grid=(tiles,),
        in_specs=[
            pl.BlockSpec((TILE, width), lambda t: (last - t, 0)),
            pl.BlockSpec((SEG, width), lambda t: ((last - t) // TPS, 1)),
            pl.BlockSpec((SEG, width), lambda t: ((last - t) // TPS, 2)),
            pl.BlockSpec((TILE, width), lambda t: (last - t, 3)),
            pl.BlockSpec((TILE, width), lambda t: (last - t, 0)),
            pl.BlockSpec((HD, width), lambda t: (0, 0)),
            pl.BlockSpec((HD, width), lambda t: (0, 0)),
            pl.BlockSpec((TILE, 1), lambda t: (last - t, 0)),
            pl.BlockSpec((1, SEG), lambda t: (0, (last - t) // TPS)),
            pl.BlockSpec(memory_space=pltpu.SMEM),
            pl.BlockSpec((TILE, HD), lambda t: (last - t, 0)),
            pl.BlockSpec((TILE, width), lambda t: (last - t, 0)),
            pl.BlockSpec((per, heads, HD, HD), lambda t: (last - t, 0, 0, 0)),
            pl.BlockSpec((TILE, width), lambda t: (last - t, 0)),
        ] + [any_spec] * 8,
        out_specs=[
            pl.BlockSpec((TILE, 4 * width), lambda t: (last - t, 0)),
            pl.BlockSpec((HD, width), lambda t: (0, 0)),
            pl.BlockSpec((HD, width), lambda t: (0, 0)),
        ] + [whole((a.shape[1], w)) for a, w, share in arrays],
        out_shape=[
            jax.ShapeDtypeStruct((total, 4 * width), BF),
            jax.ShapeDtypeStruct((HD, width), F32),
            jax.ShapeDtypeStruct((HD, width), F32),
        ] + [jax.ShapeDtypeStruct((a.shape[1], w), BF) for a, w, share in arrays],
        scratch_shapes=[
            pltpu.VMEM((heads, HD, HD), F32),
            pltpu.VMEM((heads, HD, HD), F32),
            pltpu.VMEM((SEG, width), F32),
            pltpu.VMEM((SEG, width), F32),
        ] + scatter_plan(arrays, False) + [pltpu.VMEM(a.shape, BF) for a in owns[1:3]] + scatter_sems(n, 4, True),
        compiler_params=pltpu.CompilerParams(
            collective_id=4, has_side_effects=True, vmem_limit_bytes=VMEM_MAX),
        name="mix_backward",
    )(qkvg, qkvg, qkvg, qkvg, dcomb, pkey, pvalue, segc, segr, coef, lse, reads, m0, err, *owns, *sibs)


def whole(shape):
    return pl.BlockSpec(shape, lambda t: (0,) * len(shape), pipeline_mode=pl.Buffered(1))


def ffn_kernel(tiles, comb_ref, x_ref, dy_ref, wo_ref, wg0, wg1, wu0, wu1, wd0, wd1, gain_ref,
               out_ref, dmid_ref, dgain_ref, sums_ref, dcomb_out, go_own, go_sib, gg_own, gg_sib,
               gu_own, gu_sib, gd_own, gd_sib, n2, n2t, mid, acc_out, acc_dn, hid_all, pair_all,
               dcomb_v, go_v, gbuf, ubuf, dbuf, keep_sem, send_sem, recv_sem, end_sem):
    turn = pl.program_id(0)
    core = lax.axis_index("col")
    other = 1 - core
    rows_all, dim = x_ref.shape
    half = dim // 2
    steps = rows_all // TILE
    ft = 2 * HD
    gain = gain_ref[...]
    slot = lax.rem(turn, 2)
    hidden_half = gg_own.shape[1]

    def push(src, dst, sem, rsem):
        return pltpu.make_async_remote_copy(
            src_ref=src, dst_ref=dst, send_sem=sem, recv_sem=rsem,
            device_id={"col": other}, device_id_type=MESH)

    def moves(t, s):
        stay, leave = [], []
        for i, (buf, own, sib) in enumerate(((gbuf, gg_own, gg_sib), (ubuf, gu_own, gu_sib))):
            cols = pl.ds(pl.multiple_of(t * HD, HD), HD)
            stay.append(pltpu.make_async_copy(
                buf.at[s, core], own.at[:, cols], keep_sem.at[i, s]))
            leave.append(push(buf.at[s, other], sib.at[:, cols], send_sem.at[i, s], recv_sem.at[i]))
        for i in range(2):
            rows = pl.ds(pl.multiple_of(i * hidden_half + t * HD, HD), HD)
            stay.append(pltpu.make_async_copy(
                dbuf.at[s, core, pl.ds(i * HD, HD)], gd_own.at[rows, :], keep_sem.at[2 + i, s]))
            leave.append(push(dbuf.at[s, other, pl.ds(i * HD, HD)], gd_sib.at[rows, :],
                              send_sem.at[2 + i, s], recv_sem.at[2 + i]))
        return stay, leave

    def settle(t, s):
        stay, leave = moves(t, s)
        for copy in stay:
            copy.wait()
        for copy in leave:
            copy.wait_send()

    @pl.when(turn == 0)
    def first():
        barrier = pltpu.get_barrier_semaphore()
        pl.semaphore_signal(barrier, inc=1, device_id={"col": other}, device_id_type=MESH)
        pl.semaphore_wait(barrier, 1)
        sums_ref[...] = jnp.zeros_like(sums_ref)
        dgain_ref[...] = jnp.zeros_like(dgain_ref)
        for i in range(steps):
            rows = slice(i * TILE, (i + 1) * TILE)
            xf = x_ref[rows, :].astype(F32)
            branch = nn(comb_ref[rows, :], wo_ref[...])
            middle = xf + branch
            mid[rows, :] = middle
            acc_out[rows, :] = middle
            inv = lax.rsqrt(jnp.mean(middle * middle, axis=1, keepdims=True) + EPS)
            normed = (middle * inv * gain).astype(BF)
            n2[rows, :] = normed
            n2t[:, rows] = normed.T
            acc_dn[rows, :] = jnp.zeros((TILE, dim), F32)
            sums_ref[0:1, :] += jnp.sum(xf * xf, axis=0, keepdims=True)
            sums_ref[1:2, :] += jnp.sum(branch * branch, axis=0, keepdims=True)

    wd = jnp.concatenate([wd0[...], wd1[...]], axis=0)
    both = jnp.concatenate([wg0[...], wg1[...], wu0[...], wu1[...]], axis=1)
    chunk = 2 * TILE
    for i in range(rows_all // chunk):
        rows = slice(i * chunk, (i + 1) * chunk)
        gateup = nn(n2[rows, :], both)
        gate, up = gateup[:, :ft], gateup[:, ft:]
        dh = nt(dy_ref[rows, :], wd)
        sig = jax.nn.sigmoid(gate)
        silu = gate * sig
        hid = (silu * up).astype(BF)
        dg = (dh * up * (sig * (1.0 + gate * (1.0 - sig)))).astype(BF)
        du = (dh * silu).astype(BF)
        hid_all[rows, :] = hid
        pair = jnp.concatenate([dg, du], axis=1)
        pair_all[rows, :] = pair
        acc_out[rows, :] += nn(hid, wd)
        acc_dn[rows, :] += nt(pair, both)

    @pl.when(turn >= 2)
    def reuse():
        settle(turn - 2, slot)

    down = tn(hid_all[...], dy_ref[...]).astype(BF)
    grads = nn(n2t[...], pair_all[...]).astype(BF)
    for i in range(2):
        gbuf[slot, i] = grads[:, i * HD:(i + 1) * HD]
        ubuf[slot, i] = grads[:, ft + i * HD:ft + (i + 1) * HD]
        dbuf[slot, i] = down[:, i * half:(i + 1) * half]
    stay, leave = moves(turn, slot)
    for copy in stay + leave:
        copy.start()

    @pl.when(turn == tiles - 1)
    def last():
        for i in range(steps):
            rows = slice(i * TILE, (i + 1) * TILE)
            final = acc_out[rows, :]
            out_ref[rows, :] = final.astype(BF)
            sums_ref[2:3, :] += jnp.sum(final * final, axis=0, keepdims=True)
            middle = mid[rows, :]
            inv = lax.rsqrt(jnp.mean(middle * middle, axis=1, keepdims=True) + EPS)
            dnorm = acc_dn[rows, :]
            weighted = dnorm * gain
            inner = jnp.mean(weighted * middle, axis=1, keepdims=True)
            dgain_ref[...] += jnp.sum(dnorm * middle * inv, axis=0, keepdims=True)
            dmid = dy_ref[rows, :].astype(F32) + weighted * inv - middle * (inv * inv * inv) * inner
            low = dmid.astype(BF)
            dmid_ref[rows, :] = low
            dcomb = nt(low, wo_ref[...]).astype(BF)
            dcomb_v[0, rows, :] = dcomb[:, :half]
            dcomb_v[1, rows, :] = dcomb[:, half:]
        home = pl.ds(pl.multiple_of(core * rows_all, TILE), rows_all)
        stay_c = pltpu.make_async_copy(dcomb_v.at[core], dcomb_out.at[home, :], end_sem.at[0])
        leave_c = push(dcomb_v.at[other], dcomb_out.at[home, :], end_sem.at[1], end_sem.at[2])
        stay_c.start()
        leave_c.start()
        for i in range(dim // TILE):
            part = slice(i * TILE, (i + 1) * TILE)
            go = tn(comb_ref[:, part], dmid_ref[...]).astype(BF)
            go_v[0, part, :] = go[:, :half]
            go_v[1, part, :] = go[:, half:]
        stay_o = pltpu.make_async_copy(go_v.at[core], go_own, end_sem.at[3])
        leave_o = push(go_v.at[other], go_sib, end_sem.at[4], end_sem.at[5])
        stay_o.start()
        leave_o.start()
        settle(turn - 1, 1 - slot)
        settle(turn, slot)
        for i, sib in enumerate((gg_sib, gu_sib)):
            push(sib, sib, send_sem.at[i, 0], recv_sem.at[i]).wait_recv()
        for i in range(2):
            part = gd_sib.at[pl.ds(i * hidden_half, hidden_half), :]
            push(part, part, send_sem.at[2 + i, 0], recv_sem.at[2 + i]).wait_recv()
        stay_c.wait()
        stay_o.wait()
        leave_c.wait()
        leave_o.wait()


def ffn_block(comb, x, dy, w_out, w_gate, w_up, w_down, gain):
    rows, dim = x.shape
    hidden = w_gate.shape[1]
    tiles = hidden // (2 * HD)
    full = (rows, dim)
    half = dim // 2
    any_spec = pl.BlockSpec(memory_space=pl.ANY)
    front = pl.BlockSpec((dim, HD), lambda t: (0, t))
    rear = pl.BlockSpec((dim, HD), lambda t: (0, t + tiles))
    dma = pltpu.SemaphoreType.DMA
    return pl.pallas_call(
        functools.partial(ffn_kernel, tiles),
        grid=(tiles,),
        in_specs=[
            whole(full),
            whole(full),
            whole(full),
            whole((dim, dim)),
            front,
            rear,
            front,
            rear,
            pl.BlockSpec((HD, dim), lambda t: (t, 0)),
            pl.BlockSpec((HD, dim), lambda t: (t + tiles, 0)),
            whole((1, dim)),
        ],
        out_specs=[whole(full), whole(full), whole((1, dim)), whole((8, dim))] + [any_spec] * 9,
        out_shape=[
            jax.ShapeDtypeStruct(full, BF),
            jax.ShapeDtypeStruct(full, BF),
            jax.ShapeDtypeStruct((1, dim), F32),
            jax.ShapeDtypeStruct((8, dim), F32),
            jax.ShapeDtypeStruct((2 * rows, half), BF),
        ]
        + [jax.ShapeDtypeStruct((dim, half), BF)] * 2
        + [jax.ShapeDtypeStruct((dim, hidden // 2), BF)] * 4
        + [jax.ShapeDtypeStruct((hidden, half), BF)] * 2,
        scratch_shapes=[
            pltpu.VMEM(full, BF),
            pltpu.VMEM((dim, rows), BF),
            pltpu.VMEM(full, F32),
            pltpu.VMEM(full, F32),
            pltpu.VMEM(full, F32),
            pltpu.VMEM((rows, 2 * HD), BF),
            pltpu.VMEM((rows, 4 * HD), BF),
            pltpu.VMEM((2, rows, half), BF),
            pltpu.VMEM((2, dim, half), BF),
            pltpu.VMEM((2, 2, dim, HD), BF),
            pltpu.VMEM((2, 2, dim, HD), BF),
            pltpu.VMEM((2, 2, 2 * HD, half), BF),
            dma((4, 2)),
            dma((4, 2)),
            dma((4,)),
            dma((6,)),
        ],
        compiler_params=pltpu.CompilerParams(
            collective_id=5, has_side_effects=True, vmem_limit_bytes=VMEM_MAX),
        name="ffn_block",
    )(comb, x, dy, w_out, w_gate, w_gate, w_up, w_up, w_down, w_down, gain)


def ring_place(row, n):
    return jnp.where(lax.rem(row, 2) == 0, row // 2, n - 1 - row // 2)


def ring_row(place, n):
    return jnp.where(place < n // 2, 2 * place, 2 * (n - place) - 1)


def split_cols(width, flip):
    tiles = width // HD
    if tiles == 1:
        return ((0, width),)
    first = (tiles + (0 if flip else 1)) // 2 * HD
    return ((0, first), (first, width - first))


def mod(value, n):
    return lax.rem(value + n, n)


def neighbours(n):
    me = ring_place(lax.axis_index("row"), n)
    return me, ring_row(mod(me + 1, n), n), ring_row(mod(me - 1, n), n)


def greet(n, right, left, use_col, use_dp):
    barrier = pltpu.get_barrier_semaphore()
    count = 2
    for target in (right, left):
        pl.semaphore_signal(barrier, inc=1, device_id={"row": target}, device_id_type=MESH)
    if use_col:
        other = 1 - lax.axis_index("col")
        pl.semaphore_signal(barrier, inc=1, device_id={"col": other}, device_id_type=MESH)
        count += 1
    if use_dp:
        twin = 1 - lax.axis_index("dp")
        pl.semaphore_signal(barrier, inc=1, device_id={"dp": twin}, device_id_type=MESH)
        count += 1
    pl.semaphore_wait(barrier, count)


class Gather:
    def __init__(self, n, items, sems):
        self.n = n
        self.items = items
        self.send, self.recv, self.local, self.csend, self.crecv, self.xsend = sems
        self.me, self.right, self.left = neighbours(n)
        self.row = lax.axis_index("row")
        self.other = 1 - lax.axis_index("col")
        self.plane = lax.axis_index("dp")

    def ways(self, m):
        return range(len(split_cols(self.items[m][0].shape[1], m % 2)))

    def hop(self, m, d, s):
        block, whole_ref, base = self.items[m][:3]
        place = mod(self.me - s, self.n) if d == 0 else mod(self.me + s, self.n)
        owner = ring_row(place, self.n)
        start, size = split_cols(block.shape[1], m % 2)[d]
        return start, size, whole_ref.at[owner, :, pl.ds(base + start, size)]

    def ring(self, m, d, s, first=False):
        start, size, spot = self.hop(m, d, s)
        source = self.items[m][0].at[:, pl.ds(start, size)] if first else spot
        return pltpu.make_async_remote_copy(
            src_ref=source, dst_ref=spot, send_sem=self.send.at[m, d, s], recv_sem=self.recv.at[m, d, s],
            device_id={"row": self.right if d == 0 else self.left}, device_id_type=MESH)

    def over(self, m, d, s):
        spot = self.hop(m, d, s + 1)[2]
        return pltpu.make_async_remote_copy(
            src_ref=spot, dst_ref=spot, send_sem=self.xsend.at[m, d, s], recv_sem=self.recv.at[m, d, s],
            device_id={"dp": 1 - self.plane}, device_id_type=MESH)

    def across(self, m, source, spot):
        return pltpu.make_async_remote_copy(
            src_ref=source, dst_ref=spot, send_sem=self.csend.at[m], recv_sem=self.crecv.at[m],
            device_id={"col": self.other}, device_id_type=MESH)

    def keep(self, m):
        block, whole_ref, base = self.items[m][:3]
        return pltpu.make_async_copy(
            block, whole_ref.at[self.row, :, pl.ds(base, block.shape[1])], self.local.at[m])

    def when(self, m, inside, action):
        plane = self.items[m][4]
        if plane is None:
            if inside:
                action()
        else:
            pl.when((self.plane == plane) if inside else (self.plane != plane))(action)

    def begin(self, ms):
        for m in ms:
            def launch(m=m):
                for d in self.ways(m):
                    self.ring(m, d, 0, first=True).start()

            self.when(m, True, launch)
        for m in ms:
            block, whole_ref, base, share = self.items[m][:4]
            self.keep(m).start()
            if share:
                self.across(m, block, whole_ref.at[self.row, :, pl.ds(base, block.shape[1])]).start()

    def hand(self, m, d, s):
        if self.items[m][3]:
            spot = self.hop(m, d, s + 1)[2]
            self.across(m, spot, spot).start()

    def arrive(self, m, s):
        for d in self.ways(m):
            self.over(m, d, s).wait_recv()
            self.hand(m, d, s)

    def advance(self, m, s):
        def inside():
            for d in self.ways(m):
                self.ring(m, d, s).wait_recv()

                @pl.when(s < self.n - 2)
                def on():
                    self.ring(m, d, s + 1).start()

                if self.items[m][4] is not None:
                    self.over(m, d, s).start()
                self.hand(m, d, s)

        def outside():
            @pl.when(s > 0)
            def late():
                self.arrive(m, s - 1)

        self.when(m, True, inside)
        self.when(m, False, outside)

    def finish(self, ms):
        for m in ms:
            self.when(m, False, functools.partial(self.arrive, m, self.n - 2))
        for m in ms:
            block, whole_ref, base, share, plane = self.items[m]
            self.keep(m).wait()
            if share:
                spot = whole_ref.at[:, :, pl.ds(base, block.shape[1])]
                theirs = whole_ref.at[:, :, pl.ds(self.other * block.shape[1], block.shape[1])]
                self.across(m, spot, theirs).wait_recv()
                self.across(m, spot, theirs).wait_send()

            def drain(m=m, plane=plane):
                def sent(s, carry):
                    for d in self.ways(m):
                        self.ring(m, d, s).wait_send()
                        if plane is not None:
                            self.over(m, d, s).wait_send()
                    return carry

                lax.fori_loop(0, self.n - 1, sent, 0)

            self.when(m, True, drain)


def gather_sems(n, count):
    dma = pltpu.SemaphoreType.DMA
    return [dma((count, 2, n - 1))] * 2 + [dma((count,))] * 3 + [dma((count, 2, n - 1))]


def pre_kernel(n, *refs):
    blocks, x_ref = refs[:6], refs[6]
    wide_out, small_out, full_out, normed_out, qkvg_out, gain_a_ref, gain_f_ref = refs[7:14]
    wide, small, pair, normed_v, turned_v, qkvg_v, xsems, osems = refs[14:22]
    sems = refs[22:]
    core = lax.axis_index("col")
    dim = x_ref.shape[1]
    planes = (0, 1, None, None)
    items = [(blocks[m], wide, m * blocks[m].shape[1], False, planes[m]) for m in range(4)]
    items.append((blocks[4], small, core * HD, True, None))
    items.append((blocks[5], full_out, core * blocks[5].shape[1], True, None))
    g = Gather(n, items, sems)
    greet(n, g.right, g.left, True, True)
    g.begin(range(5))
    mine = pltpu.make_async_copy(x_ref, pair.at[core], xsems.at[0])
    mine.start()
    theirs = pltpu.make_async_remote_copy(
        src_ref=x_ref, dst_ref=pair.at[core], send_sem=xsems.at[1], recv_sem=xsems.at[2],
        device_id={"col": 1 - core}, device_id_type=MESH)
    theirs.start()

    def hops(ms, low, high):
        def step(s, carry):
            for m in ms:
                g.advance(m, s)
            return carry

        lax.fori_loop(low, high, step, 0)

    lag = n // 2 - 1
    hops(range(5), 0, lag)
    g.begin((5,))

    def both(s, carry):
        for m in range(5):
            g.advance(m, s)
        g.advance(5, s - lag)
        return carry

    lax.fori_loop(lag, n - 1, both, 0)
    done = n - 1 - lag
    g.finish(range(5))
    mine.wait()
    theirs.wait()
    copies = [pltpu.make_async_copy(wide, wide_out, osems.at[0]),
              pltpu.make_async_copy(small, small_out, osems.at[1])]
    for copy in copies:
        copy.start()
    gains = jnp.zeros((16, HD), F32)
    for q in range(n):
        for i in range(2):
            gains = gains + small[q, 2 * P_SIZE:, i * HD:(i + 1) * HD].astype(F32)
    tiles = dim // HD
    gain = jnp.concatenate([gains[i:i + 1] for i in range(tiles)], axis=1)
    gain_a_ref[...] = gain
    gain_f_ref[...] = jnp.concatenate([gains[tiles + i:tiles + i + 1] for i in range(tiles)], axis=1)
    chunk = normed_v.shape[1]
    count = normed_v.shape[0]
    per_core = count // 2
    width = qkvg_v.shape[2] // 2
    slots = 2 * count - 1
    for i in range(count):
        rows = slice((i % per_core) * chunk, (i % per_core + 1) * chunk)
        xf = pair[i // per_core, rows, :].astype(F32)
        inv = lax.rsqrt(jnp.mean(xf * xf, axis=1, keepdims=True) + EPS)
        normed_v[i] = (xf * inv * gain).astype(BF)
        for j in range(2):
            cols = slice(j * width, (j + 1) * width)
            weight = wide[:, :, cols].reshape(dim, width)
            qkvg_v[i, :, cols] = nn(normed_v[i], weight).astype(BF)
            u = 2 * i + j
            if u < slots:
                hops((5,), done + u * lag // slots, done + (u + 1) * lag // slots)
        turned_v[i] = normed_v[i].T
        copies.append(pltpu.make_async_copy(
            turned_v.at[i], normed_out.at[:, pl.ds(i * chunk, chunk)], osems.at[2 + i]))
        copies[-1].start()
        copies.append(pltpu.make_async_copy(
            qkvg_v.at[i], qkvg_out.at[pl.ds(i * chunk, chunk)], osems.at[2 + count + i]))
        copies[-1].start()
    g.finish((5,))
    for copy in copies:
        copy.wait()


def pre(n, blocks, small, w_out, x):
    rows, width = blocks[0].shape
    tokens, dim = x.shape
    count = 2 * tokens // 512
    any_spec = pl.BlockSpec(memory_space=pl.ANY)
    vmem_spec = pl.BlockSpec(memory_space=pltpu.VMEM)
    dma = pltpu.SemaphoreType.DMA
    wide = (n, rows, 4 * width)
    smalls = (n, small.shape[0], 2 * small.shape[1])
    shapes = [wide, smalls, (n, rows, 2 * w_out.shape[1]), (dim, 2 * tokens), (2 * tokens, 4 * width)]
    return pl.pallas_call(
        functools.partial(pre_kernel, n),
        in_specs=[vmem_spec] * 7,
        out_specs=[any_spec] * 5 + [vmem_spec] * 2,
        out_shape=[jax.ShapeDtypeStruct(shape, BF) for shape in shapes]
        + [jax.ShapeDtypeStruct((1, dim), F32)] * 2,
        scratch_shapes=[
            pltpu.VMEM(wide, BF),
            pltpu.VMEM(smalls, BF),
            pltpu.VMEM((2,) + x.shape, BF),
            pltpu.VMEM((count, 512, dim), BF),
            pltpu.VMEM((count, dim, 512), BF),
            pltpu.VMEM((count, 512, 4 * width), BF),
            dma((3,)),
            dma((2 + 2 * count,)),
        ] + gather_sems(n, 6),
        compiler_params=pltpu.CompilerParams(
            collective_id=1, has_side_effects=True, vmem_limit_bytes=VMEM_MAX),
        name="pre",
    )(*blocks, small, w_out, x)


class Scatter:
    def __init__(self, n, items, sems):
        self.n = n
        self.items = items
        self.send, self.recv, self.local, self.sib, self.dsend, self.drecv, self.xsend, self.xrecv = sems
        self.me, self.right, self.left = neighbours(n)
        self.plane = lax.axis_index("dp")
        self.twin = 1 - self.plane

    def ways(self, m):
        return range(len(split_cols(self.items[m][2], m % 2)))

    def loads(self, m):
        ref, base, width, other, own, sib = self.items[m][:6]
        copies = [pltpu.make_async_copy(ref.at[:, :, pl.ds(base, width)], own, self.local.at[m])]
        if other is not None:
            copies.append(pltpu.make_async_copy(other, sib, self.sib.at[m]))
        return copies

    def begin(self, ms):
        for m in ms:
            for copy in self.loads(m):
                copy.start()

    def ready(self, m):
        for copy in self.loads(m):
            copy.wait()

    def part(self, m, d, s):
        place = mod(self.me - 1 - s, self.n) if d == 0 else mod(self.me + 1 + s, self.n)
        start, size = split_cols(self.items[m][2], m % 2)[d]
        return ring_row(mod(place, self.n), self.n), slice(start, start + size)

    def ring(self, m, d, s):
        own, ring = self.items[m][4], self.items[m][6]
        owner, cols = self.part(m, d, s)
        return pltpu.make_async_remote_copy(
            src_ref=own.at[owner, :, cols], dst_ref=ring.at[s, :, cols],
            send_sem=self.send.at[m, d, s], recv_sem=self.recv.at[m, d, s],
            device_id={"row": self.right if d == 0 else self.left}, device_id_type=MESH)

    def plane_of(self, m):
        return self.items[m][10] if len(self.items[m]) > 10 else None

    def inside(self, m, action):
        plane = self.plane_of(m)
        if plane is None:
            action()
        else:
            pl.when(self.plane == plane)(action)

    def over(self, m, d, s):
        own, inbox = self.items[m][4], self.items[m][11]
        owner, cols = self.part(m, d, s)
        return pltpu.make_async_remote_copy(
            src_ref=own.at[owner, :, cols], dst_ref=inbox.at[owner, :, cols],
            send_sem=self.xsend.at[m, d, s], recv_sem=self.xrecv.at[m, d, s],
            device_id={"dp": self.twin}, device_id_type=MESH)

    def send_over(self, m):
        def one(s, carry):
            for d in self.ways(m):
                owner, cols, value = self.total(m, d, s, False, False)
                self.items[m][4][owner, :, cols] = value
                self.over(m, d, s).start()
            return carry

        lax.fori_loop(0, self.n, one, 0)

    def total(self, m, d, s, arrived, dp=True):
        other, own, sib, ring = self.items[m][3:7]
        owner, cols = self.part(m, d, s)
        value = own[owner, :, cols].astype(F32)
        if other is not None:
            value = value + sib[owner, :, cols].astype(F32)
        if dp and self.plane_of(m) is not None:
            self.over(m, d, s).wait_recv()
            value = value + self.items[m][11][owner, :, cols].astype(F32)
        if arrived:
            value = value + ring[s - 1, :, cols].astype(F32)
        return owner, cols, value.astype(own.dtype)

    def launch(self, m):
        for d in self.ways(m):
            if self.items[m][3] is not None:
                owner, cols, value = self.total(m, d, 0, False)
                self.items[m][4][owner, :, cols] = value
            self.ring(m, d, 0).start()

    def give(self, m):
        pl.when(self.plane != self.plane_of(m))(lambda: self.send_over(m))

    def start(self, m):
        if self.plane_of(m) is None:
            self.launch(m)

    def advance(self, m, s):
        def go():
            for d in self.ways(m):
                self.ring(m, d, s - 1).wait_recv()
                owner, cols, value = self.total(m, d, s, True)
                self.items[m][4][owner, :, cols] = value
                self.ring(m, d, s).start()

        self.inside(m, go)

    def swap(self, m):
        low, twin = self.items[m][7:9]
        return pltpu.make_async_remote_copy(
            src_ref=low, dst_ref=twin, send_sem=self.dsend.at[m], recv_sem=self.drecv.at[m],
            device_id={"dp": self.twin}, device_id_type=MESH)

    def settle(self, m):
        def go():
            for d in self.ways(m):
                self.ring(m, d, self.n - 2).wait_recv()
                owner, cols, value = self.total(m, d, self.n - 1, True)
                self.items[m][7][:, cols] = value
            if self.items[m][8] is not None:
                self.swap(m).start()

        self.inside(m, go)

    def finish(self, m):
        low, twin, out = self.items[m][7:10]
        self.swap(m).wait_recv()
        out[...] = low[...].astype(F32) + twin[...].astype(F32)
        self.swap(m).wait_send()
        self.drain(m)

    def drain(self, m):
        def sent(s, carry):
            for d in self.ways(m):
                self.ring(m, d, s).wait_send()
            return carry

        def ring_done():
            lax.fori_loop(0, self.n - 1, sent, 0)

        self.inside(m, ring_done)
        if self.plane_of(m) is not None:
            def given(s, carry):
                for d in self.ways(m):
                    self.over(m, d, s).wait_send()
                return carry

            @pl.when(self.plane != self.plane_of(m))
            def given_done():
                lax.fori_loop(0, self.n, given, 0)


def scatter_sems(n, count, planes=False):
    dma = pltpu.SemaphoreType.DMA
    return [dma((count, 2, n - 1))] * 2 + [dma((count,))] * 4 + [dma((count, 2, n) if planes else (1,))] * 2


def scatter_plan(arrays, swap=True):
    scratch = []
    for array, width, share in arrays:
        n, rows, full = array.shape
        kind = array.dtype
        scratch.append(pltpu.VMEM((n, rows, width), kind))
        scratch.append(pltpu.VMEM((n, rows, width) if share else (1, 16, HD), kind))
        scratch.append(pltpu.VMEM((n - 1, rows, width), kind))
        if swap:
            scratch.append(pltpu.VMEM((rows, width), kind))
            scratch.append(pltpu.VMEM((rows, width), kind))
    return scratch


def post_kernel(n, turned, d_ref, w_ref, x_ref, dmid_ref, gain_ref, small, *refs):
    late = refs[:4]
    own_w = refs[4:8]
    gin_ref = refs[8]
    outs = refs[9:14]
    late_outs = refs[14:18]
    dgain_ref = refs[18]
    back, leave, came, dg_own, dg_sib, small_sib = refs[19:25]
    late_in = refs[25:29]
    scratch = refs[29:54]
    side, late_send, late_recv = refs[54:57]
    sems = refs[57:]
    turn = pl.program_id(0)
    core = lax.axis_index("col")
    other = 1 - core
    rows_all, dim = x_ref.shape
    width = outs[0].shape[1]
    block = outs[0].shape[0]
    items = []
    for m in range(5):
        first, sib = (0, None) if m < 4 else (core * HD, small_sib)
        items.append((None if m < 4 else small, first, outs[m].shape[1], sib)
                     + tuple(scratch[5 * m:5 * m + 5]) + (outs[m],))
    g = Scatter(n, items, sems)
    steps = 2 * rows_all // TILE

    def push(src, dst, at):
        return pltpu.make_async_remote_copy(
            src_ref=src, dst_ref=dst, send_sem=side.at[2 * at], recv_sem=side.at[2 * at + 1],
            device_id={"col": other}, device_id_type=MESH)

    def late_swap(i):
        return pltpu.make_async_remote_copy(
            src_ref=late[i], dst_ref=late_in[i], send_sem=late_send.at[i], recv_sem=late_recv.at[i],
            device_id={"dp": g.twin}, device_id_type=MESH)

    planes = (None, 0, 1, None)

    def late_start(i):
        if planes[i] is None:
            late_swap(i).start()
        else:
            pl.when(g.plane == planes[i])(lambda: late_swap(i).start())

    def late_end(i):
        if planes[i] is None:
            late_swap(i).wait()
            late_outs[i][...] = late[i][...].astype(F32) + late_in[i][...].astype(F32)
        else:
            @pl.when(g.plane == planes[i])
            def given():
                late_swap(i).wait_send()
                late_outs[i][...] = late[i][...].astype(F32)

            @pl.when(g.plane != planes[i])
            def taken():
                late_swap(i).wait_recv()
                late_outs[i][...] = late_in[i][...].astype(F32)

    cross = push(small.at[:, :, pl.ds(other * HD, HD)], small_sib, 0)
    swap_back = push(leave, came, 1)
    swap_gain = push(dg_own, dg_sib, 2)

    @pl.when(turn == 0)
    def first_turn():
        greet(n, g.right, g.left, True, True)
        cross.start()
        for i in range(4):
            late_start(i)

    rate = (n + 5) // 7

    def slot(u):
        for m in range(5):
            v = u - 2 * (m % 4)
            if v < 1:
                continue
            low, high = max(1, rate * (v - 1) + 1), min(n - 1, rate * v + 1)
            if low < high:
                def one(s, carry, m=m):
                    g.advance(m, s)
                    return carry

                lax.fori_loop(low, high, one, 0)
            elif rate * (v - 1) + 1 < n - 1 + rate:
                g.settle(m)

    for m in range(4):
        @pl.when(turn == m)
        def this():
            for part in range(2):
                cols = slice(part * (width // 2), (part + 1) * (width // 2))
                grad = nn(turned[...], d_ref[:, cols]).astype(BF)
                for q in range(n):
                    items[m][4][q, :, cols] = grad[q * block:(q + 1) * block]
            g.start(m)
            slot(2 * m)
            if m == 0:
                cross.wait()
                g.begin((4,))
                g.ready(4)
                g.start(4)
            for i in range(steps // 2):
                rows = slice(2 * i * TILE, 2 * (i + 1) * TILE)
                if m == 0:
                    back[rows, :] = nt(d_ref[rows, :], w_ref[...])
                else:
                    back[rows, :] += nt(d_ref[rows, :], w_ref[...])
            slot(2 * m + 1)

    @pl.when(turn == 3)
    def rest():
        theirs = pl.multiple_of(other * rows_all, TILE)
        for i in range(rows_all // TILE):
            rows = slice(i * TILE, (i + 1) * TILE)
            leave[rows, :] = back[pl.ds(theirs + i * TILE, TILE), :].astype(BF)
        swap_back.start()
        slot(8)
        slot(9)
        swap_back.wait()
        mine = pl.multiple_of(core * rows_all, TILE)
        gain = gain_ref[...]
        for i in range(rows_all // TILE):
            rows = slice(i * TILE, (i + 1) * TILE)
            xf = x_ref[rows, :].astype(F32)
            inv = lax.rsqrt(jnp.mean(xf * xf, axis=1, keepdims=True) + EPS)
            weighted = (back[pl.ds(mine + i * TILE, TILE), :] + came[rows, :].astype(F32)) * gain
            inner = jnp.mean(weighted * xf, axis=1, keepdims=True)
            value = dmid_ref[rows, :].astype(F32) + weighted * inv - xf * (inv * inv * inv) * inner
            gin_ref[rows, :] = value.astype(BF)
            if i < 2:
                slot(10 + i)
        for u in range(12, 15):
            slot(u)
        for i in range(4):
            late_end(i)
        total = jnp.zeros((block, 1), F32)
        for m in range(4):
            g.finish(m)
            total = total + jnp.sum(outs[m][...] * own_w[m][...].astype(F32), axis=1, keepdims=True)
        dg_own[...] = jnp.broadcast_to(total, (block, HD))
        swap_gain.start()
        g.finish(4)
        swap_gain.wait()
        dgain_ref[...] = dg_own[...] + dg_sib[...]


def post(n, normed, dqkvg, wide, x, dmid, gain, small, late, own_w):
    dim, total = normed.shape
    width = wide.shape[1] // 4
    rows = x.shape[0]
    block = dim // n
    arrays = [(jax.ShapeDtypeStruct((n, block, width), BF), width, False)] * 4 + [(small, HD, True)]
    any_spec = pl.BlockSpec(memory_space=pl.ANY)
    dma = pltpu.SemaphoreType.DMA
    outs = [((a.shape[1], w), F32) for a, w, share in arrays]
    late_outs = [(a.shape, F32) for a in late]
    shapes = [((rows, dim), BF)] + outs + late_outs + [((block, HD), F32)]
    return pl.pallas_call(
        functools.partial(post_kernel, n),
        grid=(4,),
        in_specs=[
            whole((dim, total)),
            pl.BlockSpec((total, width), lambda t: (0, t)),
            pl.BlockSpec((dim, width), lambda t: (0, t)),
            whole((rows, dim)),
            whole((rows, dim)),
            whole((1, dim)),
            any_spec,
        ] + [whole(a.shape) for a in late] + [whole(a.shape) for a in own_w],
        out_specs=[whole(shape) for shape, kind in shapes],
        out_shape=[jax.ShapeDtypeStruct(shape, kind) for shape, kind in shapes],
        scratch_shapes=[
            pltpu.VMEM((total, dim), F32),
            pltpu.VMEM((rows, dim), BF),
            pltpu.VMEM((rows, dim), BF),
            pltpu.VMEM((block, HD), F32),
            pltpu.VMEM((block, HD), F32),
            pltpu.VMEM((n, small.shape[1], HD), F32),
        ]
        + [pltpu.VMEM(a.shape, BF) for a in late]
        + scatter_plan(arrays)
        + [dma((6,)), dma((4,)), dma((4,))]
        + scatter_sems(n, 5),
        compiler_params=pltpu.CompilerParams(
            collective_id=2, has_side_effects=True, vmem_limit_bytes=VMEM_MAX),
        name="post",
    )(normed, dqkvg, wide, x, dmid, gain, small, *late, *own_w)


def local(
    tokens_in,
    grad_out,
    gain_attn,
    gain_ffn,
    w_query,
    w_key,
    w_value,
    w_gate,
    w_out,
    w_ffn_gate,
    w_ffn_up,
    w_ffn_down,
    persist_key,
    persist_value,
    mem_rate,
    mem_momentum,
    mem_forget,
    segment_ids,
    decay_index,
):
    n = lax.axis_size("row")
    core = lax.axis_index("col")
    local_tok, dim = tokens_in.shape
    heads = mem_rate.shape[1]
    width = heads * HD
    piece = gain_attn.shape[0]
    slot = lax.axis_index("row") * 2 + core

    def spread(part):
        return lax.dynamic_update_slice(jnp.zeros((dim,), BF), part, (slot * piece,)).reshape(dim // HD, HD)

    persist = jnp.pad(jnp.concatenate([persist_key, persist_value], axis=0), ((0, 0), (0, HD - piece)))
    small = jnp.concatenate([persist, spread(gain_attn), spread(gain_ffn)], axis=0)
    wide, small_all, full_out, normed, qkvg, gain_a, gain_f = pre(
        n, (w_query, w_key, w_value, w_gate), small, w_out, tokens_in)
    wide = wide.reshape(dim, 4 * width)
    small_all = small_all[:, :2 * P_SIZE].reshape(n, 2 * P_SIZE, 2, HD)[:, :, :, :piece]
    small_all = small_all.transpose(1, 0, 2, 3).reshape(2 * P_SIZE, dim)
    own_small = lax.dynamic_slice_in_dim(small_all, core * width, width, 1)
    pad = ((0, HD - P_SIZE), (0, 0))
    pkey = jnp.pad(own_small[:P_SIZE], pad)
    pvalue = jnp.pad(own_small[P_SIZE:2 * P_SIZE], pad)

    total = qkvg.shape[0]
    spans = total // CH
    span_ids = segment_ids.reshape(total // SEQ, SEQ // CH, CH)
    same = (span_ids[:, 1:, 0] == span_ids[:, :-1, CH - 1]).astype(F32)
    keep = jnp.concatenate([jnp.zeros((total // SEQ, 1), F32), same], axis=1).reshape(spans, 1)
    choose = (decay_index[:, None] == jnp.arange(mem_rate.shape[0])[None, :]).astype(F32)
    tables = jnp.concatenate([mem_rate, mem_momentum, 1.0 - mem_forget], axis=1)
    picked = jnp.dot(choose, tables, precision=HIGH)
    coef = jnp.stack(
        [jnp.broadcast_to(keep, (spans, heads))] + [picked[:, i * heads:(i + 1) * heads] for i in range(3)]
    ).reshape(4, spans * heads)
    segc, segr = segment_ids[:, None], segment_ids[None, :]

    later = (w_ffn_gate, w_ffn_up, w_ffn_down)
    lse, reads, m0, err, comb_tok, full_gate, full_up, full_down = mix_forward(
        n, qkvg, pkey, pvalue, segc, segr, coef, heads, later)
    full_out, full_gate, full_up = [a.reshape(dim, -1) for a in (full_out, full_gate, full_up)]
    full_down = full_down.reshape(-1, dim)
    result, dmid, dgain_f, sums, dcomb, *parts = ffn_block(
        comb_tok, tokens_in, grad_out, full_out, full_gate, full_up, full_down, gain_f)
    parts = [a.reshape(n, a.shape[0] // n, a.shape[1]) for a in parts]
    dqkvg, dpk, dpv, *grads_late = mix_backward(
        n, qkvg, dcomb, pkey, pvalue, segc, segr, coef, lse, reads, m0, err, heads,
        parts[0::2], parts[1::2])

    place = jnp.zeros((2 * P_SIZE, dim), F32)
    place = lax.dynamic_update_slice_in_dim(
        place, jnp.concatenate([dpk[:P_SIZE], dpv[:P_SIZE]], axis=0), core * width, 1)
    packed = jnp.concatenate([place, jnp.zeros((1, dim), F32), dgain_f], axis=0)
    packed = packed.reshape(2 * P_SIZE + 2, n, 2, piece).transpose(1, 0, 2, 3)
    packed = jnp.pad(packed, ((0, 0), (0, 0), (0, 0), (0, HD - piece)))
    stats = jnp.sum(sums.reshape(8, dim // HD, HD), axis=1)[:6]
    stats = jnp.broadcast_to(stats[None, :, None, :], (n, 6, 2, HD))
    packed = jnp.concatenate([packed, stats], axis=1).reshape(n, 2 * P_SIZE + 8, 2 * HD)
    grad_in, *rest = post(
        n, normed, dqkvg, wide, tokens_in, dmid, gain_a, packed, grads_late,
        (w_query, w_key, w_value, w_gate))
    grads, part, dgain_a = rest[:4] + rest[5:9], rest[4], rest[9]
    dgain_a = lax.dynamic_slice_in_dim(dgain_a[:, 0], core * piece, piece, 0) / gain_attn.astype(F32)
    entry_count = local_tok * dim * lax.axis_size("dp") * n * lax.axis_size("col")
    rms_stats = jnp.sqrt(jnp.sum(part[2 * P_SIZE + 2:2 * P_SIZE + 5], axis=1) / entry_count)
    part = part[:, :piece]
    return (
        result,
        grad_in,
        grads[0],
        grads[1],
        grads[2],
        grads[3],
        grads[4],
        grads[5],
        grads[6],
        grads[7],
        dgain_a,
        part[2 * P_SIZE + 1],
        part[:P_SIZE],
        part[P_SIZE:2 * P_SIZE],
        rms_stats,
    )


def solution(mesh):
    tokens = P(("dp", "row", "col"), None)
    vector = P(("row", "col"))
    weight = P("row", "col")
    persist = P(None, ("row", "col"))
    table = P(None, "col")
    ids = P(("dp", "row"))
    return jax.shard_map(
        local,
        mesh=mesh,
        in_specs=(tokens, tokens, vector, vector) + (weight,) * 8 + (persist,) * 2 + (table,) * 3 + (ids,) * 2,
        out_specs=(tokens, tokens) + (weight,) * 8 + (vector,) * 2 + (persist,) * 2 + (P(),),
        check_vma=False,
    )
```
